32 devices in a mesh: gx: 8 (over z, x), gy: 4 (over y, core).
Axes of the slice: x: 2, y: 2, z: 4, core: 2. Of those that a mesh axis runs over, the one named last changes fastest.
Arguments:
- displacement: float32 [64, 16, 3, 128], P('gx', 'gy'), may hold values from -6 to 6
- volume: float32 [64, 16, 128], P('gx', 'gy'), may hold values from 0.5 to 2
- health: float32 [64, 16, 128], P('gx', 'gy'), may hold values from 0.2 to 1
- damage: int32 [64, 16, 128], P('gx', 'gy'), may hold values 0 or 1
- block_pairs: int32 [8, 4, 162, 4], P('gx', 'gy'), may hold values from -1 to 9, as said below
Outputs:
- deform_grad: float32 [64, 16, 9, 128], P('gx', 'gy')
- force_density: float32 [64, 16, 3, 128], P('gx', 'gy')
The draws below stay inside these ranges and needn't reach their ends.
Inputs may be any that keep to these rules, and one draw needn't show every extreme that they name: `block_pairs`: every row is (ax, ay, bx, by) with blocks in a device's frame: its own blocks at 1 to 8 and 1 to 4, the blocks beside them at 0 and 9, 0 and 5; (bx - ax, by - ay) is (1, 0), (0, 1), (1, 1) or (1, -1); both blocks lie inside the plate and at least one is the device's own. A pair of adjacent plate blocks is named at most once over all devices; pairs named nowhere are severed. Live rows come first, then rows of -1. In every draw some device names all 162 pairs that touch its blocks.
All inputs are finite; a program needn't handle non-finite values. No bound on the sum of `damage` on one device may be relied on, other than what follows from the above.
Results may differ from the reference program's by a relative error of at most 0.0003.
Values sent between devices are 32-bit elements; how exact they have to be, the bound alone decides.
No kernel may reach another device: no remote copies, remote signals or barrier semaphores. Data moves between devices by JAX's collectives and lax.ppermute only.
A program may use at most 64 MiB of HBM per device.

```python
import math
import jax
import jax.numpy as jnp
import numpy as np
from jax import lax

PTS_BLK = 128
BX_DEV = 8
BY_DEV = 4
PLATE_X = 64
PLATE_Y = 16
PAIRS_MAX = 162
N_GX = 8
N_GY = 4


def pair_template():
    ext_x = BX_DEV + 2
    ext_y = BY_DEV + 2
    entries = []
    for first_x in range(ext_x):
        for first_y in range(ext_y):
            for kind_index, step_pair in enumerate(((1, 0), (0, 1), (1, 1), (1, -1))):
                second_x = first_x + step_pair[0]
                second_y = first_y + step_pair[1]
                inside_ext = 0 <= second_x < ext_x and 0 <= second_y < ext_y
                own_first = 1 <= first_x <= BX_DEV and 1 <= first_y <= BY_DEV
                own_second = 1 <= second_x <= BX_DEV and 1 <= second_y <= BY_DEV
                if inside_ext and (own_first or own_second):
                    entries.append((first_x, first_y, second_x, second_y, kind_index))
    return np.array(entries, dtype=np.int32)


def draw_block_pairs(key, part):
    template = jnp.asarray(pair_template())
    plate_x = BX_DEV * N_GX
    plate_y = BY_DEV * N_GY
    pick_side = jax.random.randint(jax.random.fold_in(key, 11), (plate_x, plate_y, 4), 0, 2)
    cut_flag = jax.random.randint(jax.random.fold_in(key, 12), (plate_x, plate_y, 4), 0, 8) == 0
    star_x = jax.random.randint(jax.random.fold_in(key, 13), (), 1, N_GX - 1)
    star_y = jax.random.randint(jax.random.fold_in(key, 14), (), 1, N_GY - 1)
    star_device = star_x * N_GY + star_y
    dev_x = jnp.arange(N_GX, dtype=jnp.int32)[:, None, None]
    dev_y = jnp.arange(N_GY, dtype=jnp.int32)[None, :, None]
    first_x = dev_x * BX_DEV + template[:, 0] - 1
    first_y = dev_y * BY_DEV + template[:, 1] - 1
    second_x = dev_x * BX_DEV + template[:, 2] - 1
    second_y = dev_y * BY_DEV + template[:, 3] - 1
    inside = (first_x >= 0) & (first_x < plate_x) & (first_y >= 0) & (first_y < plate_y)
    inside = inside & (second_x >= 0) & (second_x < plate_x) & (second_y >= 0) & (second_y < plate_y)
    owner_first = first_x // BX_DEV * N_GY + first_y // BY_DEV
    owner_second = second_x // BX_DEV * N_GY + second_y // BY_DEV
    anchor_x = jnp.clip(first_x, 0, plate_x - 1)
    anchor_y = jnp.clip(first_y, 0, plate_y - 1)
    kind_index = jnp.broadcast_to(template[:, 4], first_x.shape)
    chosen = pick_side[anchor_x, anchor_y, kind_index]
    severed = cut_flag[anchor_x, anchor_y, kind_index]
    touches = (owner_first == star_device) | (owner_second == star_device)
    runner = jnp.where(chosen == 0, owner_first, owner_second)
    runner = jnp.where(touches, star_device, runner)
    device = dev_x * N_GY + dev_y
    live_flag = inside & (runner == device) & (touches | jnp.logical_not(severed))
    order_noise = jax.random.randint(jax.random.fold_in(key, 15), first_x.shape, 0, PAIRS_MAX) * PAIRS_MAX + jnp.arange(PAIRS_MAX, dtype=jnp.int32)
    order_score = jnp.where(live_flag, 0, PAIRS_MAX * PAIRS_MAX) + order_noise
    slot_order = jnp.argsort(order_score, axis=-1, stable=True)
    rows_all = jnp.broadcast_to(template[:, 0:4], first_x.shape + (4,))
    picked = jnp.take_along_axis(rows_all, slot_order[..., None], axis=2)
    keep_flag = jnp.take_along_axis(live_flag, slot_order, axis=2)
    return jnp.where(keep_flag[..., None], picked, -1).astype(jnp.int32)


def touch_ends(values, key, smallest, top_value):
    extent = values.shape
    index_at = [jax.random.randint(jax.random.fold_in(key, axis), (), 0, extent[axis]) for axis in range(len(extent))]
    values = values.at[tuple(index_at)].set(smallest)
    longest = extent.index(max(extent))
    index_at[longest] = (index_at[longest] + 1) % extent[longest]
    return values.at[tuple(index_at)].set(top_value)


def block_scale(stream_key, dims, cuts, low, top_value):
    factor_of, own = 1.0, jax.random.fold_in(stream_key, 6)
    for axis_at, blocks in cuts:
        draws = jnp.exp(jax.random.uniform(jax.random.fold_in(own, axis_at), (blocks,), jnp.float32, low / len(cuts), top_value / len(cuts)))
        factor_of = factor_of * jnp.repeat(draws, dims[axis_at] // blocks).reshape([-1 if axis == axis_at else 1 for axis in range(len(dims))])
    return factor_of


def normal_values(rng, extent, width, reach, split=(), kind=jnp.bfloat16):
    values = jax.random.normal(rng, extent, jnp.float32) * width
    if len(split) > 0:
        values = block_scale(rng, extent, split, -0.22, 0.18) * values
    return jnp.clip(values, min=-reach, max=reach).astype(kind)


def setup_inputs(seed: int = 0) -> dict:
    arg_keys = jax.random.split(jax.random.key(seed), 6)
    displacement = normal_values(arg_keys[0], (PLATE_X, PLATE_Y, 3, PTS_BLK), 1.0, 6.0, ((0, 8), (1, 4)), jnp.float32)
    volume = jnp.clip(jnp.exp(math.log(2.0) - 1.3862944 * jax.random.uniform(arg_keys[1], (PLATE_X, PLATE_Y, PTS_BLK), jnp.float32) ** block_scale(arg_keys[1], (PLATE_X, PLATE_Y, PTS_BLK), ((0, 8), (1, 4)), -0.2, 0.2)), 0.5, 2.0)
    health = jnp.clip(0.2 + 0.8 * jax.random.uniform(arg_keys[2], (PLATE_X, PLATE_Y, PTS_BLK), jnp.float32) ** block_scale(arg_keys[2], (PLATE_X, PLATE_Y, PTS_BLK), ((0, 8), (1, 4)), -0.2, 0.2), 0.2, 1.0)
    damage = touch_ends((jax.random.randint(arg_keys[3], (PLATE_X, PLATE_Y, PTS_BLK), 0, 8) < 1).astype(jnp.int32), jax.random.fold_in(arg_keys[3], 1), 0, 1)
    block_pairs = draw_block_pairs(jax.random.fold_in(arg_keys[5], 71), 0)
    return dict(displacement=displacement, volume=volume, health=health, damage=damage, block_pairs=block_pairs)


highest = lax.Precision.HIGHEST
lame_first = 24.0
shear_modulus = 16.0
transpose_order = np.array([0, 3, 6, 1, 4, 7, 2, 5, 8])


def lattice(points):
    index = jnp.arange(points, dtype=jnp.int32)
    return jnp.stack([index % 4, (index // 4) % 4, index // 16])


def block_offset(step_x, step_y):
    return jnp.stack([4 * step_x, 4 * step_y, jnp.zeros_like(step_x)], axis=1)


def bond_weights(health_first, health_second, step_x, step_y):
    points = health_first.shape[-1]
    lattice_grid = lattice(points)
    shifted = lattice_grid[None] + block_offset(step_x, step_y)[:, :, None]
    distance = jnp.zeros((step_x.shape[0], points, points), jnp.int32)
    for comp_index in range(3):
        gap_comp = shifted[:, comp_index, None, :] - lattice_grid[None, comp_index, :, None]
        distance = distance + gap_comp * gap_comp
    linked = (distance <= 9) & (distance > 0)
    lower_health = jnp.minimum(health_first[:, :, None], health_second[:, None, :])
    return jnp.where(linked, lower_health, jnp.zeros_like(lower_health))


def positions(point_pack, step_x, step_y):
    reference_pos = (lattice(point_pack.shape[-1])[None] + block_offset(step_x, step_y)[:, :, None]).astype(jnp.float32)
    return reference_pos, reference_pos + point_pack[:, 0:3], point_pack[:, 3], point_pack[:, 4]


def shape_features(ref_pos, cur_pos, vol_pts):
    slot_count, points = ref_pos.shape[0], ref_pos.shape[-1]
    outer_rr = (ref_pos[:, :, None] * ref_pos[:, None]).reshape(slot_count, 9, points)
    outer_cr = (cur_pos[:, :, None] * ref_pos[:, None]).reshape(slot_count, 9, points)
    ones_row = jnp.ones((slot_count, 1, points), jnp.float32)
    return jnp.concatenate([outer_rr, outer_cr, ref_pos, cur_pos, ones_row], axis=1) * vol_pts[:, None]


def shape_terms(tile_sums, ref_pos, cur_pos):
    slot_count, points = ref_pos.shape[0], ref_pos.shape[-1]
    sum_rr = tile_sums[:, 0:9].reshape(slot_count, 3, 3, points)
    sum_cr = tile_sums[:, 9:18].reshape(slot_count, 3, 3, points)
    sum_r = tile_sums[:, 18:21]
    sum_c = tile_sums[:, 21:24]
    sum_one = tile_sums[:, 24][:, None, None]
    shape_k = sum_rr - ref_pos[:, :, None] * sum_r[:, None] - sum_r[:, :, None] * ref_pos[:, None] + sum_one * ref_pos[:, :, None] * ref_pos[:, None]
    shape_n = sum_cr - cur_pos[:, :, None] * sum_r[:, None] - sum_c[:, :, None] * ref_pos[:, None] + sum_one * cur_pos[:, :, None] * ref_pos[:, None]
    return jnp.concatenate([shape_k.reshape(slot_count, 9, points), shape_n.reshape(slot_count, 9, points)], axis=1)


def force_features(ref_pos, stress_map, vol_pts):
    slot_count, points = ref_pos.shape[0], ref_pos.shape[-1]
    mapped = jnp.sum(stress_map * ref_pos[:, None], axis=2)
    ones_row = jnp.ones((slot_count, 1, points), jnp.float32)
    return jnp.concatenate([mapped, stress_map.reshape(slot_count, 9, points), ref_pos, ones_row], axis=1) * vol_pts[:, None]


def force_terms(tile_sums, ref_pos, stress_map):
    slot_count, points = ref_pos.shape[0], ref_pos.shape[-1]
    sum_ar = tile_sums[:, 0:3]
    sum_a = tile_sums[:, 3:12].reshape(slot_count, 3, 3, points)
    spread = tile_sums[:, 12:15] - tile_sums[:, 15][:, None] * ref_pos
    return jnp.sum(stress_map * spread[:, None], axis=2) + sum_ar - jnp.sum(sum_a * ref_pos[:, None], axis=2)


def tile_terms(pack_first, pack_second, map_first, map_second, step_x, step_y, section):
    zero_step = jnp.zeros_like(step_x)
    ref_a, cur_a, vol_a, health_a = positions(pack_first, zero_step, zero_step)
    ref_b, cur_b, vol_b, health_b = positions(pack_second, step_x, step_y)
    weights = bond_weights(health_a, health_b, step_x, step_y)
    if section == "shape":
        feat_a = shape_features(ref_a, cur_a, vol_a)
        feat_b = shape_features(ref_b, cur_b, vol_b)
    else:
        feat_a = force_features(ref_a, map_first, vol_a)
        feat_b = force_features(ref_b, map_second, vol_b)
    sums_a = jnp.einsum("gcj,gij->gci", feat_b, weights, precision=highest)
    sums_b = jnp.einsum("gci,gij->gcj", feat_a, weights, precision=highest)
    if section == "shape":
        return shape_terms(sums_a, ref_a, cur_a), shape_terms(sums_b, ref_b, cur_b)
    return force_terms(sums_a, ref_a, map_first), force_terms(sums_b, ref_b, map_second)


def block_sums(row_pack, row_map, section):
    rows_count, points = row_pack.shape[0], row_pack.shape[-1]
    zero_step = jnp.zeros((rows_count,), jnp.int32)
    ref_pos, cur_pos, vol_pts, health_pts = positions(row_pack, zero_step, zero_step)
    weights = bond_weights(health_pts, health_pts, zero_step, zero_step)
    if section == "shape":
        feats = shape_features(ref_pos, cur_pos, vol_pts)
        return shape_terms(jnp.einsum("gcj,gij->gci", feats, weights, precision=highest), ref_pos, cur_pos)
    stress_map = row_map.reshape(rows_count, 3, 3, points)
    feats = force_features(ref_pos, stress_map, vol_pts)
    return force_terms(jnp.einsum("gcj,gij->gci", feats, weights, precision=highest), ref_pos, stress_map)


def pair_sums(ext_pack, ext_map, slot_list, section):
    ext_x, ext_y, fields, points = ext_pack.shape
    blocks = ext_x * ext_y
    flat_pack = ext_pack.reshape(blocks, fields, points)
    slot_count = slot_list.shape[0]
    turn_count = min(slot_count, 20)
    group_size = -(-slot_count // turn_count)
    filler = jnp.full((group_size * turn_count - slot_count, 4), -1, jnp.int32)
    padded_slots = jnp.concatenate([slot_list, filler], axis=0)
    comp_width = 18 if section == "shape" else 3
    block_ids = jnp.arange(blocks, dtype=jnp.int32)

    def one_group(running, group_slots):
        usable = group_slots[:, 0] >= 0
        first_block = jnp.where(usable, group_slots[:, 0] * ext_y + group_slots[:, 1], 0)
        second_block = jnp.where(usable, group_slots[:, 2] * ext_y + group_slots[:, 3], 0)
        step_x = jnp.where(usable, group_slots[:, 2] - group_slots[:, 0], 0)
        step_y = jnp.where(usable, group_slots[:, 3] - group_slots[:, 1], 0)
        if section == "shape":
            map_first, map_second = None, None
        else:
            flat_map = ext_map.reshape(blocks, 3, 3, points)
            map_first, map_second = flat_map[first_block], flat_map[second_block]
        to_first, to_second = tile_terms(flat_pack[first_block], flat_pack[second_block], map_first, map_second, step_x, step_y, section)
        hit_first = ((first_block[:, None] == block_ids[None]) & usable[:, None]).astype(jnp.float32)
        hit_second = ((second_block[:, None] == block_ids[None]) & usable[:, None]).astype(jnp.float32)
        running = running + jnp.dot(hit_first.T, to_first.reshape(group_size, comp_width * points), precision=highest, preferred_element_type=jnp.float32)
        running = running + jnp.dot(hit_second.T, to_second.reshape(group_size, comp_width * points), precision=highest, preferred_element_type=jnp.float32)
        return running, None

    running, _ = lax.scan(one_group, jnp.zeros((blocks, comp_width * points), jnp.float32), padded_slots.reshape(turn_count, group_size, 4))
    return running.reshape(ext_x, ext_y, comp_width, points)


def product_three(left_mat, right_mat):
    entry_list = []
    for row_index in range(3):
        for col_index in range(3):
            entry_list.append(left_mat[..., 3 * row_index, :] * right_mat[..., col_index, :] + left_mat[..., 3 * row_index + 1, :] * right_mat[..., 3 + col_index, :] + left_mat[..., 3 * row_index + 2, :] * right_mat[..., 6 + col_index, :])
    return jnp.stack(entry_list, axis=-2)


def invert_three(matrix):
    entry = [matrix[..., slot_index, :] for slot_index in range(9)]
    cof_00 = entry[4] * entry[8] - entry[5] * entry[7]
    cof_01 = entry[5] * entry[6] - entry[3] * entry[8]
    cof_02 = entry[3] * entry[7] - entry[4] * entry[6]
    cof_10 = entry[2] * entry[7] - entry[1] * entry[8]
    cof_11 = entry[0] * entry[8] - entry[2] * entry[6]
    cof_12 = entry[1] * entry[6] - entry[0] * entry[7]
    cof_20 = entry[1] * entry[5] - entry[2] * entry[4]
    cof_21 = entry[2] * entry[3] - entry[0] * entry[5]
    cof_22 = entry[0] * entry[4] - entry[1] * entry[3]
    determinant = entry[0] * cof_00 + entry[1] * cof_01 + entry[2] * cof_02
    adjugate = jnp.stack([cof_00, cof_10, cof_20, cof_01, cof_11, cof_21, cof_02, cof_12, cof_22], axis=-2)
    return adjugate / determinant[..., None, :]


def material(shape_sums, damage):
    identity = jnp.eye(3, dtype=jnp.float32).reshape(9)[:, None]
    inverse = invert_three(shape_sums[..., 0:9, :] + identity)
    deform_grad = product_three(shape_sums[..., 9:18, :], inverse)
    strain = 0.5 * (product_three(deform_grad[..., transpose_order, :], deform_grad) - identity)
    strain_trace = strain[..., 0, :] + strain[..., 4, :] + strain[..., 8, :]
    second_pk = lame_first * strain_trace[..., None, :] * identity + 2.0 * shear_modulus * strain
    first_pk = product_three(deform_grad, second_pk) * (1.0 - damage.astype(jnp.float32))[..., None, :]
    return deform_grad, product_three(first_pk, inverse)


def reference(displacement, volume, health, damage, block_pairs):
    point_pack = jnp.concatenate([displacement, volume[:, :, None], health[:, :, None]], axis=2)
    padded_pack = jnp.pad(point_pack, ((1, 1), (1, 1), (0, 0), (0, 0)))
    slot_lists = block_pairs.reshape(N_GX * N_GY, PAIRS_MAX, 4)
    device_ids = jnp.arange(N_GX * N_GY, dtype=jnp.int32)
    zero_index = jnp.zeros((), jnp.int32)

    def corner_of(device):
        return ((device // N_GY) * BX_DEV).astype(jnp.int32), ((device % N_GY) * BY_DEV).astype(jnp.int32)

    def window_of(array, device):
        corner_x, corner_y = corner_of(device)
        return lax.dynamic_slice(array, (corner_x, corner_y, zero_index, zero_index), (BX_DEV + 2, BY_DEV + 2) + array.shape[2:])

    def accumulate_pairs(section, padded_map, comp_width):
        def one_device(running, items):
            device, slot_list = items
            map_window = None if section == "shape" else window_of(padded_map, device)
            tile_total = pair_sums(window_of(padded_pack, device), map_window, slot_list, section)
            corner_x, corner_y = corner_of(device)
            start = (corner_x, corner_y, zero_index, zero_index)
            current = lax.dynamic_slice(running, start, tile_total.shape)
            return lax.dynamic_update_slice(running, current + tile_total, start), None

        running = jnp.zeros((PLATE_X + 2, PLATE_Y + 2, comp_width, PTS_BLK), jnp.float32)
        running, _ = lax.scan(one_device, running, (device_ids, slot_lists))
        return running[1:-1, 1:-1]

    own_shape = lax.map(lambda row_pack: block_sums(row_pack, None, "shape"), point_pack)
    shape_sums = accumulate_pairs("shape", None, 18) + own_shape
    deform_grad, stress_map = material(shape_sums, damage)
    padded_map = jnp.pad(stress_map, ((1, 1), (1, 1), (0, 0), (0, 0)))
    own_force = lax.map(lambda row_items: block_sums(row_items[0], row_items[1], "force"), (point_pack, stress_map))
    force_density = accumulate_pairs("force", padded_map, 3) + own_force
    return deform_grad, force_density
```

```python
import functools

import jax
import jax.numpy as jnp
from jax import lax
from jax.experimental import pallas as pl
from jax.experimental.pallas import tpu as pltpu
from jax.sharding import PartitionSpec as P

LANES = 128
ROWS = 8
SIDE = 4
REACH = 3
REACH_SQ = 9
RING = 2
FIELDS = 6
VOL, HEALTH, DAMAGE = 3, 4, 5
LAME = 24.0
SHEAR = 16.0
KINDS = ((1, 0), (0, 1), (1, 1), (1, -1))
SITES = 2 * SIDE
PATCH_X = SIDE + 2 * REACH
PATCH_Y = 2 + 2 * REACH
ENTRIES = PATCH_X * PATCH_Y


def iota(shape, dim):
    return lax.broadcasted_iota(jnp.int32, shape, dim)


def divide(value, step, top):
    total = jnp.zeros_like(value)
    for k in range(1, top):
        total = total + jnp.where(value >= step * k, 1, 0)
    return total


def lanes_of(value, index):
    return jnp.take_along_axis(value, index, axis=1, mode="promise_in_bounds")


def even_odd(array, axis):
    count = lax.axis_size(axis)
    even = [(i, i ^ 1) for i in range(count) if i ^ 1 < count]
    odd = [(i, ((i + 1) ^ 1) - 1) for i in range(1, count) if ((i + 1) ^ 1) - 1 < count]
    return even, odd


def entry_used(x_at, y_at):
    return any(
        (x_at - i) ** 2 + (y_at - j) ** 2 <= REACH_SQ for i in range(SIDE) for j in range(2)
    )


ENTRY_LIST = [
    (x_at, y_at)
    for x_at in range(-REACH, SIDE + REACH)
    for y_at in range(-REACH, 2 + REACH)
    if entry_used(x_at, y_at)
]


def entry_index(x_at, y_at):
    return (x_at + REACH) * PATCH_Y + y_at + REACH


def own_row(raw, field, x, y):
    disp, vol, health, damage = raw
    if field < 3:
        return disp[x, y, field : field + 1, :]
    if field == VOL:
        return vol[x, pl.ds(y, 1), :]
    if field == HEALTH:
        return health[x, pl.ds(y, 1), :]
    return damage[x, pl.ds(y, 1), :].astype(jnp.float32)


def pack_kernel(nx, ny, disp, vol, health, damage, pairs, to_even, to_odd):
    raw = (disp, vol, health, damage)
    odd_here = lax.rem(lax.axis_index("gy"), 2)
    ext_x = nx + 2 * RING
    slots = pairs.shape[0]
    ax, ay = pairs[:, 0:1], pairs[:, 1:2]
    bx, by = pairs[:, 2:3], pairs[:, 3:4]
    kind = jnp.where(bx == ax, 1, jnp.where(by == ay, 0, jnp.where(by > ay, 2, 3)))
    code = jnp.where(ax >= 0, kind * ext_x + ax + 1, -1)
    hit_x = jnp.where(code == iota((slots, LANES), 1), 1.0, 0.0).astype(jnp.bfloat16)
    hit_y = jnp.where(ay + 1 == iota((slots, LANES), 1), 1.0, 0.0).astype(jnp.bfloat16)
    table = lax.dot_general(
        hit_y, hit_x, (((0,), (0,)), ((), ())), preferred_element_type=jnp.float32
    )[0:ROWS]
    for target, start in ((to_even, (1 - odd_here) * (ny - RING)), (to_odd, odd_here * (ny - RING))):
        for field in range(FIELDS):
            for x in range(nx):
                for y in range(RING):
                    row = (field * nx + x) * RING + y
                    target[row : row + 1, :] = own_row(raw, field, x, start + y)
        target[FIELDS * nx * RING :, :] = table


def sides(from_even, from_odd, odd_here):
    low = jnp.where(odd_here == 1, from_even[...], from_odd[...])
    high = jnp.where(odd_here == 1, from_odd[...], from_even[...])
    return low, high


def middle_kernel(nx, ny, disp, vol, health, damage, y_mine, y_even, y_odd, to_even, to_odd):
    raw = (disp, vol, health, damage)
    odd_x, odd_y = lax.rem(lax.axis_index("gx"), 2), lax.rem(lax.axis_index("gy"), 2)
    ext_y = ny + 2 * RING
    halo_rows = FIELDS * nx * RING
    is_odd = odd_y == 1
    at_row = iota((ROWS, LANES), 0)
    table = y_mine[halo_rows:, :]
    even_table = y_even[halo_rows:, :]
    odd_table = y_odd[halo_rows:, :]
    low_table = jnp.where(is_odd, even_table, odd_table)
    high_table = jnp.where(is_odd, odd_table, even_table)
    table = table + jnp.where(at_row >= ny, pltpu.roll(high_table, ny, 0), 0.0)
    table = table + jnp.where(at_row < 2 * RING, pltpu.roll(low_table, ROWS - ny, 0), 0.0)
    for target, start in ((to_even, (1 - odd_x) * (nx - RING)), (to_odd, odd_x * (nx - RING))):
        for field in range(FIELDS):
            for x in range(RING):
                base = (field * RING + x) * ext_y
                for y in range(ny):
                    target[base + RING + y : base + RING + y + 1, :] = own_row(
                        raw, field, start + x, y
                    )
                for y in range(RING):
                    halo = pl.ds((field * nx + start + x) * RING + y, 1)
                    even_row, odd_row = y_even[halo, :], y_odd[halo, :]
                    at = base + y
                    target[at : at + 1, :] = jnp.where(is_odd, even_row, odd_row)
                    at = base + RING + ny + y
                    target[at : at + 1, :] = jnp.where(is_odd, odd_row, even_row)
        target[FIELDS * RING * ext_y :, :] = table


def bond_steps(dz):
    left = REACH_SQ - dz * dz
    for dx in range(-REACH, REACH + 1):
        steps = [
            dy
            for dy in range(-REACH, REACH + 1)
            if dx * dx + dy * dy <= left and (dx, dy, dz) != (0, 0, 0)
        ]
        if steps:
            yield dx, steps


def plus(total, term):
    return term if total is None else total + term


def scaled(value, factor):
    if factor == 0 or value is None:
        return None
    if factor == 1:
        return value
    if factor == -1:
        return -value
    return value * float(factor)


def add_scaled(total, value, factor):
    if factor == 0 or value is None:
        return total
    if total is None:
        return scaled(value, factor)
    if factor == 1:
        return total + value
    if factor == -1:
        return total - value
    return total + value * float(factor)


def signed_sums(terms, order):
    even, odd = {}, {}
    for dy in sorted({abs(dy) for dy in terms}):
        if dy == 0:
            even[0] = terms[0]
        else:
            even[dy] = terms[dy] + terms[-dy]
            odd[dy] = terms[dy] - terms[-dy]
    sums = [None] * (order + 1)
    for dy, value in even.items():
        sums[0] = plus(sums[0], value)
    for dy, value in odd.items():
        sums[1] = add_scaled(sums[1], value, dy)
    if order == 2:
        for dy, value in even.items():
            sums[2] = add_scaled(sums[2], value, dy * dy)
    return sums


def product(left, right):
    return [
        sum(left[3 * a + k] * right[3 * k + b] for k in range(1, 3)) + left[3 * a] * right[b]
        for a in range(3)
        for b in range(3)
    ]


def material(shape, moment, alive):
    e = shape
    cof_00 = e[4] * e[8] - e[5] * e[7]
    cof_01 = e[5] * e[6] - e[3] * e[8]
    cof_02 = e[3] * e[7] - e[4] * e[6]
    cof_11 = e[0] * e[8] - e[2] * e[6]
    cof_12 = e[1] * e[6] - e[0] * e[7]
    cof_22 = e[0] * e[4] - e[1] * e[3]
    scale = 1.0 / (e[0] * cof_00 + e[1] * cof_01 + e[2] * cof_02)
    i00, i01, i02 = cof_00 * scale, cof_01 * scale, cof_02 * scale
    i11, i12, i22 = cof_11 * scale, cof_12 * scale, cof_22 * scale
    inverse = [i00, i01, i02, i01, i11, i12, i02, i12, i22]
    grad = product(moment, inverse)
    strain = {}
    for a in range(3):
        for b in range(a, 3):
            value = grad[a] * grad[b] + grad[3 + a] * grad[3 + b] + grad[6 + a] * grad[6 + b]
            strain[a, b] = value - 1.0 if a == b else value
    trace = strain[0, 0] + strain[1, 1] + strain[2, 2]
    second = [None] * 9
    for (a, b), value in strain.items():
        entry = value * SHEAR
        if a == b:
            entry = entry + trace * (0.5 * LAME)
        second[3 * a + b] = second[3 * b + a] = entry
    inverse = [value * alive for value in inverse]
    return grad, product(product(grad, second), inverse)


def main_kernel(
    nx, ny, disp, vol, health, damage, x_mine, y_even, y_odd, x_even, x_odd, out_grad, out_force,
    ext, turned, weighted, patch, tall, site, stress, spread, result, gathered, rows_out
):
    raw = (disp, vol, health, damage)
    odd_x, odd_y = lax.rem(lax.axis_index("gx"), 2), lax.rem(lax.axis_index("gy"), 2)
    ext_x, ext_y = nx + 2 * RING, ny + 2 * RING
    ring_y = ny + 2
    wide = 2 * ring_y
    tile = (ROWS, LANES)
    lane = iota(tile, 1)
    at_row = iota(tile, 0)
    at_x = divide(lane, wide, nx + 4)
    at_half = lane - wide * at_x
    at_y = lax.shift_right_logical(at_half, 1)
    upper = (at_half & 1) == 1

    y_low, y_high = sides(y_even, y_odd, odd_y)
    x_low, x_high = sides(x_even, x_odd, odd_x)
    side_rows = RING * ext_y
    for field in range(FIELDS):
        base = field * LANES
        ext[base : base + side_rows, :] = x_low[field * side_rows : (field + 1) * side_rows]
        high_at = base + (RING + nx) * ext_y
        ext[high_at : high_at + side_rows, :] = x_high[field * side_rows : (field + 1) * side_rows]
        for x in range(nx):
            at = base + (RING + x) * ext_y
            halo = (field * nx + x) * RING
            ext[at : at + RING, :] = y_low[halo : halo + RING]
            ext[at + RING + ny : at + 2 * RING + ny, :] = y_high[halo : halo + RING]
            for y in range(ny):
                ext[at + RING + y : at + RING + y + 1, :] = own_row(raw, field, x, y)

    for field in range(FIELDS):
        turned[field * LANES : (field + 1) * LANES, :] = ext[
            field * LANES : (field + 1) * LANES, :
        ].T
    for comp in range(3):
        weighted[comp * LANES : (comp + 1) * LANES, :] = (
            turned[comp * LANES : (comp + 1) * LANES, :]
            * turned[VOL * LANES : (VOL + 1) * LANES, :]
        )

    table = x_mine[FIELDS * side_rows :, :]
    at_e = lane - ext_x * divide(lane, ext_x, LANES // ext_x + 1)
    table = table + jnp.where(
        at_e >= nx, pltpu.roll(x_high[FIELDS * side_rows :], nx, 1), 0.0
    )
    table = table + jnp.where(
        at_e < 2 * RING, pltpu.roll(x_low[FIELDS * side_rows :], LANES - nx, 1), 0.0
    )
    link = {}
    for kind, step in enumerate(KINDS):
        for sign in (1, -1):
            move = (0, 0) if sign == 1 else (-step[0], -step[1])
            picked = lanes_of(table, kind * ext_x + at_x + 1 + move[0])
            picked = jnp.where(at_row == at_y + 1 + move[1], picked, 0.0)
            link[sign * step[0], sign * step[1]] = jnp.broadcast_to(
                jnp.sum(picked, axis=0, keepdims=True), tile
            )

    index = {
        (sx, sy): (at_x + 1 + sx) * ext_y + at_y + 1 + sy for sx in (-1, 0, 1) for sy in (-1, 0, 1)
    }

    def half_blocks(source, field, x_at, y_at):
        sx, sy0, sy1 = x_at // SIDE, y_at // SIDE, (y_at + 2) // SIDE
        i, j0, j1 = x_at % SIDE, y_at % SIDE, (y_at + 2) % SIDE
        first = source[pl.ds(field * LANES + SIDE * j0 + i, ROWS, stride=SIDE * SIDE), :]
        second = source[pl.ds(field * LANES + SIDE * j1 + i, ROWS, stride=SIDE * SIDE), :]
        return jnp.where(
            upper, lanes_of(second, index[sx, sy1]), lanes_of(first, index[sx, sy0])
        )

    masks = {}
    for x_at, y_at in ENTRY_LIST:
        sx, sy0, sy1 = x_at // SIDE, y_at // SIDE, (y_at + 2) // SIDE
        at = entry_index(x_at, y_at)
        strength = half_blocks(turned, HEALTH, x_at, y_at)
        if (sx, sy0, sy1) != (0, 0, 0):
            if (sx, sy0, sy1) not in masks:
                one = jnp.ones(tile, jnp.float32)
                masks[sx, sy0, sy1] = jnp.where(
                    upper, link.get((sx, sy1), one), link.get((sx, sy0), one)
                )
            strength = strength * masks[sx, sy0, sy1]
        patch[at] = strength
        patch[ENTRIES + at] = half_blocks(turned, VOL, x_at, y_at)
        for comp in range(3):
            patch[(2 + comp) * ENTRIES + at] = half_blocks(weighted, comp, x_at, y_at)
    for i in range(SIDE):
        for j in range(2):
            at = 2 * i + j
            tall[24 * at : 24 * at + 8, :] = jnp.zeros(tile, jnp.float32)
            tall[24 * at + 8 : 24 * at + 16, :] = patch[entry_index(i, j)]
            tall[24 * at + 16 : 24 * at + 24, :] = jnp.zeros(tile, jnp.float32)
            for comp in range(3):
                site[comp * SITES + at] = half_blocks(turned, comp, i, j)
            site[3 * SITES + at] = 1.0 - half_blocks(turned, DAMAGE, i, j)

    def shape_site(at, carry):
        base = lax.shift_right_logical(at, 1) * PATCH_Y + (at & 1)
        shape = {}
        moment = {}
        first = {}
        for dz in range(-REACH, REACH + 1):
            here = tall[pl.ds(24 * at + 8 - dz, ROWS), :]
            acc = {}
            acc_u = [{}, {}, {}]

            def gain(store, key, value, factor=1):
                store[key] = add_scaled(store.get(key), value, factor)

            for dx, steps in bond_steps(dz):
                terms = {}
                terms_u = [{}, {}, {}]
                for dy in steps:
                    k = base + (dx + REACH) * PATCH_Y + dy + REACH
                    strength = jnp.minimum(here, patch[k])
                    terms[dy] = strength * patch[ENTRIES + k]
                    for comp in range(3):
                        terms_u[comp][dy] = strength * patch[(2 + comp) * ENTRIES + k]
                t0, t1, t2 = signed_sums(terms, 2)
                if dz:
                    gain(acc, "1", t0)
                gain(acc, "x", t0, dx)
                gain(acc, "xx", t0, dx * dx)
                gain(acc, "y", t1)
                gain(acc, "xy", t1, dx)
                gain(acc, "yy", t2)
                for comp in range(3):
                    s0, s1 = signed_sums(terms_u[comp], 1)
                    if dz:
                        gain(acc_u[comp], "1", s0)
                    gain(acc_u[comp], "x", s0, dx)
                    gain(acc_u[comp], "y", s1)

            def back(value):
                if value is None or dz == 0:
                    return value
                return pltpu.roll(value, (-dz) % ROWS, 0)

            moved = {key: back(value) for key, value in acc.items()}
            for key in ("xx", "xy", "yy"):
                gain(shape, key, moved.get(key))
            gain(shape, "xz", moved.get("x"), dz)
            gain(shape, "yz", moved.get("y"), dz)
            gain(shape, "zz", moved.get("1"), dz * dz)
            gain(first, "x", moved.get("x"))
            gain(first, "y", moved.get("y"))
            gain(first, "z", moved.get("1"), dz)
            for comp in range(3):
                moved_u = {key: back(value) for key, value in acc_u[comp].items()}
                gain(moment, (comp, 0), moved_u.get("x"))
                gain(moment, (comp, 1), moved_u.get("y"))
                gain(moment, (comp, 2), moved_u.get("1"), dz)
        kxx, kxy, kyy = shape["xx"], shape["xy"], shape["yy"]
        kxz, kyz, kzz = shape["xz"], shape["yz"], shape["zz"]
        plain = [kxx, kxy, kxz, kxy, kyy, kyz, kxz, kyz, kzz]
        arm = [first["x"], first["y"], first["z"]]
        moments = []
        for a in range(3):
            here_u = site[a * SITES + at]
            for b in range(3):
                moments.append(moment[a, b] + plain[3 * a + b] - here_u * arm[b])
        full = [value + 1.0 if k in (0, 4, 8) else value for k, value in enumerate(plain)]
        grad, carried = material(full, moments, site[3 * SITES + at])
        here_vol = patch[ENTRIES + base + REACH * PATCH_Y + REACH]
        for k in range(9):
            result[k * SITES + at] = grad[k]
            stress[k * SITES + at] = carried[k] * here_vol
        for a in range(3):
            result[(9 + a) * SITES + at] = (
                carried[3 * a] * arm[0] + carried[3 * a + 1] * arm[1] + carried[3 * a + 2] * arm[2]
            )
        return carry

    lax.fori_loop(0, SITES, shape_site, 0)

    for k in range(9):
        for x_at, y_at in ENTRY_LIST:
            sx, i = x_at // SIDE, x_at % SIDE
            half, j = y_at // 2, y_at % 2
            value = stress[k * SITES + 2 * i + j]
            move = (-(wide * sx + half)) % LANES
            if move:
                value = pltpu.roll(value, move, 1)
            spread[k * ENTRIES + entry_index(x_at, y_at)] = value

    def force_site(at, carry):
        base = lax.shift_right_logical(at, 1) * PATCH_Y + (at & 1)
        here = {
            dz: tall[pl.ds(24 * at + 8 - dz, ROWS), :] for dz in range(-REACH, REACH + 1)
        }
        acc = {}
        for dx in range(-REACH, REACH + 1):
            for dy in range(-REACH, REACH + 1):
                if dx * dx + dy * dy > REACH_SQ:
                    continue
                k = base + (dx + REACH) * PATCH_Y + dy + REACH
                deep = [
                    dz
                    for dz in range(-REACH, REACH + 1)
                    if dx * dx + dy * dy + dz * dz <= REACH_SQ and (dx, dy, dz) != (0, 0, 0)
                ]
                strength = {dz: jnp.minimum(here[dz], patch[k]) for dz in deep}
                for a in range(3):
                    flat = None
                    if dx:
                        flat = add_scaled(flat, spread[3 * a * ENTRIES + k], dx)
                    if dy:
                        flat = add_scaled(flat, spread[(3 * a + 1) * ENTRIES + k], dy)
                    upright = spread[(3 * a + 2) * ENTRIES + k]
                    for dz in deep:
                        value = add_scaled(flat, upright, dz)
                        acc[a, dz] = plus(acc.get((a, dz)), strength[dz] * value)
        for a in range(3):
            total = result[(9 + a) * SITES + at]
            for dz in range(-REACH, REACH + 1):
                value = acc[a, dz]
                total = total + (pltpu.roll(value, (-dz) % ROWS, 0) if dz else value)
            result[(9 + a) * SITES + at] = total
        return carry

    lax.fori_loop(0, SITES, force_site, 0)

    blocks = nx * ny
    per_group = LANES // blocks
    slot = divide(lane, blocks, per_group + 1)
    block = lane - blocks * slot
    block_x = divide(block, ny, nx)
    block_y = block - ny * block_x
    comps = 12
    for jh in range(2):
        pick = (block_x + 1) * wide + 2 * (block_y + 1) + jh
        for i in range(SIDE):
            for j in range(2):
                for group in range(comps // per_group):
                    merged = None
                    for part in range(per_group):
                        value = lanes_of(result[(group * per_group + part) * SITES + 2 * i + j], pick)
                        merged = value if merged is None else jnp.where(slot == part, value, merged)
                    start = group * LANES + (2 * jh + j) * SIDE + i
                    gathered[pl.ds(start, ROWS, stride=SIDE * SIDE), :] = merged
    for group in range(comps // per_group):
        rows_out[group * LANES : (group + 1) * LANES, :] = gathered[
            group * LANES : (group + 1) * LANES, :
        ].T
    for x in range(nx):
        for y in range(ny):
            at = x * ny + y
            out_grad[x, y, 0:8, :] = rows_out[pl.ds(at, 8, stride=blocks), :]
            out_grad[x, y, 8:9, :] = rows_out[8 * blocks + at : 8 * blocks + at + 1, :]
            for a in range(3):
                source = (9 + a) * blocks + at
                out_force[x, y, a : a + 1, :] = rows_out[source : source + 1, :]


def local(displacement, volume, health, damage, block_pairs):
    nx, ny, points = volume.shape
    ext_y = ny + 2 * RING
    f32 = jnp.float32
    pairs = block_pairs.reshape(block_pairs.shape[2:])
    raw = (displacement, volume, health, damage)
    params = pltpu.CompilerParams(vmem_limit_bytes=48 * 1024 * 1024)
    y_shape = jax.ShapeDtypeStruct((FIELDS * nx * RING + ROWS, points), f32)
    y_to_even, y_to_odd = pl.pallas_call(
        functools.partial(pack_kernel, nx, ny),
        out_shape=(y_shape, y_shape),
        compiler_params=params,
        name="pack",
    )(*raw, pairs)
    even, odd = even_odd(None, "gy")
    y_odd = lax.ppermute(y_to_odd, "gy", odd)
    y_even = lax.ppermute(y_to_even, "gy", even)
    x_shape = jax.ShapeDtypeStruct((FIELDS * RING * ext_y + ROWS, points), f32)
    x_to_even, x_to_odd = pl.pallas_call(
        functools.partial(middle_kernel, nx, ny),
        out_shape=(x_shape, x_shape),
        compiler_params=params,
        name="middle",
    )(*raw, y_to_even, y_even, y_odd)
    even, odd = even_odd(None, "gx")
    x_odd = lax.ppermute(x_to_odd, "gx", odd)
    x_even = lax.ppermute(x_to_even, "gx", even)
    tiles = lambda count: pltpu.VMEM((count, ROWS, LANES), f32)
    rows = lambda count: pltpu.VMEM((count * LANES, LANES), f32)
    return pl.pallas_call(
        functools.partial(main_kernel, nx, ny),
        out_shape=(
            jax.ShapeDtypeStruct((nx, ny, 9, points), f32),
            jax.ShapeDtypeStruct((nx, ny, 3, points), f32),
        ),
        scratch_shapes=[
            rows(FIELDS),
            rows(FIELDS),
            rows(3),
            tiles(5 * ENTRIES),
            pltpu.VMEM((24 * SITES, LANES), f32),
            tiles(4 * SITES),
            tiles(9 * SITES),
            tiles(9 * ENTRIES),
            tiles(12 * SITES),
            rows(3),
            rows(3),
        ],
        compiler_params=params,
        name="main",
    )(*raw, x_to_even, y_even, y_odd, x_even, x_odd)


def solution(mesh):
    in_specs = (
        P("gx", "gy", None, None),
        P("gx", "gy", None),
        P("gx", "gy", None),
        P("gx", "gy", None),
        P("gx", "gy", None, None),
    )
    out_specs = (P("gx", "gy", None, None), P("gx", "gy", None, None))
    return jax.shard_map(local, mesh=mesh, in_specs=in_specs, out_specs=out_specs, check_vma=False)
```

```python
import functools

import jax
import jax.numpy as jnp
from jax import lax
from jax.experimental import pallas as pl
from jax.experimental.pallas import tpu as pltpu
from jax.sharding import PartitionSpec as P

LANES = 128
ROWS = 8
SIDE = 4
REACH = 3
REACH_SQ = 9
RING = 2
FIELDS = 6
VOL, HEALTH, DAMAGE = 3, 4, 5
LAME = 24.0
SHEAR = 16.0
KINDS = ((1, 0), (0, 1), (1, 1), (1, -1))
SITES = 2 * SIDE
PATCH_X = SIDE + 2 * REACH
PATCH_Y = 2 + 2 * REACH
ENTRIES = PATCH_X * PATCH_Y


def iota(shape, dim):
    return lax.broadcasted_iota(jnp.int32, shape, dim)


def divide(value, step, top):
    total = jnp.zeros_like(value)
    for k in range(1, top):
        total = total + jnp.where(value >= step * k, 1, 0)
    return total


def lanes_of(value, index):
    return jnp.take_along_axis(value, index, axis=1, mode="promise_in_bounds")


def even_odd(axis):
    count = lax.axis_size(axis)
    even = [(i, i ^ 1) for i in range(count) if i ^ 1 < count]
    odd = [(i, ((i + 1) ^ 1) - 1) for i in range(1, count) if ((i + 1) ^ 1) - 1 < count]
    return even, odd


def entry_used(x_at, y_at):
    return any(
        (x_at - i) ** 2 + (y_at - j) ** 2 <= REACH_SQ for i in range(SIDE) for j in range(2)
    )


ENTRY_LIST = [
    (x_at, y_at)
    for x_at in range(-REACH, SIDE + REACH)
    for y_at in range(-REACH, 2 + REACH)
    if entry_used(x_at, y_at)
]


def entry_index(x_at, y_at):
    return (x_at + REACH) * PATCH_Y + y_at + REACH


def own_rows(own, nx, ny, field, x, start, count):
    return own[pl.ds((field * nx + x) * ny + start, count), :]


def pack_kernel(nx, ny, disp, vol, health, damage, pairs, own, to_even, to_odd, here, sems):
    copies = []
    for k, (source, target) in enumerate(zip((disp, vol, health, damage, pairs), here)):
        copies.append(pltpu.make_async_copy(source, target, sems.at[k]))
        copies[-1].start()
    disp, vol, health, damage, pairs = here
    odd_here = lax.rem(lax.axis_index("gx"), 2)
    ext_x = nx + 2 * RING
    slots = pairs.shape[1]
    copies[4].wait()
    ax, ay = pairs[0:1, :], pairs[1:2, :]
    bx, by = pairs[2:3, :], pairs[3:4, :]
    kind = jnp.where(bx == ax, 1, jnp.where(by == ay, 0, jnp.where(by > ay, 2, 3)))
    code = jnp.where(ax >= 0, kind * ext_x + ax + 1, -1)
    hit_x = jnp.where(code == iota((LANES, slots), 0), 1.0, 0.0).astype(jnp.bfloat16)
    hit_y = jnp.where(ay + 1 == iota((2 * ROWS, slots), 0), 1.0, 0.0).astype(jnp.bfloat16)
    table = lax.dot_general(
        hit_y, hit_x, (((1,), (1,)), ((), ())), preferred_element_type=jnp.float32
    )[0:ROWS]
    for copy in copies[:4]:
        copy.wait()
    for x in range(nx):
        for field in range(FIELDS):
            if field < 3:
                value = disp[x, field, :, :]
            elif field == VOL:
                value = vol[x, :, :]
            elif field == HEALTH:
                value = health[x, :, :]
            else:
                value = damage[x, :, :].astype(jnp.float32)
            row = (field * nx + x) * ny
            own[row : row + ny, :] = value
    for target, start in ((to_even, (1 - odd_here) * (nx - RING)), (to_odd, odd_here * (nx - RING))):
        for field in range(FIELDS):
            row = field * RING * ny
            target[row : row + RING * ny, :] = own_rows(own, nx, ny, field, start, 0, RING * ny)
        target[FIELDS * RING * ny :, :] = table


def sides(from_even, from_odd, odd_here):
    low = jnp.where(odd_here == 1, from_even, from_odd)
    high = jnp.where(odd_here == 1, from_odd, from_even)
    return low, high


def joined(table, low, high, count, axis, at, size):
    table = table + jnp.where(at >= count, pltpu.roll(high, count, axis), 0.0)
    return table + jnp.where(at < 2 * RING, pltpu.roll(low, size - count, axis), 0.0)


def middle_kernel(nx, ny, own, x_mine, x_even, x_odd, to_even, to_odd):
    odd_x, odd_y = lax.rem(lax.axis_index("gx"), 2), lax.rem(lax.axis_index("gy"), 2)
    ext_x = nx + 2 * RING
    side_rows = RING * ny
    lane = iota((ROWS, LANES), 1)
    at_e = lane - ext_x * divide(lane, ext_x, LANES // ext_x + 1)
    low, high = sides(x_even[FIELDS * side_rows :, :], x_odd[FIELDS * side_rows :, :], odd_x)
    table = joined(x_mine[FIELDS * side_rows :, :], low, high, nx, 1, at_e, LANES)
    for target, start in ((to_even, (1 - odd_y) * (ny - RING)), (to_odd, odd_y * (ny - RING))):
        for field in range(FIELDS):
            for x in range(RING):
                halo = pl.ds((field * RING + x) * ny + start, RING)
                low, high = sides(x_even[halo, :], x_odd[halo, :], odd_x)
                row = (field * ext_x + x) * RING
                target[row : row + RING, :] = low
                row += (RING + nx) * RING
                target[row : row + RING, :] = high
            for x in range(nx):
                row = (field * ext_x + RING + x) * RING
                target[row : row + RING, :] = own_rows(own, nx, ny, field, x, start, RING)
        target[FIELDS * ext_x * RING :, :] = table


def bond_steps(dz):
    left = REACH_SQ - dz * dz
    for dx in range(-REACH, REACH + 1):
        steps = [
            dy
            for dy in range(-REACH, REACH + 1)
            if dx * dx + dy * dy <= left and (dx, dy, dz) != (0, 0, 0)
        ]
        if steps:
            yield dx, steps


def plus(total, term):
    return term if total is None else total + term


def scaled(value, factor):
    if factor == 0 or value is None:
        return None
    if factor == 1:
        return value
    if factor == -1:
        return -value
    return value * float(factor)


def add_scaled(total, value, factor):
    if factor == 0 or value is None:
        return total
    if total is None:
        return scaled(value, factor)
    if factor == 1:
        return total + value
    if factor == -1:
        return total - value
    return total + value * float(factor)


def signed_sums(terms, order):
    even, odd = {}, {}
    for dy in sorted({abs(dy) for dy in terms}):
        if dy == 0:
            even[0] = terms[0]
        else:
            even[dy] = terms[dy] + terms[-dy]
            odd[dy] = terms[dy] - terms[-dy]
    sums = [None] * (order + 1)
    for dy, value in even.items():
        sums[0] = plus(sums[0], value)
    for dy, value in odd.items():
        sums[1] = add_scaled(sums[1], value, dy)
    if order == 2:
        for dy, value in even.items():
            sums[2] = add_scaled(sums[2], value, dy * dy)
    return sums


def product(left, right):
    return [
        sum(left[3 * a + k] * right[3 * k + b] for k in range(1, 3)) + left[3 * a] * right[b]
        for a in range(3)
        for b in range(3)
    ]


def material(shape, moment, alive):
    e = shape
    cof_00 = e[4] * e[8] - e[5] * e[7]
    cof_01 = e[5] * e[6] - e[3] * e[8]
    cof_02 = e[3] * e[7] - e[4] * e[6]
    cof_11 = e[0] * e[8] - e[2] * e[6]
    cof_12 = e[1] * e[6] - e[0] * e[7]
    cof_22 = e[0] * e[4] - e[1] * e[3]
    scale = 1.0 / (e[0] * cof_00 + e[1] * cof_01 + e[2] * cof_02)
    i00, i01, i02 = cof_00 * scale, cof_01 * scale, cof_02 * scale
    i11, i12, i22 = cof_11 * scale, cof_12 * scale, cof_22 * scale
    inverse = [i00, i01, i02, i01, i11, i12, i02, i12, i22]
    grad = product(moment, inverse)
    strain = {}
    for a in range(3):
        for b in range(a, 3):
            value = grad[a] * grad[b] + grad[3 + a] * grad[3 + b] + grad[6 + a] * grad[6 + b]
            strain[a, b] = value - 1.0 if a == b else value
    trace = strain[0, 0] + strain[1, 1] + strain[2, 2]
    second = [None] * 9
    for (a, b), value in strain.items():
        entry = value * SHEAR
        if a == b:
            entry = entry + trace * (0.5 * LAME)
        second[3 * a + b] = second[3 * b + a] = entry
    inverse = [value * alive for value in inverse]
    return grad, product(product(grad, second), inverse)


def main_kernel(
    nx, ny, own, y_mine, x_even, x_odd, y_even, y_odd, out_grad, out_force,
    ext, turned, weighted, patch, tall, site, stress, spread, result, gathered, rows_out
):
    odd_x, odd_y = lax.rem(lax.axis_index("gx"), 2), lax.rem(lax.axis_index("gy"), 2)
    ext_x, ext_y = nx + 2 * RING, ny + 2 * RING
    ring_y = ny + 2
    wide = 2 * ring_y
    tile = (ROWS, LANES)
    lane = iota(tile, 1)
    at_row = iota(tile, 0)
    at_x = divide(lane, wide, nx + 4)
    at_half = lane - wide * at_x
    at_y = lax.shift_right_logical(at_half, 1)
    upper = (at_half & 1) == 1

    low_x_at, low_y_at = nx * ny, nx * ny + 2 * RING * ny
    side_x, side_y = RING * ny, ext_x * RING
    x_low, x_high = sides(x_even[0 : FIELDS * side_x, :], x_odd[0 : FIELDS * side_x, :], odd_x)
    y_low, y_high = sides(y_even[...], y_odd[...], odd_y)
    for field in range(FIELDS):
        base = field * LANES
        ext[base : base + nx * ny, :] = own_rows(own, nx, ny, field, 0, 0, nx * ny)
        at = base + low_x_at
        ext[at : at + side_x, :] = x_low[field * side_x : (field + 1) * side_x]
        ext[at + side_x : at + 2 * side_x, :] = x_high[field * side_x : (field + 1) * side_x]
        at = base + low_y_at
        ext[at : at + side_y, :] = y_low[field * side_y : (field + 1) * side_y]
        ext[at + side_y : at + 2 * side_y, :] = y_high[field * side_y : (field + 1) * side_y]

    def block_row(e, f):
        own = (e - RING) * ny + f - RING
        beside = low_x_at + jnp.where(e < RING, e, e - nx) * ny + f - RING
        above = low_y_at + jnp.where(f < RING, 0, side_y) + e * RING + jnp.where(f < RING, f, f - RING - ny)
        row = jnp.where((e < RING) | (e >= RING + nx), beside, own)
        row = jnp.where((f < RING) | (f >= RING + ny), above, row)
        return jnp.clip(row, 0, LANES - 1)

    for field in range(FIELDS):
        turned[field * LANES : (field + 1) * LANES, :] = ext[
            field * LANES : (field + 1) * LANES, :
        ].T
    for comp in range(3):
        weighted[comp * LANES : (comp + 1) * LANES, :] = (
            turned[comp * LANES : (comp + 1) * LANES, :]
            * turned[VOL * LANES : (VOL + 1) * LANES, :]
        )

    table = joined(
        y_mine[FIELDS * side_y :, :],
        y_low[FIELDS * side_y :],
        y_high[FIELDS * side_y :],
        ny,
        0,
        at_row,
        ROWS,
    )
    link = {}
    for kind, step in enumerate(KINDS):
        for sign in (1, -1):
            move = (0, 0) if sign == 1 else (-step[0], -step[1])
            picked = lanes_of(table, kind * ext_x + at_x + 1 + move[0])
            picked = jnp.where(at_row == at_y + 1 + move[1], picked, 0.0)
            link[sign * step[0], sign * step[1]] = jnp.broadcast_to(
                jnp.sum(picked, axis=0, keepdims=True), tile
            )

    index = {
        (sx, sy): block_row(at_x + 1 + sx, at_y + 1 + sy) for sx in (-1, 0, 1) for sy in (-1, 0, 1)
    }

    def half_blocks(source, field, x_at, y_at):
        sx, sy0, sy1 = x_at // SIDE, y_at // SIDE, (y_at + 2) // SIDE
        i, j0, j1 = x_at % SIDE, y_at % SIDE, (y_at + 2) % SIDE
        first = source[pl.ds(field * LANES + SIDE * j0 + i, ROWS, stride=SIDE * SIDE), :]
        second = source[pl.ds(field * LANES + SIDE * j1 + i, ROWS, stride=SIDE * SIDE), :]
        return jnp.where(
            upper, lanes_of(second, index[sx, sy1]), lanes_of(first, index[sx, sy0])
        )

    masks = {}
    for x_at, y_at in ENTRY_LIST:
        sx, sy0, sy1 = x_at // SIDE, y_at // SIDE, (y_at + 2) // SIDE
        at = entry_index(x_at, y_at)
        strength = half_blocks(turned, HEALTH, x_at, y_at)
        if (sx, sy0, sy1) != (0, 0, 0):
            if (sx, sy0, sy1) not in masks:
                one = jnp.ones(tile, jnp.float32)
                masks[sx, sy0, sy1] = jnp.where(
                    upper, link.get((sx, sy1), one), link.get((sx, sy0), one)
                )
            strength = strength * masks[sx, sy0, sy1]
        patch[at] = strength
        patch[ENTRIES + at] = half_blocks(turned, VOL, x_at, y_at)
        for comp in range(3):
            patch[(2 + comp) * ENTRIES + at] = half_blocks(weighted, comp, x_at, y_at)
    for i in range(SIDE):
        for j in range(2):
            at = 2 * i + j
            tall[24 * at : 24 * at + 8, :] = jnp.zeros(tile, jnp.float32)
            tall[24 * at + 8 : 24 * at + 16, :] = patch[entry_index(i, j)]
            tall[24 * at + 16 : 24 * at + 24, :] = jnp.zeros(tile, jnp.float32)
            for comp in range(3):
                site[comp * SITES + at] = half_blocks(turned, comp, i, j)
            site[3 * SITES + at] = 1.0 - half_blocks(turned, DAMAGE, i, j)

    def shape_site(at, carry):
        base = lax.shift_right_logical(at, 1) * PATCH_Y + (at & 1)
        shape = {}
        moment = {}
        first = {}
        for dz in range(-REACH, REACH + 1):
            here = tall[pl.ds(24 * at + 8 - dz, ROWS), :]
            acc = {}
            acc_u = [{}, {}, {}]

            def gain(store, key, value, factor=1):
                store[key] = add_scaled(store.get(key), value, factor)

            for dx, steps in bond_steps(dz):
                terms = {}
                terms_u = [{}, {}, {}]
                for dy in steps:
                    k = base + (dx + REACH) * PATCH_Y + dy + REACH
                    strength = jnp.minimum(here, patch[k])
                    terms[dy] = strength * patch[ENTRIES + k]
                    for comp in range(3):
                        terms_u[comp][dy] = strength * patch[(2 + comp) * ENTRIES + k]
                t0, t1, t2 = signed_sums(terms, 2)
                if dz:
                    gain(acc, "1", t0)
                gain(acc, "x", t0, dx)
                gain(acc, "xx", t0, dx * dx)
                gain(acc, "y", t1)
                gain(acc, "xy", t1, dx)
                gain(acc, "yy", t2)
                for comp in range(3):
                    s0, s1 = signed_sums(terms_u[comp], 1)
                    if dz:
                        gain(acc_u[comp], "1", s0)
                    gain(acc_u[comp], "x", s0, dx)
                    gain(acc_u[comp], "y", s1)

            def back(value):
                if value is None or dz == 0:
                    return value
                return pltpu.roll(value, (-dz) % ROWS, 0)

            moved = {key: back(value) for key, value in acc.items()}
            for key in ("xx", "xy", "yy"):
                gain(shape, key, moved.get(key))
            gain(shape, "xz", moved.get("x"), dz)
            gain(shape, "yz", moved.get("y"), dz)
            gain(shape, "zz", moved.get("1"), dz * dz)
            gain(first, "x", moved.get("x"))
            gain(first, "y", moved.get("y"))
            gain(first, "z", moved.get("1"), dz)
            for comp in range(3):
                moved_u = {key: back(value) for key, value in acc_u[comp].items()}
                gain(moment, (comp, 0), moved_u.get("x"))
                gain(moment, (comp, 1), moved_u.get("y"))
                gain(moment, (comp, 2), moved_u.get("1"), dz)
        kxx, kxy, kyy = shape["xx"], shape["xy"], shape["yy"]
        kxz, kyz, kzz = shape["xz"], shape["yz"], shape["zz"]
        plain = [kxx, kxy, kxz, kxy, kyy, kyz, kxz, kyz, kzz]
        arm = [first["x"], first["y"], first["z"]]
        moments = []
        for a in range(3):
            here_u = site[a * SITES + at]
            for b in range(3):
                moments.append(moment[a, b] + plain[3 * a + b] - here_u * arm[b])
        full = [value + 1.0 if k in (0, 4, 8) else value for k, value in enumerate(plain)]
        grad, carried = material(full, moments, site[3 * SITES + at])
        here_vol = patch[ENTRIES + base + REACH * PATCH_Y + REACH]
        for k in range(9):
            result[k * SITES + at] = grad[k]
            stress[k * SITES + at] = carried[k] * here_vol
        for a in range(3):
            result[(9 + a) * SITES + at] = (
                carried[3 * a] * arm[0] + carried[3 * a + 1] * arm[1] + carried[3 * a + 2] * arm[2]
            )
        return carry

    lax.fori_loop(0, SITES, shape_site, 0)

    for k in range(9):
        for x_at, y_at in ENTRY_LIST:
            sx, i = x_at // SIDE, x_at % SIDE
            half, j = y_at // 2, y_at % 2
            value = stress[k * SITES + 2 * i + j]
            move = (-(wide * sx + half)) % LANES
            if move:
                value = pltpu.roll(value, move, 1)
            spread[k * ENTRIES + entry_index(x_at, y_at)] = value

    def force_site(at, carry):
        base = lax.shift_right_logical(at, 1) * PATCH_Y + (at & 1)
        here = {
            dz: tall[pl.ds(24 * at + 8 - dz, ROWS), :] for dz in range(-REACH, REACH + 1)
        }
        acc = {}
        for dx in range(-REACH, REACH + 1):
            for dy in range(-REACH, REACH + 1):
                if dx * dx + dy * dy > REACH_SQ:
                    continue
                k = base + (dx + REACH) * PATCH_Y + dy + REACH
                deep = [
                    dz
                    for dz in range(-REACH, REACH + 1)
                    if dx * dx + dy * dy + dz * dz <= REACH_SQ and (dx, dy, dz) != (0, 0, 0)
                ]
                strength = {dz: jnp.minimum(here[dz], patch[k]) for dz in deep}
                for a in range(3):
                    flat = None
                    if dx:
                        flat = add_scaled(flat, spread[3 * a * ENTRIES + k], dx)
                    if dy:
                        flat = add_scaled(flat, spread[(3 * a + 1) * ENTRIES + k], dy)
                    upright = spread[(3 * a + 2) * ENTRIES + k]
                    for dz in deep:
                        value = add_scaled(flat, upright, dz)
                        acc[a, dz] = plus(acc.get((a, dz)), strength[dz] * value)
        for a in range(3):
            total = result[(9 + a) * SITES + at]
            for dz in range(-REACH, REACH + 1):
                value = acc[a, dz]
                total = total + (pltpu.roll(value, (-dz) % ROWS, 0) if dz else value)
            result[(9 + a) * SITES + at] = total
        return carry

    lax.fori_loop(0, SITES, force_site, 0)

    blocks = nx * ny
    per_group = LANES // blocks
    slot = divide(lane, blocks, per_group + 1)
    block = lane - blocks * slot
    block_x = divide(block, ny, nx)
    block_y = block - ny * block_x
    comps = 12
    for jh in range(2):
        pick = (block_x + 1) * wide + 2 * (block_y + 1) + jh
        for i in range(SIDE):
            for j in range(2):
                for group in range(comps // per_group):
                    merged = None
                    for part in range(per_group):
                        value = lanes_of(result[(group * per_group + part) * SITES + 2 * i + j], pick)
                        merged = value if merged is None else jnp.where(slot == part, value, merged)
                    start = group * LANES + (2 * jh + j) * SIDE + i
                    gathered[pl.ds(start, ROWS, stride=SIDE * SIDE), :] = merged
    for group in range(comps // per_group):
        rows_out[group * LANES : (group + 1) * LANES, :] = gathered[
            group * LANES : (group + 1) * LANES, :
        ].T
    for x in range(nx):
        for comp in range(comps):
            row = comp * blocks + x * ny
            value = rows_out[row : row + ny, :]
            if comp < 9:
                out_grad[x, comp, :, :] = value
            else:
                out_force[x, comp - 9, :, :] = value


def local(displacement, volume, health, damage, block_pairs):
    nx, ny, points = volume.shape
    ext_x = nx + 2 * RING
    f32 = jnp.float32
    pairs = block_pairs.reshape(block_pairs.shape[2:]).T
    raw = (displacement.transpose(0, 2, 1, 3), volume, health, damage)
    params = pltpu.CompilerParams(vmem_limit_bytes=48 * 1024 * 1024)
    x_shape = jax.ShapeDtypeStruct((FIELDS * RING * ny + ROWS, points), f32)
    own, x_to_even, x_to_odd = pl.pallas_call(
        functools.partial(pack_kernel, nx, ny),
        out_shape=(jax.ShapeDtypeStruct((FIELDS * nx * ny, points), f32), x_shape, x_shape),
        in_specs=[pl.BlockSpec(memory_space=pltpu.HBM)] * 5,
        scratch_shapes=[
            [pltpu.VMEM(a.shape, a.dtype) for a in (*raw, pairs)],
            pltpu.SemaphoreType.DMA((5,)),
        ],
        compiler_params=params,
        name="pack",
    )(*[pltpu.with_memory_space_constraint(a, pltpu.HBM) for a in (*raw, pairs)])
    even, odd = even_odd("gx")
    x_odd = lax.ppermute(x_to_odd, "gx", odd)
    x_even = lax.ppermute(x_to_even, "gx", even)
    y_shape = jax.ShapeDtypeStruct((FIELDS * ext_x * RING + ROWS, points), f32)
    y_to_even, y_to_odd = pl.pallas_call(
        functools.partial(middle_kernel, nx, ny),
        out_shape=(y_shape, y_shape),
        compiler_params=params,
        name="middle",
    )(own, x_to_even, x_even, x_odd)
    even, odd = even_odd("gy")
    y_odd = lax.ppermute(y_to_odd, "gy", odd)
    y_even = lax.ppermute(y_to_even, "gy", even)
    tiles = lambda count: pltpu.VMEM((count, ROWS, LANES), f32)
    rows = lambda count: pltpu.VMEM((count * LANES, LANES), f32)
    grad, force = pl.pallas_call(
        functools.partial(main_kernel, nx, ny),
        out_shape=(
            jax.ShapeDtypeStruct((nx, 9, ny, points), f32),
            jax.ShapeDtypeStruct((nx, 3, ny, points), f32),
        ),
        scratch_shapes=[
            rows(FIELDS),
            rows(FIELDS),
            rows(3),
            tiles(5 * ENTRIES),
            pltpu.VMEM((24 * SITES, LANES), f32),
            tiles(4 * SITES),
            tiles(9 * SITES),
            tiles(9 * ENTRIES),
            tiles(12 * SITES),
            rows(3),
            rows(3),
        ],
        compiler_params=params,
        name="main",
    )(own, y_to_even, x_even, x_odd, y_even, y_odd)
    return grad.transpose(0, 2, 1, 3), force.transpose(0, 2, 1, 3)


def solution(mesh):
    in_specs = (
        P("gx", "gy", None, None),
        P("gx", "gy", None),
        P("gx", "gy", None),
        P("gx", "gy", None),
        P("gx", "gy", None, None),
    )
    out_specs = (P("gx", "gy", None, None), P("gx", "gy", None, None))
    return jax.shard_map(local, mesh=mesh, in_specs=in_specs, out_specs=out_specs, check_vma=False)
```

```python
import functools

import jax
import jax.numpy as jnp
from jax import lax
from jax.experimental import pallas as pl
from jax.experimental.pallas import tpu as pltpu
from jax.sharding import PartitionSpec as P

LANES = 128
ROWS = 8
SIDE = 4
REACH = 3
REACH_SQ = 9
RING = 2
FIELDS = 6
VOL, HEALTH, DAMAGE = 3, 4, 5
LAME = 24.0
SHEAR = 16.0
KINDS = ((1, 0), (0, 1), (1, 1), (1, -1))
SITES = 2 * SIDE
PATCH_X = SIDE + 2 * REACH
PATCH_Y = 2 + 2 * REACH
ENTRIES = PATCH_X * PATCH_Y


def iota(shape, dim):
    return lax.broadcasted_iota(jnp.int32, shape, dim)


def divide(value, step, top):
    total = jnp.zeros_like(value)
    for k in range(1, top):
        total = total + jnp.where(value >= step * k, 1, 0)
    return total


def lanes_of(value, index):
    return jnp.take_along_axis(value, index, axis=1, mode="promise_in_bounds")


def partner(index, count, odd):
    other = ((index + 1) ^ 1) - 1 if odd else index ^ 1
    return other if 0 <= other < count else None


def swap(array, axis, odd):
    nx, ny = lax.axis_size("gx"), lax.axis_size("gy")
    to, left = {}, []
    for i in range(nx):
        for j in range(ny):
            if axis == "gx":
                other = (partner(i, nx, odd), j)
            else:
                other = (i, partner(j, ny, odd))
            if None in other:
                left.append((i, j))
            else:
                to[i, j] = other
    while left:
        one = left.pop(0)
        if not left:
            to[one] = one
            break
        other = min(left, key=lambda at: (abs(at[0] - one[0]) + abs(at[1] - one[1]), -at[0] - at[1]))
        left.remove(other)
        to[one], to[other] = other, one
    pairs = [(i * ny + j, k * ny + l) for (i, j), (k, l) in sorted(to.items())]
    return lax.ppermute(array, ("gx", "gy"), pairs)


def entry_used(x_at, y_at):
    return any(
        (x_at - i) ** 2 + (y_at - j) ** 2 <= REACH_SQ for i in range(SIDE) for j in range(2)
    )


ENTRY_LIST = [
    (x_at, y_at)
    for x_at in range(-REACH, SIDE + REACH)
    for y_at in range(-REACH, 2 + REACH)
    if entry_used(x_at, y_at)
]


def entry_index(x_at, y_at):
    return (x_at + REACH) * PATCH_Y + y_at + REACH


def own_rows(own, nx, ny, field, x, start, count):
    return own[pl.ds((field * nx + x) * ny + start, count), :]


def pack_kernel(nx, ny, disp, vol, health, damage, pairs, own, to_even, to_odd, here, sems):
    copies = []
    for k, (source, target) in enumerate(zip((disp, vol, health, damage, pairs), here)):
        copies.append(pltpu.make_async_copy(source, target, sems.at[k]))
        copies[-1].start()
    disp, vol, health, damage, pairs = here
    odd_here = lax.rem(lax.axis_index("gx"), 2)
    ext_x = nx + 2 * RING
    slots = pairs.shape[1]
    copies[4].wait()
    ax, ay = pairs[0:1, :], pairs[1:2, :]
    bx, by = pairs[2:3, :], pairs[3:4, :]
    kind = jnp.where(bx == ax, 1, jnp.where(by == ay, 0, jnp.where(by > ay, 2, 3)))
    code = jnp.where(ax >= 0, kind * ext_x + ax + 1, -1)
    hit_x = jnp.where(code == iota((LANES, slots), 0), 1.0, 0.0).astype(jnp.bfloat16)
    hit_y = jnp.where(ay + 1 == iota((2 * ROWS, slots), 0), 1.0, 0.0).astype(jnp.bfloat16)
    table = lax.dot_general(
        hit_y, hit_x, (((1,), (1,)), ((), ())), preferred_element_type=jnp.float32
    )[0:ROWS]
    for copy in copies[:4]:
        copy.wait()
    for x in range(nx):
        for field in range(FIELDS):
            if field < 3:
                value = disp[x, field, :, :]
            elif field == VOL:
                value = vol[x, :, :]
            elif field == HEALTH:
                value = health[x, :, :]
            else:
                value = damage[x, :, :].astype(jnp.float32)
            row = (field * nx + x) * ny
            own[row : row + ny, :] = value
    for target, start in ((to_even, (1 - odd_here) * (nx - RING)), (to_odd, odd_here * (nx - RING))):
        for field in range(FIELDS):
            row = field * RING * ny
            target[row : row + RING * ny, :] = own_rows(own, nx, ny, field, start, 0, RING * ny)
        target[FIELDS * RING * ny :, :] = table


def sides(from_even, from_odd, axis):
    here = lax.axis_index(axis)
    odd_here = lax.rem(here, 2) == 1
    low = jnp.where(odd_here, from_even, from_odd)
    high = jnp.where(odd_here, from_odd, from_even)
    low = jnp.where(here == 0, 0.0, low)
    return low, jnp.where(here == lax.axis_size(axis) - 1, 0.0, high)


def joined(table, low, high, count, axis, at, size):
    table = table + jnp.where(at >= count, pltpu.roll(high, count, axis), 0.0)
    return table + jnp.where(at < 2 * RING, pltpu.roll(low, size - count, axis), 0.0)


def middle_kernel(nx, ny, own, x_mine, x_even, x_odd, to_even, to_odd):
    odd_y = lax.rem(lax.axis_index("gy"), 2)
    ext_x = nx + 2 * RING
    side_rows = RING * ny
    lane = iota((ROWS, LANES), 1)
    at_e = lane - ext_x * divide(lane, ext_x, LANES // ext_x + 1)
    low, high = sides(x_even[FIELDS * side_rows :, :], x_odd[FIELDS * side_rows :, :], "gx")
    table = joined(x_mine[FIELDS * side_rows :, :], low, high, nx, 1, at_e, LANES)
    for target, start in ((to_even, (1 - odd_y) * (ny - RING)), (to_odd, odd_y * (ny - RING))):
        for field in range(FIELDS):
            for x in range(RING):
                halo = pl.ds((field * RING + x) * ny + start, RING)
                low, high = sides(x_even[halo, :], x_odd[halo, :], "gx")
                row = (field * ext_x + x) * RING
                target[row : row + RING, :] = low
                row += (RING + nx) * RING
                target[row : row + RING, :] = high
            for x in range(nx):
                row = (field * ext_x + RING + x) * RING
                target[row : row + RING, :] = own_rows(own, nx, ny, field, x, start, RING)
        target[FIELDS * ext_x * RING :, :] = table


def bond_steps(dz):
    left = REACH_SQ - dz * dz
    for dx in range(-REACH, REACH + 1):
        steps = [
            dy
            for dy in range(-REACH, REACH + 1)
            if dx * dx + dy * dy <= left and (dx, dy, dz) != (0, 0, 0)
        ]
        if steps:
            yield dx, steps


def plus(total, term):
    return term if total is None else total + term


def scaled(value, factor):
    if factor == 0 or value is None:
        return None
    if factor == 1:
        return value
    if factor == -1:
        return -value
    return value * float(factor)


def add_scaled(total, value, factor):
    if factor == 0 or value is None:
        return total
    if total is None:
        return scaled(value, factor)
    if factor == 1:
        return total + value
    if factor == -1:
        return total - value
    return total + value * float(factor)


def signed_sums(terms, order):
    even, odd = {}, {}
    for dy in sorted({abs(dy) for dy in terms}):
        if dy == 0:
            even[0] = terms[0]
        else:
            even[dy] = terms[dy] + terms[-dy]
            odd[dy] = terms[dy] - terms[-dy]
    sums = [None] * (order + 1)
    for dy, value in even.items():
        sums[0] = plus(sums[0], value)
    for dy, value in odd.items():
        sums[1] = add_scaled(sums[1], value, dy)
    if order == 2:
        for dy, value in even.items():
            sums[2] = add_scaled(sums[2], value, dy * dy)
    return sums


def product(left, right):
    return [
        sum(left[3 * a + k] * right[3 * k + b] for k in range(1, 3)) + left[3 * a] * right[b]
        for a in range(3)
        for b in range(3)
    ]


def material(shape, moment, alive):
    e = shape
    cof_00 = e[4] * e[8] - e[5] * e[7]
    cof_01 = e[5] * e[6] - e[3] * e[8]
    cof_02 = e[3] * e[7] - e[4] * e[6]
    cof_11 = e[0] * e[8] - e[2] * e[6]
    cof_12 = e[1] * e[6] - e[0] * e[7]
    cof_22 = e[0] * e[4] - e[1] * e[3]
    scale = 1.0 / (e[0] * cof_00 + e[1] * cof_01 + e[2] * cof_02)
    i00, i01, i02 = cof_00 * scale, cof_01 * scale, cof_02 * scale
    i11, i12, i22 = cof_11 * scale, cof_12 * scale, cof_22 * scale
    inverse = [i00, i01, i02, i01, i11, i12, i02, i12, i22]
    grad = product(moment, inverse)
    strain = {}
    for a in range(3):
        for b in range(a, 3):
            value = grad[a] * grad[b] + grad[3 + a] * grad[3 + b] + grad[6 + a] * grad[6 + b]
            strain[a, b] = value - 1.0 if a == b else value
    trace = strain[0, 0] + strain[1, 1] + strain[2, 2]
    second = [None] * 9
    for (a, b), value in strain.items():
        entry = value * SHEAR
        if a == b:
            entry = entry + trace * (0.5 * LAME)
        second[3 * a + b] = second[3 * b + a] = entry
    inverse = [value * alive for value in inverse]
    return grad, product(product(grad, second), inverse)


def main_kernel(
    nx, ny, own, y_mine, x_even, x_odd, y_even, y_odd, out_grad, out_force,
    ext, turned, weighted, patch, tall, site, stress, spread, result, gathered, rows_out
):
    ext_x, ext_y = nx + 2 * RING, ny + 2 * RING
    ring_y = ny + 2
    wide = 2 * ring_y
    tile = (ROWS, LANES)
    lane = iota(tile, 1)
    at_row = iota(tile, 0)
    at_x = divide(lane, wide, nx + 4)
    at_half = lane - wide * at_x
    at_y = lax.shift_right_logical(at_half, 1)
    upper = (at_half & 1) == 1

    low_x_at, low_y_at = nx * ny, nx * ny + 2 * RING * ny
    side_x, side_y = RING * ny, ext_x * RING
    x_low, x_high = sides(x_even[0 : FIELDS * side_x, :], x_odd[0 : FIELDS * side_x, :], "gx")
    y_low, y_high = sides(y_even[...], y_odd[...], "gy")
    for field in range(FIELDS):
        base = field * LANES
        ext[base : base + nx * ny, :] = own_rows(own, nx, ny, field, 0, 0, nx * ny)
        at = base + low_x_at
        ext[at : at + side_x, :] = x_low[field * side_x : (field + 1) * side_x]
        ext[at + side_x : at + 2 * side_x, :] = x_high[field * side_x : (field + 1) * side_x]
        at = base + low_y_at
        ext[at : at + side_y, :] = y_low[field * side_y : (field + 1) * side_y]
        ext[at + side_y : at + 2 * side_y, :] = y_high[field * side_y : (field + 1) * side_y]

    def block_row(e, f):
        own = (e - RING) * ny + f - RING
        beside = low_x_at + jnp.where(e < RING, e, e - nx) * ny + f - RING
        above = low_y_at + jnp.where(f < RING, 0, side_y) + e * RING + jnp.where(f < RING, f, f - RING - ny)
        row = jnp.where((e < RING) | (e >= RING + nx), beside, own)
        row = jnp.where((f < RING) | (f >= RING + ny), above, row)
        return jnp.clip(row, 0, LANES - 1)

    for field in range(FIELDS):
        turned[field * LANES : (field + 1) * LANES, :] = ext[
            field * LANES : (field + 1) * LANES, :
        ].T
    for comp in range(3):
        weighted[comp * LANES : (comp + 1) * LANES, :] = (
            turned[comp * LANES : (comp + 1) * LANES, :]
            * turned[VOL * LANES : (VOL + 1) * LANES, :]
        )

    table = joined(
        y_mine[FIELDS * side_y :, :],
        y_low[FIELDS * side_y :],
        y_high[FIELDS * side_y :],
        ny,
        0,
        at_row,
        ROWS,
    )
    link = {}
    for kind, step in enumerate(KINDS):
        for sign in (1, -1):
            move = (0, 0) if sign == 1 else (-step[0], -step[1])
            picked = lanes_of(table, kind * ext_x + at_x + 1 + move[0])
            picked = jnp.where(at_row == at_y + 1 + move[1], picked, 0.0)
            link[sign * step[0], sign * step[1]] = jnp.broadcast_to(
                jnp.sum(picked, axis=0, keepdims=True), tile
            )

    index = {
        (sx, sy): block_row(at_x + 1 + sx, at_y + 1 + sy) for sx in (-1, 0, 1) for sy in (-1, 0, 1)
    }

    def half_blocks(source, field, x_at, y_at):
        sx, sy0, sy1 = x_at // SIDE, y_at // SIDE, (y_at + 2) // SIDE
        i, j0, j1 = x_at % SIDE, y_at % SIDE, (y_at + 2) % SIDE
        first = source[pl.ds(field * LANES + SIDE * j0 + i, ROWS, stride=SIDE * SIDE), :]
        second = source[pl.ds(field * LANES + SIDE * j1 + i, ROWS, stride=SIDE * SIDE), :]
        return jnp.where(
            upper, lanes_of(second, index[sx, sy1]), lanes_of(first, index[sx, sy0])
        )

    masks = {}
    for x_at, y_at in ENTRY_LIST:
        sx, sy0, sy1 = x_at // SIDE, y_at // SIDE, (y_at + 2) // SIDE
        at = entry_index(x_at, y_at)
        strength = half_blocks(turned, HEALTH, x_at, y_at)
        if (sx, sy0, sy1) != (0, 0, 0):
            if (sx, sy0, sy1) not in masks:
                one = jnp.ones(tile, jnp.float32)
                masks[sx, sy0, sy1] = jnp.where(
                    upper, link.get((sx, sy1), one), link.get((sx, sy0), one)
                )
            strength = strength * masks[sx, sy0, sy1]
        patch[at] = strength
        patch[ENTRIES + at] = half_blocks(turned, VOL, x_at, y_at)
        for comp in range(3):
            patch[(2 + comp) * ENTRIES + at] = half_blocks(weighted, comp, x_at, y_at)
    for i in range(SIDE):
        for j in range(2):
            at = 2 * i + j
            tall[24 * at : 24 * at + 8, :] = jnp.zeros(tile, jnp.float32)
            tall[24 * at + 8 : 24 * at + 16, :] = patch[entry_index(i, j)]
            tall[24 * at + 16 : 24 * at + 24, :] = jnp.zeros(tile, jnp.float32)
            for comp in range(3):
                site[comp * SITES + at] = half_blocks(turned, comp, i, j)
            site[3 * SITES + at] = 1.0 - half_blocks(turned, DAMAGE, i, j)

    def shape_site(at, carry):
        base = lax.shift_right_logical(at, 1) * PATCH_Y + (at & 1)
        shape = {}
        moment = {}
        first = {}
        for dz in range(-REACH, REACH + 1):
            here = tall[pl.ds(24 * at + 8 - dz, ROWS), :]
            acc = {}
            acc_u = [{}, {}, {}]

            def gain(store, key, value, factor=1):
                store[key] = add_scaled(store.get(key), value, factor)

            for dx, steps in bond_steps(dz):
                terms = {}
                terms_u = [{}, {}, {}]
                for dy in steps:
                    k = base + (dx + REACH) * PATCH_Y + dy + REACH
                    strength = jnp.minimum(here, patch[k])
                    terms[dy] = strength * patch[ENTRIES + k]
                    for comp in range(3):
                        terms_u[comp][dy] = strength * patch[(2 + comp) * ENTRIES + k]
                t0, t1, t2 = signed_sums(terms, 2)
                if dz:
                    gain(acc, "1", t0)
                gain(acc, "x", t0, dx)
                gain(acc, "xx", t0, dx * dx)
                gain(acc, "y", t1)
                gain(acc, "xy", t1, dx)
                gain(acc, "yy", t2)
                for comp in range(3):
                    s0, s1 = signed_sums(terms_u[comp], 1)
                    if dz:
                        gain(acc_u[comp], "1", s0)
                    gain(acc_u[comp], "x", s0, dx)
                    gain(acc_u[comp], "y", s1)

            def back(value):
                if value is None or dz == 0:
                    return value
                return pltpu.roll(value, (-dz) % ROWS, 0)

            moved = {key: back(value) for key, value in acc.items()}
            for key in ("xx", "xy", "yy"):
                gain(shape, key, moved.get(key))
            gain(shape, "xz", moved.get("x"), dz)
            gain(shape, "yz", moved.get("y"), dz)
            gain(shape, "zz", moved.get("1"), dz * dz)
            gain(first, "x", moved.get("x"))
            gain(first, "y", moved.get("y"))
            gain(first, "z", moved.get("1"), dz)
            for comp in range(3):
                moved_u = {key: back(value) for key, value in acc_u[comp].items()}
                gain(moment, (comp, 0), moved_u.get("x"))
                gain(moment, (comp, 1), moved_u.get("y"))
                gain(moment, (comp, 2), moved_u.get("1"), dz)
        kxx, kxy, kyy = shape["xx"], shape["xy"], shape["yy"]
        kxz, kyz, kzz = shape["xz"], shape["yz"], shape["zz"]
        plain = [kxx, kxy, kxz, kxy, kyy, kyz, kxz, kyz, kzz]
        arm = [first["x"], first["y"], first["z"]]
        moments = []
        for a in range(3):
            here_u = site[a * SITES + at]
            for b in range(3):
                moments.append(moment[a, b] + plain[3 * a + b] - here_u * arm[b])
        full = [value + 1.0 if k in (0, 4, 8) else value for k, value in enumerate(plain)]
        grad, carried = material(full, moments, site[3 * SITES + at])
        here_vol = patch[ENTRIES + base + REACH * PATCH_Y + REACH]
        for k in range(9):
            result[k * SITES + at] = grad[k]
            stress[k * SITES + at] = carried[k] * here_vol
        for a in range(3):
            result[(9 + a) * SITES + at] = (
                carried[3 * a] * arm[0] + carried[3 * a + 1] * arm[1] + carried[3 * a + 2] * arm[2]
            )
        return carry

    lax.fori_loop(0, SITES, shape_site, 0)

    for k in range(9):
        for x_at, y_at in ENTRY_LIST:
            sx, i = x_at // SIDE, x_at % SIDE
            half, j = y_at // 2, y_at % 2
            value = stress[k * SITES + 2 * i + j]
            move = (-(wide * sx + half)) % LANES
            if move:
                value = pltpu.roll(value, move, 1)
            spread[k * ENTRIES + entry_index(x_at, y_at)] = value

    def force_site(at, carry):
        base = lax.shift_right_logical(at, 1) * PATCH_Y + (at & 1)
        here = {
            dz: tall[pl.ds(24 * at + 8 - dz, ROWS), :] for dz in range(-REACH, REACH + 1)
        }
        acc = {}
        for dx in range(-REACH, REACH + 1):
            for dy in range(-REACH, REACH + 1):
                if dx * dx + dy * dy > REACH_SQ:
                    continue
                k = base + (dx + REACH) * PATCH_Y + dy + REACH
                deep = [
                    dz
                    for dz in range(-REACH, REACH + 1)
                    if dx * dx + dy * dy + dz * dz <= REACH_SQ and (dx, dy, dz) != (0, 0, 0)
                ]
                strength = {dz: jnp.minimum(here[dz], patch[k]) for dz in deep}
                for a in range(3):
                    flat = None
                    if dx:
                        flat = add_scaled(flat, spread[3 * a * ENTRIES + k], dx)
                    if dy:
                        flat = add_scaled(flat, spread[(3 * a + 1) * ENTRIES + k], dy)
                    upright = spread[(3 * a + 2) * ENTRIES + k]
                    for dz in deep:
                        value = add_scaled(flat, upright, dz)
                        acc[a, dz] = plus(acc.get((a, dz)), strength[dz] * value)
        for a in range(3):
            total = result[(9 + a) * SITES + at]
            for dz in range(-REACH, REACH + 1):
                value = acc[a, dz]
                total = total + (pltpu.roll(value, (-dz) % ROWS, 0) if dz else value)
            result[(9 + a) * SITES + at] = total
        return carry

    lax.fori_loop(0, SITES, force_site, 0)

    blocks = nx * ny
    per_group = LANES // blocks
    slot = divide(lane, blocks, per_group + 1)
    block = lane - blocks * slot
    block_x = divide(block, ny, nx)
    block_y = block - ny * block_x
    comps = 12
    for jh in range(2):
        pick = (block_x + 1) * wide + 2 * (block_y + 1) + jh
        for i in range(SIDE):
            for j in range(2):
                for group in range(comps // per_group):
                    merged = None
                    for part in range(per_group):
                        value = lanes_of(result[(group * per_group + part) * SITES + 2 * i + j], pick)
                        merged = value if merged is None else jnp.where(slot == part, value, merged)
                    start = group * LANES + (2 * jh + j) * SIDE + i
                    gathered[pl.ds(start, ROWS, stride=SIDE * SIDE), :] = merged
    for group in range(comps // per_group):
        rows_out[group * LANES : (group + 1) * LANES, :] = gathered[
            group * LANES : (group + 1) * LANES, :
        ].T
    for x in range(nx):
        for comp in range(comps):
            row = comp * blocks + x * ny
            value = rows_out[row : row + ny, :]
            if comp < 9:
                out_grad[x, comp, :, :] = value
            else:
                out_force[x, comp - 9, :, :] = value


def local(displacement, volume, health, damage, block_pairs):
    nx, ny, points = volume.shape
    ext_x = nx + 2 * RING
    f32 = jnp.float32
    pairs = block_pairs.reshape(block_pairs.shape[2:]).T
    raw = (displacement.transpose(0, 2, 1, 3), volume, health, damage)
    params = pltpu.CompilerParams(vmem_limit_bytes=48 * 1024 * 1024)
    x_shape = jax.ShapeDtypeStruct((FIELDS * RING * ny + ROWS, points), f32)
    own, x_to_even, x_to_odd = pl.pallas_call(
        functools.partial(pack_kernel, nx, ny),
        out_shape=(jax.ShapeDtypeStruct((FIELDS * nx * ny, points), f32), x_shape, x_shape),
        in_specs=[pl.BlockSpec(memory_space=pltpu.HBM)] * 5,
        scratch_shapes=[
            [pltpu.VMEM(a.shape, a.dtype) for a in (*raw, pairs)],
            pltpu.SemaphoreType.DMA((5,)),
        ],
        compiler_params=params,
        name="pack",
    )(*[pltpu.with_memory_space_constraint(a, pltpu.HBM) for a in (*raw, pairs)])
    x_odd = swap(x_to_odd, "gx", True)
    x_even = swap(x_to_even, "gx", False)
    y_shape = jax.ShapeDtypeStruct((FIELDS * ext_x * RING + ROWS, points), f32)
    y_to_even, y_to_odd = pl.pallas_call(
        functools.partial(middle_kernel, nx, ny),
        out_shape=(y_shape, y_shape),
        compiler_params=params,
        name="middle",
    )(own, x_to_even, x_even, x_odd)
    y_odd = swap(y_to_odd, "gy", True)
    y_even = swap(y_to_even, "gy", False)
    tiles = lambda count: pltpu.VMEM((count, ROWS, LANES), f32)
    rows = lambda count: pltpu.VMEM((count * LANES, LANES), f32)
    grad, force = pl.pallas_call(
        functools.partial(main_kernel, nx, ny),
        out_shape=(
            jax.ShapeDtypeStruct((nx, 9, ny, points), f32),
            jax.ShapeDtypeStruct((nx, 3, ny, points), f32),
        ),
        scratch_shapes=[
            rows(FIELDS),
            rows(FIELDS),
            rows(3),
            tiles(5 * ENTRIES),
            pltpu.VMEM((24 * SITES, LANES), f32),
            tiles(4 * SITES),
            tiles(9 * SITES),
            tiles(9 * ENTRIES),
            tiles(12 * SITES),
            rows(3),
            rows(3),
        ],
        compiler_params=params,
        name="main",
    )(own, y_to_even, x_even, x_odd, y_even, y_odd)
    return grad.transpose(0, 2, 1, 3), force.transpose(0, 2, 1, 3)


def solution(mesh):
    in_specs = (
        P("gx", "gy", None, None),
        P("gx", "gy", None),
        P("gx", "gy", None),
        P("gx", "gy", None),
        P("gx", "gy", None, None),
    )
    out_specs = (P("gx", "gy", None, None), P("gx", "gy", None, None))
    return jax.shard_map(local, mesh=mesh, in_specs=in_specs, out_specs=out_specs, check_vma=False)
```

```python
import functools

import jax
import jax.numpy as jnp
from jax import lax
from jax.experimental import pallas as pl
from jax.experimental.pallas import tpu as pltpu
from jax.sharding import PartitionSpec as P

LANES = 128
ROWS = 8
SIDE = 4
REACH = 3
REACH_SQ = 9
RING = 2
FIELDS = 6
VOL, HEALTH, DAMAGE = 3, 4, 5
LAME = 24.0
SHEAR = 16.0
KINDS = ((1, 0), (0, 1), (1, 1), (1, -1))
SITES = 2 * SIDE
PATCH_X = SIDE + 2 * REACH
PATCH_Y = 2 + 2 * REACH
ENTRIES = PATCH_X * PATCH_Y
QUARTERS = PATCH_Y * PATCH_Y
COLUMN_ORDER = (0, 2, 1, 3)
CHUNK = 2


def iota(shape, dim):
    return lax.broadcasted_iota(jnp.int32, shape, dim)


def divide(value, step, top):
    total = jnp.zeros_like(value)
    for k in range(1, top):
        total = total + jnp.where(value >= step * k, 1, 0)
    return total


def lanes_of(value, index):
    return jnp.take_along_axis(value, index, axis=1, mode="promise_in_bounds")


def pieces(value):
    high = value.astype(jnp.bfloat16)
    low = (value - high.astype(jnp.float32)).astype(jnp.bfloat16)
    return jnp.concatenate([high, low], axis=0)


def moved(halves, moves):
    both = jnp.dot(halves, moves, preferred_element_type=jnp.float32)
    rows = halves.shape[0] // 2
    return both[0:rows] + both[rows:]


def partner(index, count, odd):
    other = ((index + 1) ^ 1) - 1 if odd else index ^ 1
    return other if 0 <= other < count else None


def swap(array, axis, odd):
    nx, ny = lax.axis_size("gx"), lax.axis_size("gy")
    to, left = {}, []
    for i in range(nx):
        for j in range(ny):
            if axis == "gx":
                other = (partner(i, nx, odd), j)
            else:
                other = (i, partner(j, ny, odd))
            if None in other:
                left.append((i, j))
            else:
                to[i, j] = other
    while left:
        one = left.pop(0)
        if not left:
            to[one] = one
            break
        other = min(left, key=lambda at: (abs(at[0] - one[0]) + abs(at[1] - one[1]), -at[0] - at[1]))
        left.remove(other)
        to[one], to[other] = other, one
    pairs = [(i * ny + j, k * ny + l) for (i, j), (k, l) in sorted(to.items())]
    return lax.ppermute(array, ("gx", "gy"), pairs)


def entry_list(wide, high):
    return [
        (x_at, y_at)
        for x_at in range(-REACH, wide + REACH)
        for y_at in range(-REACH, high + REACH)
        if any(
            (x_at - i) ** 2 + (y_at - j) ** 2 <= REACH_SQ for i in range(wide) for j in range(high)
        )
    ]


ENTRY_LIST = entry_list(SIDE, 2)
QUARTER_LIST = entry_list(2, 2)


SIDE_MOVES = [(0, -3)] + [(sx, y_at) for sx in (0, -1, 1) for y_at in (-2, 0, 2)] + [(0, 4)]
QUARTER_MOVES = [(x_at, half) for x_at in (-2, 0, 2) for half in (-1, 0, 1)]
QUARTER_MOVES += [(0, -2), (0, 2), (-3, 0), (4, 0)]


def lane_places(nx, ny):
    lane = iota((ROWS, LANES), 1)
    wide = 2 * (ny + 2)
    at_x = divide(lane, wide, nx + 4)
    at_half = lane - wide * at_x
    return lane, wide, at_x, lax.shift_right_logical(at_half, 1), (at_half & 1) == 1


def output_places(nx, ny):
    lane = iota((ROWS, LANES), 1)
    blocks = nx * ny
    slot = divide(lane, blocks, LANES // blocks + 1)
    block = lane - blocks * slot
    block_x = divide(block, ny, nx)
    return slot, block_x, block - ny * block_x


def moves_kernel(nx, ny, after, side_moves, quarter_moves, grad_moves, force_moves):
    lane, wide, at_x, at_y, upper = lane_places(nx, ny)
    ext_x = nx + 2 * RING
    low_x_at, low_y_at = nx * ny, nx * ny + 2 * RING * ny
    side_y = ext_x * RING
    rows = iota((2 * ROWS, LANES), 0)

    def block_row(e, f):
        own = (e - RING) * ny + f - RING
        beside = low_x_at + jnp.where(e < RING, e, e - nx) * ny + f - RING
        above = low_y_at + jnp.where(f < RING, 0, side_y) + e * RING
        above = above + jnp.where(f < RING, f, f - RING - ny)
        row = jnp.where((e < RING) | (e >= RING + nx), beside, own)
        return jnp.where((f < RING) | (f >= RING + ny), above, row)

    def fill(target, column, source):
        source = jnp.concatenate([source, source], axis=0)
        for row in range(0, target.shape[0], 2 * ROWS):
            hit = jnp.where(source == rows + row, 1.0, 0.0).astype(jnp.bfloat16)
            target[row : row + 2 * ROWS, column * LANES : (column + 1) * LANES] = hit

    for column, (sx, y_at) in enumerate(SIDE_MOVES):
        sources = []
        for at in (y_at, y_at + 2):
            part = (at % SIDE - y_at % 2) // 2
            sources.append(part * LANES + block_row(at_x + 1 + sx, at_y + 1 + at // SIDE))
        source = jnp.where(upper, sources[1], sources[0])
        fill(side_moves, column, jnp.where(at_x < nx + 2, source, -1))

    quarter_x = divide(lane, 2 * ny, 2 * nx)
    quarter_y = lane - 2 * ny * quarter_x
    right = (quarter_x & 1) == 1
    owner = (lax.shift_right_logical(quarter_x, 1) + 1) * wide + quarter_y + 2
    for column, (x_at, half) in enumerate(QUARTER_MOVES):
        sources = []
        for at in (x_at, x_at + 2):
            part = (at % SIDE - x_at % 2) // 2
            sources.append(part * LANES + owner + (wide * (at // SIDE) + half))
        fill(quarter_moves, column, jnp.where(right, sources[1], sources[0]))

    slot, block_x, block_y = output_places(nx, ny)
    for jh in range(2):
        fill(grad_moves, jh, slot * LANES + (block_x + 1) * wide + 2 * (block_y + 1) + jh)
    for ih in range(2):
        for jh in range(2):
            source = slot * LANES + (2 * block_x + ih) * 2 * ny + 2 * block_y + jh
            fill(force_moves, 2 * ih + jh, jnp.where(slot < 3, source, -1))


def entry_index(x_at, y_at):
    return (x_at + REACH) * PATCH_Y + y_at + REACH


def own_rows(own, nx, ny, field, x, start, count):
    return own[pl.ds((field * nx + x) * ny + start, count), :]


def pack_kernel(nx, ny, disp, vol, health, damage, pairs, own, to_even, to_odd, here, sems):
    copies = []
    for k, (source, target) in enumerate(zip((disp, vol, health, damage, pairs), here)):
        copies.append(pltpu.make_async_copy(source, target, sems.at[k]))
        copies[-1].start()
    disp, vol, health, damage, pairs = here
    odd_here = lax.rem(lax.axis_index("gx"), 2)
    ext_x = nx + 2 * RING
    slots = pairs.shape[1]
    copies[4].wait()
    ax, ay = pairs[0:1, :], pairs[1:2, :]
    bx, by = pairs[2:3, :], pairs[3:4, :]
    kind = jnp.where(bx == ax, 1, jnp.where(by == ay, 0, jnp.where(by > ay, 2, 3)))
    code = jnp.where(ax >= 0, kind * ext_x + ax + 1, -1)
    hit_x = jnp.where(code == iota((LANES, slots), 0), 1.0, 0.0).astype(jnp.bfloat16)
    hit_y = jnp.where(ay + 1 == iota((2 * ROWS, slots), 0), 1.0, 0.0).astype(jnp.bfloat16)
    table = lax.dot_general(
        hit_y, hit_x, (((1,), (1,)), ((), ())), preferred_element_type=jnp.float32
    )[0:ROWS]
    for copy in copies[:4]:
        copy.wait()
    for x in range(nx):
        for field in range(FIELDS):
            if field < 3:
                value = disp[x, field, :, :]
            elif field == VOL:
                value = vol[x, :, :]
            elif field == HEALTH:
                value = health[x, :, :]
            else:
                value = damage[x, :, :].astype(jnp.float32)
            row = (field * nx + x) * ny
            own[row : row + ny, :] = value
    for target, start in ((to_even, (1 - odd_here) * (nx - RING)), (to_odd, odd_here * (nx - RING))):
        for field in range(FIELDS):
            row = field * RING * ny
            target[row : row + RING * ny, :] = own_rows(own, nx, ny, field, start, 0, RING * ny)
        target[FIELDS * RING * ny :, :] = table


def sides(from_even, from_odd, axis):
    here = lax.axis_index(axis)
    odd_here = lax.rem(here, 2) == 1
    low = jnp.where(odd_here, from_even, from_odd)
    high = jnp.where(odd_here, from_odd, from_even)
    low = jnp.where(here == 0, 0.0, low)
    return low, jnp.where(here == lax.axis_size(axis) - 1, 0.0, high)


def joined(table, low, high, count, axis, at, size):
    table = table + jnp.where(at >= count, pltpu.roll(high, count, axis), 0.0)
    return table + jnp.where(at < 2 * RING, pltpu.roll(low, size - count, axis), 0.0)


def middle_kernel(nx, ny, own, x_mine, x_even, x_odd, to_even, to_odd):
    odd_y = lax.rem(lax.axis_index("gy"), 2)
    ext_x = nx + 2 * RING
    side_rows = RING * ny
    lane = iota((ROWS, LANES), 1)
    at_e = lane - ext_x * divide(lane, ext_x, LANES // ext_x + 1)
    low, high = sides(x_even[FIELDS * side_rows :, :], x_odd[FIELDS * side_rows :, :], "gx")
    table = joined(x_mine[FIELDS * side_rows :, :], low, high, nx, 1, at_e, LANES)
    for target, start in ((to_even, (1 - odd_y) * (ny - RING)), (to_odd, odd_y * (ny - RING))):
        for field in range(FIELDS):
            for x in range(RING):
                halo = pl.ds((field * RING + x) * ny + start, RING)
                low, high = sides(x_even[halo, :], x_odd[halo, :], "gx")
                row = (field * ext_x + x) * RING
                target[row : row + RING, :] = low
                row += (RING + nx) * RING
                target[row : row + RING, :] = high
            for x in range(nx):
                row = (field * ext_x + RING + x) * RING
                target[row : row + RING, :] = own_rows(own, nx, ny, field, x, start, RING)
        target[FIELDS * ext_x * RING :, :] = table


def bond_steps(dz):
    left = REACH_SQ - dz * dz
    for dx in range(-REACH, REACH + 1):
        steps = [
            dy
            for dy in range(-REACH, REACH + 1)
            if dx * dx + dy * dy <= left and (dx, dy, dz) != (0, 0, 0)
        ]
        if steps:
            yield dx, steps


def plus(total, term):
    return term if total is None else total + term


def scaled(value, factor):
    if factor == 0 or value is None:
        return None
    if factor == 1:
        return value
    if factor == -1:
        return -value
    return value * float(factor)


def add_scaled(total, value, factor):
    if factor == 0 or value is None:
        return total
    if total is None:
        return scaled(value, factor)
    if factor == 1:
        return total + value
    if factor == -1:
        return total - value
    return total + value * float(factor)


def signed_sums(terms, order):
    even, odd = {}, {}
    for dy in sorted({abs(dy) for dy in terms}):
        if dy == 0:
            even[0] = terms[0]
        else:
            even[dy] = terms[dy] + terms[-dy]
            odd[dy] = terms[dy] - terms[-dy]
    sums = [None] * (order + 1)
    for dy, value in even.items():
        sums[0] = plus(sums[0], value)
    for dy, value in odd.items():
        sums[1] = add_scaled(sums[1], value, dy)
    if order == 2:
        for dy, value in even.items():
            sums[2] = add_scaled(sums[2], value, dy * dy)
    return sums


def product(left, right):
    return [
        sum(left[3 * a + k] * right[3 * k + b] for k in range(1, 3)) + left[3 * a] * right[b]
        for a in range(3)
        for b in range(3)
    ]


def material(shape, moment, alive):
    e = shape
    cof_00 = e[4] * e[8] - e[5] * e[7]
    cof_01 = e[5] * e[6] - e[3] * e[8]
    cof_02 = e[3] * e[7] - e[4] * e[6]
    cof_11 = e[0] * e[8] - e[2] * e[6]
    cof_12 = e[1] * e[6] - e[0] * e[7]
    cof_22 = e[0] * e[4] - e[1] * e[3]
    scale = 1.0 / (e[0] * cof_00 + e[1] * cof_01 + e[2] * cof_02)
    i00, i01, i02 = cof_00 * scale, cof_01 * scale, cof_02 * scale
    i11, i12, i22 = cof_11 * scale, cof_12 * scale, cof_22 * scale
    inverse = [i00, i01, i02, i01, i11, i12, i02, i12, i22]
    grad = product(moment, inverse)
    strain = {}
    for a in range(3):
        for b in range(a, 3):
            value = grad[a] * grad[b] + grad[3 + a] * grad[3 + b] + grad[6 + a] * grad[6 + b]
            strain[a, b] = value - 1.0 if a == b else value
    trace = strain[0, 0] + strain[1, 1] + strain[2, 2]
    second = [None] * 9
    for (a, b), value in strain.items():
        entry = value * SHEAR
        if a == b:
            entry = entry + trace * (0.5 * LAME)
        second[3 * a + b] = second[3 * b + a] = entry
    inverse = [value * alive for value in inverse]
    return grad, product(product(grad, second), inverse)


def main_kernel(
    nx, ny, own, y_mine, x_even, x_odd, y_even, y_odd, side_moves, quarter_moves, grad_moves,
    force_moves, out_grad, out_force, ext, turned, weighted, patch, tall, site, stress, spread,
    spread_health, tall_quarter, start_force, result, gathered, rows_out, hold_grad, hold_force, sems
):
    ext_x, ext_y = nx + 2 * RING, ny + 2 * RING
    tile = (ROWS, LANES)
    at_row = iota(tile, 0)
    lane, wide, at_x, at_y, upper = lane_places(nx, ny)

    low_x_at, low_y_at = nx * ny, nx * ny + 2 * RING * ny
    side_x, side_y = RING * ny, ext_x * RING
    x_low, x_high = sides(x_even[0 : FIELDS * side_x, :], x_odd[0 : FIELDS * side_x, :], "gx")
    y_low, y_high = sides(y_even[...], y_odd[...], "gy")
    for field in range(FIELDS):
        base = field * LANES
        ext[base : base + nx * ny, :] = own_rows(own, nx, ny, field, 0, 0, nx * ny)
        at = base + low_x_at
        ext[at : at + side_x, :] = x_low[field * side_x : (field + 1) * side_x]
        ext[at + side_x : at + 2 * side_x, :] = x_high[field * side_x : (field + 1) * side_x]
        at = base + low_y_at
        ext[at : at + side_y, :] = y_low[field * side_y : (field + 1) * side_y]
        ext[at + side_y : at + 2 * side_y, :] = y_high[field * side_y : (field + 1) * side_y]
        at += 2 * side_y
        if at < base + LANES:
            ext[at : base + LANES, :] = jnp.zeros((base + LANES - at, LANES), jnp.float32)

    for field in range(FIELDS):
        turned[field * LANES : (field + 1) * LANES, :] = ext[
            field * LANES : (field + 1) * LANES, :
        ].T
    for comp in range(3):
        weighted[comp * LANES : (comp + 1) * LANES, :] = (
            turned[comp * LANES : (comp + 1) * LANES, :]
            * turned[VOL * LANES : (VOL + 1) * LANES, :]
        )

    table = joined(
        y_mine[FIELDS * side_y :, :],
        y_low[FIELDS * side_y :],
        y_high[FIELDS * side_y :],
        ny,
        0,
        at_row,
        ROWS,
    )
    link = {}
    for kind, step in enumerate(KINDS):
        for sign in (1, -1):
            move = (0, 0) if sign == 1 else (-step[0], -step[1])
            picked = lanes_of(table, kind * ext_x + at_x + 1 + move[0])
            picked = jnp.where(at_row == at_y + 1 + move[1], picked, 0.0)
            link[sign * step[0], sign * step[1]] = jnp.broadcast_to(
                jnp.sum(picked, axis=0, keepdims=True), tile
            )

    masks = {}

    def mask_of(sx, sy0, sy1):
        if (sx, sy0, sy1) not in masks:
            one = jnp.ones(tile, jnp.float32)
            masks[sx, sy0, sy1] = jnp.where(
                upper, link.get((sx, sy1), one), link.get((sx, sy0), one)
            )
        return masks[sx, sy0, sy1]

    def points(source, field, i, odd):
        start = field * LANES + SIDE * odd + i
        near = source[pl.ds(start, ROWS, stride=SIDE * SIDE), :]
        far = source[pl.ds(start + 2 * SIDE, ROWS, stride=SIDE * SIDE), :]
        return jnp.concatenate([near, far], axis=1)

    def columns(moves, first, count):
        return moves[:, first * LANES : (first + count) * LANES]

    moving = ((turned, HEALTH), (turned, VOL), (weighted, 0), (weighted, 1), (weighted, 2))
    parts = pieces(
        jnp.concatenate(
            [
                points(source, field, i, odd)
                for odd in range(2)
                for i in range(SIDE)
                for source, field in moving
            ],
            axis=0,
        )
    )

    def keep(values, step, sx, y_even):
        row = 0
        for odd in range(2):
            y_at = y_even + odd
            for i in range(SIDE):
                x_at = i + SIDE * sx
                for field in range(len(moving)):
                    if (x_at, y_at) in ENTRY_LIST:
                        value = values[row : row + ROWS, step * LANES : (step + 1) * LANES]
                        links = (sx, y_at // SIDE, (y_at + 2) // SIDE)
                        if field == 0 and links != (0, 0, 0):
                            value = value * mask_of(*links)
                        patch[field * ENTRIES + entry_index(x_at, y_at)] = value
                    row += ROWS

    for first in range(0, len(SIDE_MOVES), CHUNK):
        chosen = SIDE_MOVES[first : first + CHUNK]
        values = moved(parts, columns(side_moves, first, len(chosen)))
        for step, (sx, y_at) in enumerate(chosen):
            keep(values, step, sx, y_at - y_at % 2)

    fixed = [0, 1, 2, DAMAGE]
    values = moved(
        pieces(
            jnp.concatenate(
                [points(turned, f, i, odd) for odd in range(2) for i in range(SIDE) for f in fixed],
                axis=0,
            )
        ),
        columns(side_moves, SIDE_MOVES.index((0, 0)), 1),
    )
    for i in range(SIDE):
        for j in range(2):
            at = 2 * i + j
            tall[24 * at : 24 * at + 8, :] = jnp.zeros(tile, jnp.float32)
            tall[24 * at + 8 : 24 * at + 16, :] = patch[entry_index(i, j)]
            tall[24 * at + 16 : 24 * at + 24, :] = jnp.zeros(tile, jnp.float32)
            for k in range(4):
                row = ((j * SIDE + i) * 4 + k) * ROWS
                value = values[row : row + ROWS]
                site[k * SITES + at] = value if k < 3 else 1.0 - value

    def shape_site(i, j):
        at = 2 * i + j
        base = i * PATCH_Y + j
        shape = {}
        moment = {}
        first = {}
        def gain(store, key, value, factor=1):
            store[key] = add_scaled(store.get(key), value, factor)

        for depths in ((0,), (1, -1), (2, -2), (3, -3)):
            here = {dz: tall[pl.ds(24 * at + 8 - dz, ROWS), :] for dz in depths}
            acc = {dz: {} for dz in depths}
            acc_u = {dz: [{}, {}, {}] for dz in depths}
            for dx, steps in bond_steps(depths[0]):
                terms = {dz: {} for dz in depths}
                terms_u = {dz: [{}, {}, {}] for dz in depths}
                for dy in steps:
                    k = base + (dx + REACH) * PATCH_Y + dy + REACH
                    limit = patch[k]
                    amounts = [patch[(1 + c) * ENTRIES + k] for c in range(4)]
                    for dz in depths:
                        strength = jnp.minimum(here[dz], limit)
                        terms[dz][dy] = strength * amounts[0]
                        for comp in range(3):
                            terms_u[dz][comp][dy] = strength * amounts[1 + comp]
                for dz in depths:
                    t0, t1, t2 = signed_sums(terms[dz], 2)
                    if dz:
                        gain(acc[dz], "1", t0)
                    gain(acc[dz], "x", t0, dx)
                    gain(acc[dz], "xx", t0, dx * dx)
                    gain(acc[dz], "y", t1)
                    gain(acc[dz], "xy", t1, dx)
                    gain(acc[dz], "yy", t2)
                    for comp in range(3):
                        s0, s1 = signed_sums(terms_u[dz][comp], 1)
                        if dz:
                            gain(acc_u[dz][comp], "1", s0)
                        gain(acc_u[dz][comp], "x", s0, dx)
                        gain(acc_u[dz][comp], "y", s1)

            for dz in depths:

                def back(value):
                    if value is None or dz == 0:
                        return value
                    return pltpu.roll(value, (-dz) % ROWS, 0)

                moved = {key: back(value) for key, value in acc[dz].items()}
                for key in ("xx", "xy", "yy"):
                    gain(shape, key, moved.get(key))
                gain(shape, "xz", moved.get("x"), dz)
                gain(shape, "yz", moved.get("y"), dz)
                gain(shape, "zz", moved.get("1"), dz * dz)
                gain(first, "x", moved.get("x"))
                gain(first, "y", moved.get("y"))
                gain(first, "z", moved.get("1"), dz)
                for comp in range(3):
                    moved_u = {key: back(value) for key, value in acc_u[dz][comp].items()}
                    gain(moment, (comp, 0), moved_u.get("x"))
                    gain(moment, (comp, 1), moved_u.get("y"))
                    gain(moment, (comp, 2), moved_u.get("1"), dz)
        kxx, kxy, kyy = shape["xx"], shape["xy"], shape["yy"]
        kxz, kyz, kzz = shape["xz"], shape["yz"], shape["zz"]
        plain = [kxx, kxy, kxz, kxy, kyy, kyz, kxz, kyz, kzz]
        arm = [first["x"], first["y"], first["z"]]
        moments = []
        for a in range(3):
            here_u = site[a * SITES + at]
            for b in range(3):
                moments.append(moment[a, b] + plain[3 * a + b] - here_u * arm[b])
        full = [value + 1.0 if k in (0, 4, 8) else value for k, value in enumerate(plain)]
        grad, carried = material(full, moments, site[3 * SITES + at])
        here_vol = patch[ENTRIES + base + REACH * PATCH_Y + REACH]
        for k in range(9):
            result[k * SITES + at] = grad[k]
            stress[k * SITES + at] = carried[k] * here_vol
        for a in range(3):
            result[(9 + a) * SITES + at] = (
                carried[3 * a] * arm[0] + carried[3 * a + 1] * arm[1] + carried[3 * a + 2] * arm[2]
            )

    def quarter_at(x_at, y_at):
        return (x_at + REACH) * PATCH_Y + y_at + REACH

    def site_pairs(source, first, odd, j, count):
        return [
            jnp.concatenate(
                [source[first + k * SITES + 2 * i + j] for i in (odd, odd + 2)], axis=1
            )
            for k in range(count)
        ]

    def quarter_entries(odd):
        parts = [part for j in range(2) for part in site_pairs(stress, 0, odd, j, 9)]
        parts = pieces(jnp.concatenate(parts, axis=0))
        for first in range(0, len(QUARTER_MOVES), CHUNK):
            chosen = QUARTER_MOVES[first : first + CHUNK]
            values = moved(parts, columns(quarter_moves, first, len(chosen)))
            for step, (x_even, half) in enumerate(chosen):
                row = 0
                x_at = x_even - x_even % 2 + odd
                for j in range(2):
                    y_at = 2 * half + j
                    for k in range(9):
                        if (x_at, y_at) in QUARTER_LIST:
                            value = values[row : row + ROWS, step * LANES : (step + 1) * LANES]
                            spread[k * QUARTERS + quarter_at(x_at, y_at)] = value
                        row += ROWS

    own_moves = columns(quarter_moves, QUARTER_MOVES.index((0, 0)), 1)

    def quarter_health():
        values = moved(
            pieces(jnp.concatenate(
                [
                    jnp.concatenate(
                        [patch[entry_index(x_at, y_at)], patch[entry_index(x_at + 2, y_at)]], axis=1
                    )
                    for x_at, y_at in QUARTER_LIST
                ],
                axis=0,
            )),
            own_moves,
        )
        for k, (x_at, y_at) in enumerate(QUARTER_LIST):
            value = values[k * ROWS : (k + 1) * ROWS]
            spread_health[quarter_at(x_at, y_at)] = value
            if 0 <= x_at < 2 and 0 <= y_at < 2:
                row = 24 * (2 * x_at + y_at)
                tall_quarter[row : row + 8, :] = jnp.zeros(tile, jnp.float32)
                tall_quarter[row + 8 : row + 16, :] = value
                tall_quarter[row + 16 : row + 24, :] = jnp.zeros(tile, jnp.float32)

    blocks = nx * ny
    per_group = LANES // blocks

    def gather_grad(group, comps):
        sites = [
            jnp.concatenate([result[comp * SITES + at] for comp in comps], axis=1)
            for at in range(SITES)
        ]
        values = moved(pieces(jnp.concatenate(sites, axis=0)), grad_moves[0 : len(comps) * LANES, :])
        for at in range(SITES):
            for jh in range(2):
                start = group * LANES + (2 * jh + at % 2) * SIDE + at // 2
                gathered[pl.ds(start, ROWS, stride=SIDE * SIDE), :] = values[
                    at * ROWS : (at + 1) * ROWS, jh * LANES : (jh + 1) * LANES
                ]

    def group_out(group, comps, target, first):
        rows_out[group * LANES : (group + 1) * LANES, :] = gathered[
            group * LANES : (group + 1) * LANES, :
        ].T
        for part, comp in enumerate(comps):
            for x in range(nx):
                row = group * LANES + part * blocks + x * ny
                target[x, comp - first, :, :] = rows_out[row : row + ny, :]

    grad_groups = [list(range(9))[k : k + per_group] for k in range(0, 9, per_group)]

    for i in COLUMN_ORDER:
        for j in range(2):
            shape_site(i, j)
        if i == COLUMN_ORDER[1]:
            quarter_entries(0)
            quarter_health()
    quarter_entries(1)
    for group, comps in enumerate(grad_groups):
        gather_grad(group, comps)
        group_out(group, comps, hold_grad, 0)
    grad_copy = pltpu.make_async_copy(hold_grad, out_grad, sems.at[0])
    grad_copy.start()

    parts = [
        part for i in range(2) for j in range(2) for part in site_pairs(result, 9 * SITES, i, j, 3)
    ]
    values = moved(pieces(jnp.concatenate(parts, axis=0)), own_moves)
    for k in range(12):
        start_force[k] = values[k * ROWS : (k + 1) * ROWS]

    def force_site(i, j):
        at = 2 * i + j
        base = (i + REACH) * PATCH_Y + j + REACH
        here = {
            dz: tall_quarter[24 * at + 8 - dz : 24 * at + 16 - dz, :]
            for dz in range(-REACH, REACH + 1)
        }
        acc = {}
        for dx in range(-REACH, REACH + 1):
            for dy in range(-REACH, REACH + 1):
                if dx * dx + dy * dy > REACH_SQ:
                    continue
                k = base + dx * PATCH_Y + dy
                deep = [
                    dz
                    for dz in range(-REACH, REACH + 1)
                    if dx * dx + dy * dy + dz * dz <= REACH_SQ and (dx, dy, dz) != (0, 0, 0)
                ]
                strength = {dz: jnp.minimum(here[dz], spread_health[k]) for dz in deep}
                for a in range(3):
                    flat = None
                    if dx:
                        flat = add_scaled(flat, spread[3 * a * QUARTERS + k], dx)
                    if dy:
                        flat = add_scaled(flat, spread[(3 * a + 1) * QUARTERS + k], dy)
                    upright = spread[(3 * a + 2) * QUARTERS + k]
                    for dz in deep:
                        value = add_scaled(flat, upright, dz)
                        acc[a, dz] = plus(acc.get((a, dz)), strength[dz] * value)
        for a in range(3):
            total = start_force[3 * at + a]
            for dz in range(-REACH, REACH + 1):
                value = acc[a, dz]
                total = total + (pltpu.roll(value, (-dz) % ROWS, 0) if dz else value)
            start_force[3 * at + a] = total

    for i in range(2):
        for j in range(2):
            force_site(i, j)
    group = len(grad_groups)
    sites = [
        jnp.concatenate([start_force[3 * at + a] for a in range(3)], axis=1) for at in range(4)
    ]
    values = moved(pieces(jnp.concatenate(sites, axis=0)), force_moves[...])
    for at in range(4):
        for ih in range(2):
            for jh in range(2):
                start = group * LANES + (2 * jh + at % 2) * SIDE + 2 * ih + at // 2
                column = (2 * ih + jh) * LANES
                gathered[pl.ds(start, ROWS, stride=SIDE * SIDE), :] = values[
                    at * ROWS : (at + 1) * ROWS, column : column + LANES
                ]
    group_out(group, [9, 10, 11], hold_force, 9)
    force_copy = pltpu.make_async_copy(hold_force, out_force, sems.at[1])
    force_copy.start()
    grad_copy.wait()
    force_copy.wait()


def local(displacement, volume, health, damage, block_pairs):
    nx, ny, points = volume.shape
    ext_x = nx + 2 * RING
    f32 = jnp.float32
    pairs = block_pairs.reshape(block_pairs.shape[2:]).T
    raw = (displacement.transpose(0, 2, 1, 3), volume, health, damage)
    params = pltpu.CompilerParams(vmem_limit_bytes=48 * 1024 * 1024)
    x_shape = jax.ShapeDtypeStruct((FIELDS * RING * ny + ROWS, points), f32)
    own, x_to_even, x_to_odd = pl.pallas_call(
        functools.partial(pack_kernel, nx, ny),
        out_shape=(jax.ShapeDtypeStruct((FIELDS * nx * ny, points), f32), x_shape, x_shape),
        in_specs=[pl.BlockSpec(memory_space=pltpu.HBM)] * 5,
        scratch_shapes=[
            [pltpu.VMEM(a.shape, a.dtype) for a in (*raw, pairs)],
            pltpu.SemaphoreType.DMA((5,)),
        ],
        compiler_params=params,
        name="pack",
    )(*[pltpu.with_memory_space_constraint(a, pltpu.HBM) for a in (*raw, pairs)])
    x_odd = swap(x_to_odd, "gx", True)
    x_even = swap(x_to_even, "gx", False)
    move_shapes = [
        jax.ShapeDtypeStruct((height * LANES, width * LANES), jnp.bfloat16)
        for height, width in (
            (2, len(SIDE_MOVES)),
            (2, len(QUARTER_MOVES)),
            (LANES // (nx * ny), 2),
            (3, 4),
        )
    ]
    moves = pl.pallas_call(
        functools.partial(moves_kernel, nx, ny),
        out_shape=move_shapes,
        in_specs=[pl.BlockSpec(memory_space=pl.ANY)],
        compiler_params=params,
        name="moves",
    )(x_to_even)
    y_shape = jax.ShapeDtypeStruct((FIELDS * ext_x * RING + ROWS, points), f32)
    y_to_even, y_to_odd = pl.pallas_call(
        functools.partial(middle_kernel, nx, ny),
        out_shape=(y_shape, y_shape),
        compiler_params=params,
        name="middle",
    )(own, x_to_even, x_even, x_odd)
    y_odd = swap(y_to_odd, "gy", True)
    y_even = swap(y_to_even, "gy", False)
    tiles = lambda count: pltpu.VMEM((count, ROWS, LANES), f32)
    rows = lambda count: pltpu.VMEM((count * LANES, LANES), f32)
    grad, force = pl.pallas_call(
        functools.partial(main_kernel, nx, ny),
        out_shape=(
            jax.ShapeDtypeStruct((nx, 9, ny, points), f32),
            jax.ShapeDtypeStruct((nx, 3, ny, points), f32),
        ),
        scratch_shapes=[
            rows(FIELDS),
            rows(FIELDS),
            rows(3),
            tiles(5 * ENTRIES),
            pltpu.VMEM((24 * SITES, LANES), f32),
            tiles(4 * SITES),
            tiles(9 * SITES),
            tiles(9 * QUARTERS),
            tiles(QUARTERS),
            pltpu.VMEM((24 * 4, LANES), f32),
            tiles(12),
            tiles(12 * SITES),
            rows(4),
            rows(4),
            pltpu.VMEM((nx, 9, ny, points), f32),
            pltpu.VMEM((nx, 3, ny, points), f32),
            pltpu.SemaphoreType.DMA((2,)),
        ],
        out_specs=(pl.BlockSpec(memory_space=pltpu.HBM),) * 2,
        compiler_params=params,
        name="main",
    )(own, y_to_even, x_even, x_odd, y_even, y_odd, *moves)
    return grad.transpose(0, 2, 1, 3), force.transpose(0, 2, 1, 3)


def solution(mesh):
    in_specs = (
        P("gx", "gy", None, None),
        P("gx", "gy", None),
        P("gx", "gy", None),
        P("gx", "gy", None),
        P("gx", "gy", None, None),
    )
    out_specs = (P("gx", "gy", None, None), P("gx", "gy", None, None))
    return jax.shard_map(local, mesh=mesh, in_specs=in_specs, out_specs=out_specs, check_vma=False)
```

```python
import functools

import jax
import jax.numpy as jnp
from jax import lax
from jax.experimental import pallas as pl
from jax.experimental.pallas import tpu as pltpu
from jax.sharding import PartitionSpec as P

LANES = 128
ROWS = 8
SIDE = 4
REACH = 3
REACH_SQ = 9
RING = 2
FIELDS = 6
FAR = 5
VOL, HEALTH, DAMAGE = 3, 4, 5
LAME = 24.0
SHEAR = 16.0
KINDS = ((1, 0), (0, 1), (1, 1), (1, -1))
SITES = 2 * SIDE
PATCH_X = SIDE + 2 * REACH
PATCH_Y = 2 + 2 * REACH
ENTRIES = PATCH_X * PATCH_Y
QUARTERS = PATCH_Y * PATCH_Y
COLUMN_ORDER = (0, 2, 1, 3)
CHUNK = 2


def iota(shape, dim):
    return lax.broadcasted_iota(jnp.int32, shape, dim)


def divide(value, step, top):
    total = jnp.zeros_like(value)
    for k in range(1, top):
        total = total + jnp.where(value >= step * k, 1, 0)
    return total


def lanes_of(value, index):
    return jnp.take_along_axis(value, index, axis=1, mode="promise_in_bounds")


def pieces(value):
    high = value.astype(jnp.bfloat16)
    low = (value - high.astype(jnp.float32)).astype(jnp.bfloat16)
    return jnp.concatenate([high, low], axis=0)


def moved(halves, moves):
    both = jnp.dot(halves, moves, preferred_element_type=jnp.float32)
    rows = halves.shape[0] // 2
    return both[0:rows] + both[rows:]


def partner(index, count, odd):
    other = ((index + 1) ^ 1) - 1 if odd else index ^ 1
    return other if 0 <= other < count else None


def swap(array, axis, odd):
    nx, ny = lax.axis_size("gx"), lax.axis_size("gy")
    to, left = {}, []
    for i in range(nx):
        for j in range(ny):
            if axis == "gx":
                other = (partner(i, nx, odd), j)
            else:
                other = (i, partner(j, ny, odd))
            if None in other:
                left.append((i, j))
            else:
                to[i, j] = other
    while left:
        one = left.pop(0)
        if not left:
            to[one] = one
            break
        other = min(left, key=lambda at: (axis == "gy" and at != (one[0] ^ 2, one[1]), abs(at[0] - one[0]) + abs(at[1] - one[1]), -at[0] - at[1]))
        left.remove(other)
        to[one], to[other] = other, one
    pairs = [(i * ny + j, k * ny + l) for (i, j), (k, l) in to.items()]
    return lax.ppermute(array, ("gx", "gy"), pairs)


def entry_list(wide, high):
    return [
        (x_at, y_at)
        for x_at in range(-REACH, wide + REACH)
        for y_at in range(-REACH, high + REACH)
        if any(
            (x_at - i) ** 2 + (y_at - j) ** 2 <= REACH_SQ for i in range(wide) for j in range(high)
        )
    ]


ENTRY_LIST = entry_list(SIDE, 2)
QUARTER_LIST = entry_list(2, 2)


SIDE_MOVES = [(0, -3)] + [(sx, y_at) for sx in (0, -1, 1) for y_at in (-2, 0, 2)] + [(0, 4)]
QUARTER_MOVES = [(x_at, half) for x_at in (-2, 0, 2) for half in (-1, 0, 1)]
QUARTER_MOVES += [(0, -2), (0, 2), (-3, 0), (4, 0)]


def lane_places(nx, ny):
    lane = iota((ROWS, LANES), 1)
    wide = 2 * (ny + 2)
    at_x = divide(lane, wide, nx + 4)
    at_half = lane - wide * at_x
    return lane, wide, at_x, lax.shift_right_logical(at_half, 1), (at_half & 1) == 1


def output_places(nx, ny):
    lane = iota((ROWS, LANES), 1)
    blocks = nx * ny
    slot = divide(lane, blocks, LANES // blocks + 1)
    block = lane - blocks * slot
    block_x = divide(block, ny, nx)
    return slot, block_x, block - ny * block_x


def moves_kernel(nx, ny, after, side_moves, quarter_moves, grad_moves, force_moves):
    lane, wide, at_x, at_y, upper = lane_places(nx, ny)
    ext_x, ext_y = nx + 2 * RING, ny + 2 * RING
    low_x_at, low_y_at = nx * ny, nx * ny + 2 * RING * ny
    rows = iota((2 * ROWS, LANES), 0)

    def block_row(e, f):
        own = (e - RING) * ny + f - RING
        column = jnp.where(e < RING, e, RING + ext_x - 1 - e)
        beside = low_x_at + column * ny + f - RING
        line = jnp.where(f < RING, f, RING + ext_y - 1 - f)
        above = low_y_at + line * ext_x + e
        row = jnp.where((e < RING) | (e >= RING + nx), beside, own)
        return jnp.where((f < RING) | (f >= RING + ny), above, row)

    def fill(target, column, source):
        source = jnp.concatenate([source, source], axis=0)
        for row in range(0, target.shape[0], 2 * ROWS):
            hit = jnp.where(source == rows + row, 1.0, 0.0).astype(jnp.bfloat16)
            target[row : row + 2 * ROWS, column * LANES : (column + 1) * LANES] = hit

    for column, (sx, y_at) in enumerate(SIDE_MOVES):
        sources = []
        for at in (y_at, y_at + 2):
            part = (at % SIDE - y_at % 2) // 2
            sources.append(part * LANES + block_row(at_x + 1 + sx, at_y + 1 + at // SIDE))
        source = jnp.where(upper, sources[1], sources[0])
        fill(side_moves, column, jnp.where(at_x < nx + 2, source, -1))

    quarter_x = divide(lane, 2 * ny, 2 * nx)
    quarter_y = lane - 2 * ny * quarter_x
    right = (quarter_x & 1) == 1
    owner = (lax.shift_right_logical(quarter_x, 1) + 1) * wide + quarter_y + 2
    for column, (x_at, half) in enumerate(QUARTER_MOVES):
        sources = []
        for at in (x_at, x_at + 2):
            part = (at % SIDE - x_at % 2) // 2
            sources.append(part * LANES + owner + (wide * (at // SIDE) + half))
        fill(quarter_moves, column, jnp.where(right, sources[1], sources[0]))

    slot, block_x, block_y = output_places(nx, ny)
    for jh in range(2):
        fill(grad_moves, jh, slot * LANES + (block_x + 1) * wide + 2 * (block_y + 1) + jh)
    for ih in range(2):
        for jh in range(2):
            source = slot * LANES + (2 * block_x + ih) * 2 * ny + 2 * block_y + jh
            fill(force_moves, 2 * ih + jh, jnp.where(slot < 3, source, -1))


def entry_index(x_at, y_at):
    return (x_at + REACH) * PATCH_Y + y_at + REACH


def own_rows(own, nx, ny, field, x, start, count):
    return own[pl.ds((field * nx + x) * ny + start, count), :]


def pack_kernel(nx, ny, disp, vol, health, damage, pairs, own, to_even, to_odd, here, sems):
    copies = []
    for k, (source, target) in enumerate(zip((disp, vol, health, damage, pairs), here)):
        copies.append(pltpu.make_async_copy(source, target, sems.at[k]))
    for k in (4, 0, 1, 2, 3):
        copies[k].start()
    disp, vol, health, damage, pairs = here
    odd_here = lax.rem(lax.axis_index("gx"), 2)
    ext_x = nx + 2 * RING
    slots = pairs.shape[1]
    copies[4].wait()
    ax, ay = pairs[0:1, :], pairs[1:2, :]
    bx, by = pairs[2:3, :], pairs[3:4, :]
    kind = jnp.where(bx == ax, 1, jnp.where(by == ay, 0, jnp.where(by > ay, 2, 3)))
    code = jnp.where(ax >= 0, kind * ext_x + ax + 1, -1)
    hit_x = jnp.where(code == iota((LANES, slots), 0), 1.0, 0.0).astype(jnp.bfloat16)
    hit_y = jnp.where(ay + 1 == iota((2 * ROWS, slots), 0), 1.0, 0.0).astype(jnp.bfloat16)
    table = lax.dot_general(
        hit_y, hit_x, (((1,), (1,)), ((), ())), preferred_element_type=jnp.float32
    )[0:ROWS]
    for copy in copies[:4]:
        copy.wait()
    for x in range(nx):
        for field in range(FIELDS):
            if field < 3:
                value = disp[x, field, :, :]
            elif field == VOL:
                value = vol[x, :, :]
            elif field == HEALTH:
                value = health[x, :, :]
            else:
                value = damage[x, :, :].astype(jnp.float32)
            row = (field * nx + x) * ny
            own[row : row + ny, :] = value
    for target, high in ((to_even, 1 - odd_here), (to_odd, odd_here)):
        target[0:ROWS, :] = table
        for field in range(FIELDS):
            row = ROWS + field * ny
            target[row : row + ny, :] = own_rows(own, nx, ny, field, high * (nx - 1), 0, ny)
        outer = 1 + high * (nx - 3)
        halves = [
            jnp.concatenate(
                [own_rows(own, nx, ny, field, outer, y, ny // 2) for field in range(FAR)], axis=0
            )
            for y in (0, ny // 2)
        ]
        target[ROWS + FIELDS * ny :, :] = folded(*halves, SIDE // 2, high)


def folded(first, second, step, high):
    keep = (iota(first.shape, 1) & step) != 0
    of_high = jnp.where(keep, first, pltpu.roll(second, LANES - step, 1))
    of_low = jnp.where(keep, pltpu.roll(second, step, 1), first)
    return jnp.where(high == 1, of_high, of_low)


def unfolded(rows, step, low):
    return rows, pltpu.roll(rows, step if low else LANES - step, 1)


def sides(from_even, from_odd, axis):
    here = lax.axis_index(axis)
    odd_here = lax.rem(here, 2) == 1
    low = jnp.where(odd_here, from_even, from_odd)
    high = jnp.where(odd_here, from_odd, from_even)
    low = jnp.where(here == 0, 0.0, low)
    return low, jnp.where(here == lax.axis_size(axis) - 1, 0.0, high)


def joined(table, low, high, count, axis, at, size):
    table = table + jnp.where(at >= count, pltpu.roll(high, count, axis), 0.0)
    return table + jnp.where(at < 2 * RING, pltpu.roll(low, size - count, axis), 0.0)


def middle_kernel(nx, ny, own, x_mine, x_even, x_odd, to_even, to_odd, beside, far):
    odd_y = lax.rem(lax.axis_index("gy"), 2)
    ext_x = nx + 2 * RING
    half = ny // 2
    lane = iota((ROWS, LANES), 1)
    at_e = lane - ext_x * divide(lane, ext_x, LANES // ext_x + 1)
    received = sides(x_even[...], x_odd[...], "gx")
    table = joined(x_mine[0:ROWS, :], received[0][0:ROWS], received[1][0:ROWS], nx, 1, at_e, LANES)
    for side, rows in enumerate(received):
        outer = unfolded(rows[ROWS + FIELDS * ny :], SIDE // 2, side == 0)
        for field in range(FIELDS):
            row = (field * 2 + side) * 2 * ny
            for part in range(2):
                if field < FAR:
                    value = outer[part][field * half : (field + 1) * half]
                else:
                    value = jnp.zeros((half, LANES), jnp.float32)
                beside[row + part * half : row + (part + 1) * half, :] = value
            beside[row + ny : row + 2 * ny, :] = rows[ROWS + field * ny : ROWS + (field + 1) * ny]

    def line(target, row, field, y):
        base = field * 4 * ny
        for e, column in ((0, 0), (1, 1), (nx + 2, 3), (nx + 3, 2)):
            target[row + e : row + e + 1, :] = beside[pl.ds(base + column * ny + y, 1), :]
        target[row + RING : row + RING + nx, :] = own[pl.ds(field * nx * ny + y, nx, stride=ny), :]

    for target, high in ((to_even, 1 - odd_y), (to_odd, odd_y)):
        target[0:ROWS, :] = table
        for field in range(FIELDS):
            line(target, ROWS + field * ext_x, field, high * (ny - 1))
        for field in range(FAR):
            line(far, field * ext_x, field, 1 + high * (ny - 3))
        halves = [
            jnp.concatenate(
                [
                    far[field * ext_x + e : field * ext_x + e + ext_x // 2, :]
                    for field in range(FAR)
                ],
                axis=0,
            )
            for e in (0, ext_x // 2)
        ]
        target[ROWS + FIELDS * ext_x :, :] = folded(*halves, SIDE * SIDE // 2, high)


def bond_steps(dz):
    left = REACH_SQ - dz * dz
    for dx in range(-REACH, REACH + 1):
        steps = [
            dy
            for dy in range(-REACH, REACH + 1)
            if dx * dx + dy * dy <= left and (dx, dy, dz) != (0, 0, 0)
        ]
        if steps:
            yield dx, steps


def plus(total, term):
    return term if total is None else total + term


def weighted_sum(values):
    total = None
    for k, value in sorted(values.items()):
        total = plus(total, value if k == 1 else value * float(k))
    return total


def add_scaled(total, value, factor):
    if factor == 0:
        return total
    if abs(factor) != 1:
        value = value * float(abs(factor))
    if total is None:
        return value if factor > 0 else -value
    return total + value if factor > 0 else total - value


def lattice_sums(terms, second):
    row, slope, odd, even = {}, {}, {}, {}
    for dx in sorted({dx for dx, _ in terms}, key=abs):
        steps = {dy: terms[dx, dy] for x, dy in terms if x == dx}
        differences = {}
        for dy in sorted({abs(dy) for dy in steps}):
            if dy:
                summed = steps[dy] + steps[-dy]
                differences[dy] = steps[dy] - steps[-dy]
                even[dy] = plus(even.get(dy), summed)
                if not second:
                    odd[dy] = plus(odd.get(dy), differences[dy])
            else:
                summed = steps[0]
            row[dx] = plus(row.get(dx), summed)
        if second and differences:
            slope[dx] = weighted_sum(differences)
    rises = {dx: row[dx] - row[-dx] for dx in row if dx > 0}
    pairs = {dx: row[dx] + row[-dx] for dx in row if dx > 0}
    one = row.get(0)
    for value in pairs.values():
        one = plus(one, value)
    sums = {"1": one, "x": weighted_sum(rises)}
    if not second:
        sums["y"] = weighted_sum(odd)
        return sums
    sums["y"] = None
    for value in slope.values():
        sums["y"] = plus(sums["y"], value)
    sums["xx"] = weighted_sum({dx * dx: value for dx, value in pairs.items()})
    sums["yy"] = weighted_sum({dy * dy: value for dy, value in even.items()})
    sums["xy"] = weighted_sum({dx: slope[dx] - slope[-dx] for dx in slope if dx > 0})
    return sums


def product(left, right):
    return [
        sum(left[3 * a + k] * right[3 * k + b] for k in range(1, 3)) + left[3 * a] * right[b]
        for a in range(3)
        for b in range(3)
    ]


def material(shape, moment, alive):
    e = shape
    cof_00 = e[4] * e[8] - e[5] * e[7]
    cof_01 = e[5] * e[6] - e[3] * e[8]
    cof_02 = e[3] * e[7] - e[4] * e[6]
    cof_11 = e[0] * e[8] - e[2] * e[6]
    cof_12 = e[1] * e[6] - e[0] * e[7]
    cof_22 = e[0] * e[4] - e[1] * e[3]
    scale = 1.0 / (e[0] * cof_00 + e[1] * cof_01 + e[2] * cof_02)
    i00, i01, i02 = cof_00 * scale, cof_01 * scale, cof_02 * scale
    i11, i12, i22 = cof_11 * scale, cof_12 * scale, cof_22 * scale
    inverse = [i00, i01, i02, i01, i11, i12, i02, i12, i22]
    grad = product(moment, inverse)
    strain = {}
    for a in range(3):
        for b in range(a, 3):
            value = grad[a] * grad[b] + grad[3 + a] * grad[3 + b] + grad[6 + a] * grad[6 + b]
            strain[a, b] = value - 1.0 if a == b else value
    trace = strain[0, 0] + strain[1, 1] + strain[2, 2]
    second = [None] * 9
    for (a, b), value in strain.items():
        entry = value * SHEAR
        if a == b:
            entry = entry + trace * (0.5 * LAME)
        second[3 * a + b] = second[3 * b + a] = entry
    i00, i01, i02, i11, i12, i22 = [value * alive for value in (i00, i01, i02, i11, i12, i22)]
    inverse = [i00, i01, i02, i01, i11, i12, i02, i12, i22]
    return grad, product(product(grad, second), inverse)


def main_kernel(
    nx, ny, own, beside, y_mine, y_even, y_odd, side_moves, quarter_moves, grad_moves,
    force_moves, out_grad, out_force, ext, turned, weighted, patch, tall, site, stress, spread,
    spread_health, tall_quarter, start_force, result, gathered, rows_out, hold_grad, hold_force, sems
):
    ext_x, ext_y = nx + 2 * RING, ny + 2 * RING
    tile = (ROWS, LANES)
    at_row = iota(tile, 0)
    lane, wide, at_x, at_y, upper = lane_places(nx, ny)

    low_x_at, low_y_at = nx * ny, nx * ny + 2 * RING * ny
    side_x = 2 * RING * ny
    received = sides(y_even[...], y_odd[...], "gy")
    far = [
        unfolded(rows[ROWS + FIELDS * ext_x :], SIDE * SIDE // 2, side == 0)
        for side, rows in enumerate(received)
    ]
    half = ext_x // 2
    for field in range(FIELDS):
        base = field * LANES
        ext[base : base + nx * ny, :] = own_rows(own, nx, ny, field, 0, 0, nx * ny)
        at = base + low_x_at
        ext[at : at + side_x, :] = beside[field * side_x : (field + 1) * side_x, :]
        at = base + low_y_at
        for side in range(2):
            for part in range(2):
                if field < FAR:
                    value = far[side][part][field * half : (field + 1) * half]
                else:
                    value = jnp.zeros((half, LANES), jnp.float32)
                ext[at : at + half, :] = value
                at += half
            near = ROWS + field * ext_x
            ext[at : at + ext_x, :] = received[side][near : near + ext_x]
            at += ext_x
        if at < base + LANES:
            ext[at : base + LANES, :] = jnp.zeros((base + LANES - at, LANES), jnp.float32)

    for field in range(FIELDS):
        turned[field * LANES : (field + 1) * LANES, :] = ext[
            field * LANES : (field + 1) * LANES, :
        ].T
    for comp in range(3):
        weighted[comp * LANES : (comp + 1) * LANES, :] = (
            turned[comp * LANES : (comp + 1) * LANES, :]
            * turned[VOL * LANES : (VOL + 1) * LANES, :]
        )

    table = joined(
        y_mine[0:ROWS, :], received[0][0:ROWS], received[1][0:ROWS], ny, 0, at_row, ROWS
    )
    link = {}
    for kind, step in enumerate(KINDS):
        for sign in (1, -1):
            move = (0, 0) if sign == 1 else (-step[0], -step[1])
            picked = lanes_of(table, kind * ext_x + at_x + 1 + move[0])
            picked = jnp.where(at_row == at_y + 1 + move[1], picked, 0.0)
            link[sign * step[0], sign * step[1]] = jnp.broadcast_to(
                jnp.sum(picked, axis=0, keepdims=True), tile
            )

    masks = {}

    def mask_of(sx, sy0, sy1):
        if (sx, sy0, sy1) not in masks:
            one = jnp.ones(tile, jnp.float32)
            masks[sx, sy0, sy1] = jnp.where(
                upper, link.get((sx, sy1), one), link.get((sx, sy0), one)
            )
        return masks[sx, sy0, sy1]

    def points(source, field, i, odd):
        start = field * LANES + SIDE * odd + i
        near = source[pl.ds(start, ROWS, stride=SIDE * SIDE), :]
        far = source[pl.ds(start + 2 * SIDE, ROWS, stride=SIDE * SIDE), :]
        return jnp.concatenate([near, far], axis=1)

    def columns(moves, first, count):
        return moves[:, first * LANES : (first + count) * LANES]

    moving = ((turned, HEALTH), (turned, VOL), (weighted, 0), (weighted, 1), (weighted, 2))
    parts = pieces(
        jnp.concatenate(
            [
                points(source, field, i, odd)
                for odd in range(2)
                for i in range(SIDE)
                for source, field in moving
            ],
            axis=0,
        )
    )

    def keep(values, step, sx, y_even):
        row = 0
        for odd in range(2):
            y_at = y_even + odd
            for i in range(SIDE):
                x_at = i + SIDE * sx
                for field in range(len(moving)):
                    if (x_at, y_at) in ENTRY_LIST:
                        value = values[row : row + ROWS, step * LANES : (step + 1) * LANES]
                        links = (sx, y_at // SIDE, (y_at + 2) // SIDE)
                        if field == 0 and links != (0, 0, 0):
                            value = value * mask_of(*links)
                        patch[field * ENTRIES + entry_index(x_at, y_at)] = value
                    row += ROWS

    for first in range(0, len(SIDE_MOVES), CHUNK):
        chosen = SIDE_MOVES[first : first + CHUNK]
        values = moved(parts, columns(side_moves, first, len(chosen)))
        for step, (sx, y_at) in enumerate(chosen):
            keep(values, step, sx, y_at - y_at % 2)

    fixed = [0, 1, 2, DAMAGE]
    values = moved(
        pieces(
            jnp.concatenate(
                [points(turned, f, i, odd) for odd in range(2) for i in range(SIDE) for f in fixed],
                axis=0,
            )
        ),
        columns(side_moves, SIDE_MOVES.index((0, 0)), 1),
    )
    for i in range(SIDE):
        for j in range(2):
            at = 2 * i + j
            tall[24 * at : 24 * at + 8, :] = jnp.zeros(tile, jnp.float32)
            tall[24 * at + 8 : 24 * at + 16, :] = patch[entry_index(i, j)]
            tall[24 * at + 16 : 24 * at + 24, :] = jnp.zeros(tile, jnp.float32)
            for k in range(4):
                row = ((j * SIDE + i) * 4 + k) * ROWS
                value = values[row : row + ROWS]
                site[k * SITES + at] = value if k < 3 else 1.0 - value

    def shape_site(i, j):
        at = 2 * i + j
        base = i * PATCH_Y + j
        shape = {}
        moment = {}
        first = {}
        def gain(store, key, value, factor=1):
            if value is not None:
                store[key] = add_scaled(store.get(key), value, factor)

        for depths in ((0,), (1,), (-1,), (2,), (-2,), (3,), (-3,)):
            here = {dz: tall[24 * at + 8 - dz : 24 * at + 16 - dz, :] for dz in depths}
            terms = {dz: [{} for _ in range(4)] for dz in depths}
            for dx, steps in bond_steps(depths[0]):
                for dy in steps:
                    k = base + (dx + REACH) * PATCH_Y + dy + REACH
                    limit = patch[k]
                    amounts = [patch[(1 + c) * ENTRIES + k] for c in range(4)]
                    for dz in depths:
                        strength = jnp.minimum(here[dz], limit)
                        for c in range(4):
                            terms[dz][c][dx, dy] = strength * amounts[c]
            acc = {dz: lattice_sums(terms[dz][0], True) for dz in depths}
            acc_u = {dz: [lattice_sums(terms[dz][1 + c], False) for c in range(3)] for dz in depths}

            for dz in depths:

                def back(value):
                    if value is None or dz == 0:
                        return value
                    return pltpu.roll(value, (-dz) % ROWS, 0)

                moved = {key: back(value) for key, value in acc[dz].items()}
                for key in ("xx", "xy", "yy"):
                    gain(shape, key, moved.get(key))
                gain(shape, "xz", moved.get("x"), dz)
                gain(shape, "yz", moved.get("y"), dz)
                gain(shape, "zz", moved.get("1"), dz * dz)
                gain(first, "x", moved.get("x"))
                gain(first, "y", moved.get("y"))
                gain(first, "z", moved.get("1"), dz)
                for comp in range(3):
                    moved_u = {key: back(value) for key, value in acc_u[dz][comp].items()}
                    gain(moment, (comp, 0), moved_u.get("x"))
                    gain(moment, (comp, 1), moved_u.get("y"))
                    gain(moment, (comp, 2), moved_u.get("1"), dz)
        kxx, kxy, kyy = shape["xx"], shape["xy"], shape["yy"]
        kxz, kyz, kzz = shape["xz"], shape["yz"], shape["zz"]
        plain = [kxx, kxy, kxz, kxy, kyy, kyz, kxz, kyz, kzz]
        arm = [first["x"], first["y"], first["z"]]
        moments = []
        for a in range(3):
            here_u = site[a * SITES + at]
            for b in range(3):
                moments.append(moment[a, b] + plain[3 * a + b] - here_u * arm[b])
        full = [value + 1.0 if k in (0, 4, 8) else value for k, value in enumerate(plain)]
        grad, carried = material(full, moments, site[3 * SITES + at])
        here_vol = patch[ENTRIES + base + REACH * PATCH_Y + REACH]
        for k in range(9):
            result[k * SITES + at] = grad[k]
            stress[k * SITES + at] = carried[k] * here_vol
        for a in range(3):
            result[(9 + a) * SITES + at] = (
                carried[3 * a] * arm[0] + carried[3 * a + 1] * arm[1] + carried[3 * a + 2] * arm[2]
            )

    def quarter_at(x_at, y_at):
        return (x_at + REACH) * PATCH_Y + y_at + REACH

    def site_pairs(source, first, odd, j, count):
        return [
            jnp.concatenate(
                [source[first + k * SITES + 2 * i + j] for i in (odd, odd + 2)], axis=1
            )
            for k in range(count)
        ]

    def quarter_entries(odd):
        parts = [part for j in range(2) for part in site_pairs(stress, 0, odd, j, 9)]
        parts = pieces(jnp.concatenate(parts, axis=0))
        for first in range(0, len(QUARTER_MOVES), CHUNK):
            chosen = QUARTER_MOVES[first : first + CHUNK]
            values = moved(parts, columns(quarter_moves, first, len(chosen)))
            for step, (x_even, half) in enumerate(chosen):
                row = 0
                x_at = x_even - x_even % 2 + odd
                for j in range(2):
                    y_at = 2 * half + j
                    for k in range(9):
                        if (x_at, y_at) in QUARTER_LIST:
                            value = values[row : row + ROWS, step * LANES : (step + 1) * LANES]
                            spread[k * QUARTERS + quarter_at(x_at, y_at)] = value
                        row += ROWS

    own_moves = columns(quarter_moves, QUARTER_MOVES.index((0, 0)), 1)

    def quarter_health():
        values = moved(
            pieces(jnp.concatenate(
                [
                    jnp.concatenate(
                        [patch[entry_index(x_at, y_at)], patch[entry_index(x_at + 2, y_at)]], axis=1
                    )
                    for x_at, y_at in QUARTER_LIST
                ],
                axis=0,
            )),
            own_moves,
        )
        for k, (x_at, y_at) in enumerate(QUARTER_LIST):
            value = values[k * ROWS : (k + 1) * ROWS]
            spread_health[quarter_at(x_at, y_at)] = value
            if 0 <= x_at < 2 and 0 <= y_at < 2:
                row = 24 * (2 * x_at + y_at)
                tall_quarter[row : row + 8, :] = jnp.zeros(tile, jnp.float32)
                tall_quarter[row + 8 : row + 16, :] = value
                tall_quarter[row + 16 : row + 24, :] = jnp.zeros(tile, jnp.float32)

    blocks = nx * ny
    per_group = LANES // blocks

    def gather_grad(group, comps):
        sites = [
            jnp.concatenate([result[comp * SITES + at] for comp in comps], axis=1)
            for at in range(SITES)
        ]
        values = moved(pieces(jnp.concatenate(sites, axis=0)), grad_moves[0 : len(comps) * LANES, :])
        for at in range(SITES):
            for jh in range(2):
                start = group * LANES + (2 * jh + at % 2) * SIDE + at // 2
                gathered[pl.ds(start, ROWS, stride=SIDE * SIDE), :] = values[
                    at * ROWS : (at + 1) * ROWS, jh * LANES : (jh + 1) * LANES
                ]

    def group_out(group, comps, target, first):
        rows_out[group * LANES : (group + 1) * LANES, :] = gathered[
            group * LANES : (group + 1) * LANES, :
        ].T
        for part, comp in enumerate(comps):
            for x in range(nx):
                row = group * LANES + part * blocks + x * ny
                target[x, comp - first, :, :] = rows_out[row : row + ny, :]

    grad_groups = [list(range(9))[k : k + per_group] for k in range(0, 9, per_group)]

    for i in COLUMN_ORDER:
        for j in range(2):
            shape_site(i, j)
    quarter_health()
    quarter_entries(0)
    quarter_entries(1)

    parts = [
        part for i in range(2) for j in range(2) for part in site_pairs(result, 9 * SITES, i, j, 3)
    ]
    values = moved(pieces(jnp.concatenate(parts, axis=0)), own_moves)
    for k in range(12):
        start_force[k] = values[k * ROWS : (k + 1) * ROWS]

    def force_site(i, j):
        at = 2 * i + j
        base = (i + REACH) * PATCH_Y + j + REACH
        here = {
            dz: tall_quarter[24 * at + 8 - dz : 24 * at + 16 - dz, :]
            for dz in range(-REACH, REACH + 1)
        }
        acc = {}
        for dx in range(-REACH, REACH + 1):
            for dy in range(-REACH, REACH + 1):
                if dx * dx + dy * dy > REACH_SQ:
                    continue
                k = base + dx * PATCH_Y + dy
                deep = [
                    dz
                    for dz in range(-REACH, REACH + 1)
                    if dx * dx + dy * dy + dz * dz <= REACH_SQ and (dx, dy, dz) != (0, 0, 0)
                ]
                strength = {dz: jnp.minimum(here[dz], spread_health[k]) for dz in deep}
                for a in range(3):
                    flat = None
                    if dx:
                        flat = add_scaled(flat, spread[3 * a * QUARTERS + k], dx)
                    if dy:
                        flat = add_scaled(flat, spread[(3 * a + 1) * QUARTERS + k], dy)
                    upright = spread[(3 * a + 2) * QUARTERS + k]
                    lifts = {
                        dz: upright if dz == 1 else upright * float(dz) for dz in deep if dz > 0
                    }
                    for dz in deep:
                        if dz > 0:
                            value = lifts[dz] if flat is None else flat + lifts[dz]
                        elif dz < 0:
                            value = -lifts[-dz] if flat is None else flat - lifts[-dz]
                        else:
                            value = flat
                        acc[a, dz] = plus(acc.get((a, dz)), strength[dz] * value)
        for a in range(3):
            total = start_force[3 * at + a]
            for dz in range(-REACH, REACH + 1):
                value = acc[a, dz]
                total = total + (pltpu.roll(value, (-dz) % ROWS, 0) if dz else value)
            start_force[3 * at + a] = total

    force_site(0, 0)
    for group, comps in enumerate(grad_groups):
        gather_grad(group, comps)
        group_out(group, comps, hold_grad, 0)
    grad_copy = pltpu.make_async_copy(hold_grad, out_grad, sems.at[0])
    grad_copy.start()
    force_site(0, 1)
    force_site(1, 0)
    force_site(1, 1)
    group = len(grad_groups)
    sites = [
        jnp.concatenate([start_force[3 * at + a] for a in range(3)], axis=1) for at in range(4)
    ]
    values = moved(pieces(jnp.concatenate(sites, axis=0)), force_moves[...])
    for at in range(4):
        for ih in range(2):
            for jh in range(2):
                start = group * LANES + (2 * jh + at % 2) * SIDE + 2 * ih + at // 2
                column = (2 * ih + jh) * LANES
                gathered[pl.ds(start, ROWS, stride=SIDE * SIDE), :] = values[
                    at * ROWS : (at + 1) * ROWS, column : column + LANES
                ]
    group_out(group, [9, 10, 11], hold_force, 9)
    force_copy = pltpu.make_async_copy(hold_force, out_force, sems.at[1])
    force_copy.start()
    grad_copy.wait()
    force_copy.wait()


def local(displacement, volume, health, damage, block_pairs):
    nx, ny, points = volume.shape
    ext_x = nx + 2 * RING
    f32 = jnp.float32
    pairs = block_pairs.reshape(block_pairs.shape[2:]).T
    raw = (displacement.transpose(0, 2, 1, 3), volume, health, damage)
    params = pltpu.CompilerParams(vmem_limit_bytes=48 * 1024 * 1024)
    x_shape = jax.ShapeDtypeStruct((ROWS + FIELDS * ny + FAR * ny // 2, points), f32)
    own, x_to_even, x_to_odd = pl.pallas_call(
        functools.partial(pack_kernel, nx, ny),
        out_shape=(jax.ShapeDtypeStruct((FIELDS * nx * ny, points), f32), x_shape, x_shape),
        in_specs=[pl.BlockSpec(memory_space=pltpu.HBM)] * 5,
        scratch_shapes=[
            [pltpu.VMEM(a.shape, a.dtype) for a in (*raw, pairs)],
            pltpu.SemaphoreType.DMA((5,)),
        ],
        compiler_params=params,
        name="pack",
    )(*[pltpu.with_memory_space_constraint(a, pltpu.HBM) for a in (*raw, pairs)])
    x_odd = swap(x_to_odd, "gx", True)
    x_even = swap(x_to_even, "gx", False)
    move_shapes = [
        jax.ShapeDtypeStruct((height * LANES, width * LANES), jnp.bfloat16)
        for height, width in (
            (2, len(SIDE_MOVES)),
            (2, len(QUARTER_MOVES)),
            (LANES // (nx * ny), 2),
            (3, 4),
        )
    ]
    moves = pl.pallas_call(
        functools.partial(moves_kernel, nx, ny),
        out_shape=move_shapes,
        in_specs=[pl.BlockSpec(memory_space=pl.ANY)],
        compiler_params=params,
        name="moves",
    )(x_to_even)
    y_shape = jax.ShapeDtypeStruct((ROWS + FIELDS * ext_x + FAR * ext_x // 2, points), f32)
    y_to_even, y_to_odd, beside = pl.pallas_call(
        functools.partial(middle_kernel, nx, ny),
        out_shape=(y_shape, y_shape, jax.ShapeDtypeStruct((FIELDS * 2 * RING * ny, points), f32)),
        scratch_shapes=[pltpu.VMEM((FAR * ext_x, points), f32)],
        compiler_params=params,
        name="middle",
    )(own, x_to_even, x_even, x_odd)
    y_odd = swap(y_to_odd, "gy", True)
    y_even = swap(y_to_even, "gy", False)
    tiles = lambda count: pltpu.VMEM((count, ROWS, LANES), f32)
    rows = lambda count: pltpu.VMEM((count * LANES, LANES), f32)
    grad, force = pl.pallas_call(
        functools.partial(main_kernel, nx, ny),
        out_shape=(
            jax.ShapeDtypeStruct((nx, 9, ny, points), f32),
            jax.ShapeDtypeStruct((nx, 3, ny, points), f32),
        ),
        scratch_shapes=[
            rows(FIELDS),
            rows(FIELDS),
            rows(3),
            tiles(5 * ENTRIES),
            pltpu.VMEM((24 * SITES, LANES), f32),
            tiles(4 * SITES),
            tiles(9 * SITES),
            tiles(9 * QUARTERS),
            tiles(QUARTERS),
            pltpu.VMEM((24 * 4, LANES), f32),
            tiles(12),
            tiles(12 * SITES),
            rows(4),
            rows(4),
            pltpu.VMEM((nx, 9, ny, points), f32),
            pltpu.VMEM((nx, 3, ny, points), f32),
            pltpu.SemaphoreType.DMA((2,)),
        ],
        out_specs=(pl.BlockSpec(memory_space=pltpu.HBM),) * 2,
        compiler_params=params,
        name="main",
    )(own, beside, y_to_even, y_even, y_odd, *moves)
    return grad.transpose(0, 2, 1, 3), force.transpose(0, 2, 1, 3)


def solution(mesh):
    in_specs = (
        P("gx", "gy", None, None),
        P("gx", "gy", None),
        P("gx", "gy", None),
        P("gx", "gy", None),
        P("gx", "gy", None, None),
    )
    out_specs = (P("gx", "gy", None, None), P("gx", "gy", None, None))
    return jax.shard_map(local, mesh=mesh, in_specs=in_specs, out_specs=out_specs, check_vma=False)
```

```python
import functools

import jax
import jax.numpy as jnp
from jax import lax
from jax.experimental import pallas as pl
from jax.experimental.pallas import tpu as pltpu
from jax.sharding import PartitionSpec as P

LANES = 128
ROWS = 8
SIDE = 4
REACH = 3
REACH_SQ = 9
RING = 2
FIELDS = 6
FAR = 5
VOL, HEALTH, DAMAGE = 3, 4, 5
LAME = 24.0
SHEAR = 16.0
KINDS = ((1, 0), (0, 1), (1, 1), (1, -1))
SITES = 2 * SIDE
PATCH_X = SIDE + 2 * REACH
PATCH_Y = 2 + 2 * REACH
ENTRIES = PATCH_X * PATCH_Y
QUARTERS = PATCH_Y * PATCH_Y
COLUMN_ORDER = (0, 2, 1, 3)
CHUNK = 2


def iota(shape, dim):
    return lax.broadcasted_iota(jnp.int32, shape, dim)


def divide(value, step, top):
    total = jnp.zeros_like(value)
    for k in range(1, top):
        total = total + jnp.where(value >= step * k, 1, 0)
    return total


def lanes_of(value, index):
    return jnp.take_along_axis(value, index, axis=1, mode="promise_in_bounds")


def pieces(value):
    high = value.astype(jnp.bfloat16)
    low = (value - high.astype(jnp.float32)).astype(jnp.bfloat16)
    return jnp.concatenate([high, low], axis=0)


def moved(halves, moves):
    both = jnp.dot(halves, moves, preferred_element_type=jnp.float32)
    rows = halves.shape[0] // 2
    return both[0:rows] + both[rows:]


def partner(index, count, odd):
    other = ((index + 1) ^ 1) - 1 if odd else index ^ 1
    return other if 0 <= other < count else None


def swap(array, axis, odd):
    nx, ny = lax.axis_size("gx"), lax.axis_size("gy")
    to, left = {}, []
    for i in range(nx):
        for j in range(ny):
            if axis == "gx":
                other = (partner(i, nx, odd), j)
            else:
                other = (i, partner(j, ny, odd))
            if None in other:
                left.append((i, j))
            else:
                to[i, j] = other
    while left:
        one = left.pop(0)
        if not left:
            to[one] = one
            break
        other = min(left, key=lambda at: (axis == "gy" and at[0] != one[0], abs(at[0] - one[0]) + abs(at[1] - one[1]), -at[0] - at[1]))
        left.remove(other)
        to[one], to[other] = other, one
    pairs = [(i * ny + j, k * ny + l) for (i, j), (k, l) in to.items()]
    return lax.ppermute(array, ("gx", "gy"), pairs)


def entry_list(wide, high):
    return [
        (x_at, y_at)
        for x_at in range(-REACH, wide + REACH)
        for y_at in range(-REACH, high + REACH)
        if any(
            (x_at - i) ** 2 + (y_at - j) ** 2 <= REACH_SQ for i in range(wide) for j in range(high)
        )
    ]


ENTRY_LIST = entry_list(SIDE, 2)
QUARTER_LIST = entry_list(2, 2)


SIDE_MOVES = [(0, -3)] + [(sx, y_at) for sx in (0, -1, 1) for y_at in (-2, 0, 2)] + [(0, 4)]
QUARTER_MOVES = [(x_at, half) for x_at in (-2, 0, 2) for half in (-1, 0, 1)]
QUARTER_MOVES += [(0, -2), (0, 2), (-3, 0), (4, 0)]


def lane_places(nx, ny):
    lane = iota((ROWS, LANES), 1)
    wide = 2 * (ny + 2)
    at_x = divide(lane, wide, nx + 4)
    at_half = lane - wide * at_x
    return lane, wide, at_x, lax.shift_right_logical(at_half, 1), (at_half & 1) == 1


def output_places(nx, ny):
    lane = iota((ROWS, LANES), 1)
    blocks = nx * ny
    slot = divide(lane, blocks, LANES // blocks + 1)
    block = lane - blocks * slot
    block_x = divide(block, ny, nx)
    return slot, block_x, block - ny * block_x


def moves_kernel(nx, ny, after, side_moves, quarter_moves, grad_moves, force_moves):
    lane, wide, at_x, at_y, upper = lane_places(nx, ny)
    ext_x, ext_y = nx + 2 * RING, ny + 2 * RING
    low_x_at, low_y_at = nx * ny, nx * ny + 2 * RING * ny
    rows = iota((2 * ROWS, LANES), 0)

    def block_row(e, f):
        own = (e - RING) * ny + f - RING
        column = jnp.where(e < RING, e, RING + ext_x - 1 - e)
        beside = low_x_at + column * ny + f - RING
        line = jnp.where(f < RING, f, RING + ext_y - 1 - f)
        above = low_y_at + line * ext_x + e
        row = jnp.where((e < RING) | (e >= RING + nx), beside, own)
        return jnp.where((f < RING) | (f >= RING + ny), above, row)

    def fill(target, column, source):
        source = jnp.concatenate([source, source], axis=0)
        for row in range(0, target.shape[0], 2 * ROWS):
            hit = jnp.where(source == rows + row, 1.0, 0.0).astype(jnp.bfloat16)
            target[row : row + 2 * ROWS, column * LANES : (column + 1) * LANES] = hit

    for column, (sx, y_at) in enumerate(SIDE_MOVES):
        sources = []
        for at in (y_at, y_at + 2):
            part = (at % SIDE - y_at % 2) // 2
            sources.append(part * LANES + block_row(at_x + 1 + sx, at_y + 1 + at // SIDE))
        source = jnp.where(upper, sources[1], sources[0])
        fill(side_moves, column, jnp.where(at_x < nx + 2, source, -1))

    quarter_x = divide(lane, 2 * ny, 2 * nx)
    quarter_y = lane - 2 * ny * quarter_x
    right = (quarter_x & 1) == 1
    owner = (lax.shift_right_logical(quarter_x, 1) + 1) * wide + quarter_y + 2
    for column, (x_at, half) in enumerate(QUARTER_MOVES):
        sources = []
        for at in (x_at, x_at + 2):
            part = (at % SIDE - x_at % 2) // 2
            sources.append(part * LANES + owner + (wide * (at // SIDE) + half))
        fill(quarter_moves, column, jnp.where(right, sources[1], sources[0]))

    slot, block_x, block_y = output_places(nx, ny)
    for jh in range(2):
        fill(grad_moves, jh, slot * LANES + (block_x + 1) * wide + 2 * (block_y + 1) + jh)
    for ih in range(2):
        for jh in range(2):
            source = slot * LANES + (2 * block_x + ih) * 2 * ny + 2 * block_y + jh
            fill(force_moves, 2 * ih + jh, jnp.where(slot < 3, source, -1))


def entry_index(x_at, y_at):
    return (x_at + REACH) * PATCH_Y + y_at + REACH


def own_rows(own, nx, ny, field, x, start, count):
    return own[pl.ds((field * nx + x) * ny + start, count), :]


def pack_kernel(nx, ny, disp, vol, health, damage, pairs, own, to_even, to_odd, here, sems):
    copies = []
    for k, (source, target) in enumerate(zip((disp, vol, health, damage, pairs), here)):
        copies.append(pltpu.make_async_copy(source, target, sems.at[k]))
    for k in (4, 0, 1, 2, 3):
        copies[k].start()
    disp, vol, health, damage, pairs = here
    odd_here = lax.rem(lax.axis_index("gx"), 2)
    ext_x = nx + 2 * RING
    slots = pairs.shape[1]
    copies[4].wait()
    ax, ay = pairs[0:1, :], pairs[1:2, :]
    bx, by = pairs[2:3, :], pairs[3:4, :]
    kind = jnp.where(bx == ax, 1, jnp.where(by == ay, 0, jnp.where(by > ay, 2, 3)))
    code = jnp.where(ax >= 0, kind * ext_x + ax + 1, -1)
    hit_x = jnp.where(code == iota((LANES, slots), 0), 1.0, 0.0).astype(jnp.bfloat16)
    hit_y = jnp.where(ay + 1 == iota((2 * ROWS, slots), 0), 1.0, 0.0).astype(jnp.bfloat16)
    table = lax.dot_general(
        hit_y, hit_x, (((1,), (1,)), ((), ())), preferred_element_type=jnp.float32
    )[0:ROWS]
    for copy in copies[:4]:
        copy.wait()
    for x in range(nx):
        for field in range(FIELDS):
            if field < 3:
                value = disp[x, field, :, :]
            elif field == VOL:
                value = vol[x, :, :]
            elif field == HEALTH:
                value = health[x, :, :]
            else:
                value = damage[x, :, :].astype(jnp.float32)
            row = (field * nx + x) * ny
            own[row : row + ny, :] = value
    for target, high in ((to_even, 1 - odd_here), (to_odd, odd_here)):
        target[0:ROWS, :] = table
        for field in range(FIELDS):
            row = ROWS + field * ny
            target[row : row + ny, :] = own_rows(own, nx, ny, field, high * (nx - 1), 0, ny)
        outer = 1 + high * (nx - 3)
        halves = [
            jnp.concatenate(
                [own_rows(own, nx, ny, field, outer, y, ny // 2) for field in range(FAR)], axis=0
            )
            for y in (0, ny // 2)
        ]
        target[ROWS + FIELDS * ny :, :] = folded(*halves, SIDE // 2, high)


def folded(first, second, step, high):
    keep = (iota(first.shape, 1) & step) != 0
    of_high = jnp.where(keep, first, pltpu.roll(second, LANES - step, 1))
    of_low = jnp.where(keep, pltpu.roll(second, step, 1), first)
    return jnp.where(high == 1, of_high, of_low)


def unfolded(rows, step, low):
    return rows, pltpu.roll(rows, step if low else LANES - step, 1)


def sides(from_even, from_odd, axis):
    here = lax.axis_index(axis)
    odd_here = lax.rem(here, 2) == 1
    low = jnp.where(odd_here, from_even, from_odd)
    high = jnp.where(odd_here, from_odd, from_even)
    low = jnp.where(here == 0, 0.0, low)
    return low, jnp.where(here == lax.axis_size(axis) - 1, 0.0, high)


def joined(table, low, high, count, axis, at, size):
    table = table + jnp.where(at >= count, pltpu.roll(high, count, axis), 0.0)
    return table + jnp.where(at < 2 * RING, pltpu.roll(low, size - count, axis), 0.0)


def middle_kernel(nx, ny, own, x_mine, x_even, x_odd, to_even, to_odd, beside, far):
    odd_y = lax.rem(lax.axis_index("gy"), 2)
    ext_x = nx + 2 * RING
    half = ny // 2
    lane = iota((ROWS, LANES), 1)
    at_e = lane - ext_x * divide(lane, ext_x, LANES // ext_x + 1)
    received = sides(x_even[...], x_odd[...], "gx")
    table = joined(x_mine[0:ROWS, :], received[0][0:ROWS], received[1][0:ROWS], nx, 1, at_e, LANES)
    for side, rows in enumerate(received):
        outer = unfolded(rows[ROWS + FIELDS * ny :], SIDE // 2, side == 0)
        for field in range(FIELDS):
            row = (field * 2 + side) * 2 * ny
            for part in range(2):
                if field < FAR:
                    value = outer[part][field * half : (field + 1) * half]
                else:
                    value = jnp.zeros((half, LANES), jnp.float32)
                beside[row + part * half : row + (part + 1) * half, :] = value
            beside[row + ny : row + 2 * ny, :] = rows[ROWS + field * ny : ROWS + (field + 1) * ny]

    def line(target, row, field, y):
        base = field * 4 * ny
        for e, column in ((0, 0), (1, 1), (nx + 2, 3), (nx + 3, 2)):
            target[row + e : row + e + 1, :] = beside[pl.ds(base + column * ny + y, 1), :]
        target[row + RING : row + RING + nx, :] = own[pl.ds(field * nx * ny + y, nx, stride=ny), :]

    for target, high in ((to_even, 1 - odd_y), (to_odd, odd_y)):
        target[0:ROWS, :] = table
        for field in range(FIELDS):
            line(target, ROWS + field * ext_x, field, high * (ny - 1))
        for field in range(FAR):
            line(far, field * ext_x, field, 1 + high * (ny - 3))
        halves = [
            jnp.concatenate(
                [
                    far[field * ext_x + e : field * ext_x + e + ext_x // 2, :]
                    for field in range(FAR)
                ],
                axis=0,
            )
            for e in (0, ext_x // 2)
        ]
        target[ROWS + FIELDS * ext_x :, :] = folded(*halves, SIDE * SIDE // 2, high)


def bond_steps(dz):
    left = REACH_SQ - dz * dz
    for dx in range(-REACH, REACH + 1):
        steps = [
            dy
            for dy in range(-REACH, REACH + 1)
            if dx * dx + dy * dy <= left and (dx, dy, dz) != (0, 0, 0)
        ]
        if steps:
            yield dx, steps


def plus(total, term):
    return term if total is None else total + term


def weighted_sum(values):
    total = None
    for k, value in sorted(values.items()):
        total = plus(total, value if k == 1 else value * float(k))
    return total


def add_scaled(total, value, factor):
    if factor == 0:
        return total
    if abs(factor) != 1:
        value = value * float(abs(factor))
    if total is None:
        return value if factor > 0 else -value
    return total + value if factor > 0 else total - value


def lattice_sums(terms, second):
    row, slope, odd, even = {}, {}, {}, {}
    for dx in sorted({dx for dx, _ in terms}, key=abs):
        steps = {dy: terms[dx, dy] for x, dy in terms if x == dx}
        differences = {}
        for dy in sorted({abs(dy) for dy in steps}):
            if dy:
                summed = steps[dy] + steps[-dy]
                differences[dy] = steps[dy] - steps[-dy]
                even[dy] = plus(even.get(dy), summed)
                if not second:
                    odd[dy] = plus(odd.get(dy), differences[dy])
            else:
                summed = steps[0]
            row[dx] = plus(row.get(dx), summed)
        if second and differences:
            slope[dx] = weighted_sum(differences)
    rises = {dx: row[dx] - row[-dx] for dx in row if dx > 0}
    pairs = {dx: row[dx] + row[-dx] for dx in row if dx > 0}
    one = row.get(0)
    for value in pairs.values():
        one = plus(one, value)
    sums = {"1": one, "x": weighted_sum(rises)}
    if not second:
        sums["y"] = weighted_sum(odd)
        return sums
    sums["y"] = None
    for value in slope.values():
        sums["y"] = plus(sums["y"], value)
    sums["xx"] = weighted_sum({dx * dx: value for dx, value in pairs.items()})
    sums["yy"] = weighted_sum({dy * dy: value for dy, value in even.items()})
    sums["xy"] = weighted_sum({dx: slope[dx] - slope[-dx] for dx in slope if dx > 0})
    return sums


def product(left, right):
    return [
        sum(left[3 * a + k] * right[3 * k + b] for k in range(1, 3)) + left[3 * a] * right[b]
        for a in range(3)
        for b in range(3)
    ]


def material(shape, moment, alive):
    e = shape
    cof_00 = e[4] * e[8] - e[5] * e[7]
    cof_01 = e[5] * e[6] - e[3] * e[8]
    cof_02 = e[3] * e[7] - e[4] * e[6]
    cof_11 = e[0] * e[8] - e[2] * e[6]
    cof_12 = e[1] * e[6] - e[0] * e[7]
    cof_22 = e[0] * e[4] - e[1] * e[3]
    scale = 1.0 / (e[0] * cof_00 + e[1] * cof_01 + e[2] * cof_02)
    i00, i01, i02 = cof_00 * scale, cof_01 * scale, cof_02 * scale
    i11, i12, i22 = cof_11 * scale, cof_12 * scale, cof_22 * scale
    inverse = [i00, i01, i02, i01, i11, i12, i02, i12, i22]
    grad = product(moment, inverse)
    strain = {}
    for a in range(3):
        for b in range(a, 3):
            value = grad[a] * grad[b] + grad[3 + a] * grad[3 + b] + grad[6 + a] * grad[6 + b]
            strain[a, b] = value - 1.0 if a == b else value
    trace = strain[0, 0] + strain[1, 1] + strain[2, 2]
    second = [None] * 9
    for (a, b), value in strain.items():
        entry = value * SHEAR
        if a == b:
            entry = entry + trace * (0.5 * LAME)
        second[3 * a + b] = second[3 * b + a] = entry
    i00, i01, i02, i11, i12, i22 = [value * alive for value in (i00, i01, i02, i11, i12, i22)]
    inverse = [i00, i01, i02, i01, i11, i12, i02, i12, i22]
    return grad, product(product(grad, second), inverse)


def main_kernel(
    nx, ny, own, beside, y_mine, y_even, y_odd, side_moves, quarter_moves, grad_moves,
    force_moves, out_grad, out_force, ext, turned, weighted, patch, tall, site, stress, spread,
    spread_health, tall_quarter, start_force, result, gathered, rows_out, hold_grad, hold_force, sems
):
    ext_x, ext_y = nx + 2 * RING, ny + 2 * RING
    tile = (ROWS, LANES)
    at_row = iota(tile, 0)
    lane, wide, at_x, at_y, upper = lane_places(nx, ny)

    low_x_at, low_y_at = nx * ny, nx * ny + 2 * RING * ny
    side_x = 2 * RING * ny
    received = sides(y_even[...], y_odd[...], "gy")
    far = [
        unfolded(rows[ROWS + FIELDS * ext_x :], SIDE * SIDE // 2, side == 0)
        for side, rows in enumerate(received)
    ]
    half = ext_x // 2
    for field in range(FIELDS):
        base = field * LANES
        ext[base : base + nx * ny, :] = own_rows(own, nx, ny, field, 0, 0, nx * ny)
        at = base + low_x_at
        ext[at : at + side_x, :] = beside[field * side_x : (field + 1) * side_x, :]
        at = base + low_y_at
        for side in range(2):
            for part in range(2):
                if field < FAR:
                    value = far[side][part][field * half : (field + 1) * half]
                else:
                    value = jnp.zeros((half, LANES), jnp.float32)
                ext[at : at + half, :] = value
                at += half
            near = ROWS + field * ext_x
            ext[at : at + ext_x, :] = received[side][near : near + ext_x]
            at += ext_x
        if at < base + LANES:
            ext[at : base + LANES, :] = jnp.zeros((base + LANES - at, LANES), jnp.float32)

    for field in range(FIELDS):
        turned[field * LANES : (field + 1) * LANES, :] = ext[
            field * LANES : (field + 1) * LANES, :
        ].T
    for comp in range(3):
        weighted[comp * LANES : (comp + 1) * LANES, :] = (
            turned[comp * LANES : (comp + 1) * LANES, :]
            * turned[VOL * LANES : (VOL + 1) * LANES, :]
        )

    table = joined(
        y_mine[0:ROWS, :], received[0][0:ROWS], received[1][0:ROWS], ny, 0, at_row, ROWS
    )
    link = {}
    for kind, step in enumerate(KINDS):
        for sign in (1, -1):
            move = (0, 0) if sign == 1 else (-step[0], -step[1])
            picked = lanes_of(table, kind * ext_x + at_x + 1 + move[0])
            picked = jnp.where(at_row == at_y + 1 + move[1], picked, 0.0)
            link[sign * step[0], sign * step[1]] = jnp.broadcast_to(
                jnp.sum(picked, axis=0, keepdims=True), tile
            )

    masks = {}

    def mask_of(sx, sy0, sy1):
        if (sx, sy0, sy1) not in masks:
            one = jnp.ones(tile, jnp.float32)
            masks[sx, sy0, sy1] = jnp.where(
                upper, link.get((sx, sy1), one), link.get((sx, sy0), one)
            )
        return masks[sx, sy0, sy1]

    def points(source, field, i, odd):
        start = field * LANES + SIDE * odd + i
        near = source[pl.ds(start, ROWS, stride=SIDE * SIDE), :]
        far = source[pl.ds(start + 2 * SIDE, ROWS, stride=SIDE * SIDE), :]
        return jnp.concatenate([near, far], axis=1)

    def columns(moves, first, count):
        return moves[:, first * LANES : (first + count) * LANES]

    moving = ((turned, HEALTH), (turned, VOL), (weighted, 0), (weighted, 1), (weighted, 2))
    parts = pieces(
        jnp.concatenate(
            [
                points(source, field, i, odd)
                for odd in range(2)
                for i in range(SIDE)
                for source, field in moving
            ],
            axis=0,
        )
    )

    def keep(values, step, sx, y_even):
        row = 0
        for odd in range(2):
            y_at = y_even + odd
            for i in range(SIDE):
                x_at = i + SIDE * sx
                for field in range(len(moving)):
                    if (x_at, y_at) in ENTRY_LIST:
                        value = values[row : row + ROWS, step * LANES : (step + 1) * LANES]
                        links = (sx, y_at // SIDE, (y_at + 2) // SIDE)
                        if field == 0 and links != (0, 0, 0):
                            value = value * mask_of(*links)
                        patch[field * ENTRIES + entry_index(x_at, y_at)] = value
                    row += ROWS

    for first in range(0, len(SIDE_MOVES), CHUNK):
        chosen = SIDE_MOVES[first : first + CHUNK]
        values = moved(parts, columns(side_moves, first, len(chosen)))
        for step, (sx, y_at) in enumerate(chosen):
            keep(values, step, sx, y_at - y_at % 2)

    fixed = [0, 1, 2, DAMAGE]
    values = moved(
        pieces(
            jnp.concatenate(
                [points(turned, f, i, odd) for odd in range(2) for i in range(SIDE) for f in fixed],
                axis=0,
            )
        ),
        columns(side_moves, SIDE_MOVES.index((0, 0)), 1),
    )
    for i in range(SIDE):
        for j in range(2):
            at = 2 * i + j
            tall[24 * at : 24 * at + 8, :] = jnp.zeros(tile, jnp.float32)
            tall[24 * at + 8 : 24 * at + 16, :] = patch[entry_index(i, j)]
            tall[24 * at + 16 : 24 * at + 24, :] = jnp.zeros(tile, jnp.float32)
            for k in range(4):
                row = ((j * SIDE + i) * 4 + k) * ROWS
                value = values[row : row + ROWS]
                site[k * SITES + at] = value if k < 3 else 1.0 - value

    def shape_site(i, j):
        at = 2 * i + j
        base = i * PATCH_Y + j
        shape = {}
        moment = {}
        first = {}
        def gain(store, key, value, factor=1):
            if value is not None:
                store[key] = add_scaled(store.get(key), value, factor)

        for depths in ((0,), (1,), (-1,), (2,), (-2,), (3,), (-3,)):
            here = {dz: tall[24 * at + 8 - dz : 24 * at + 16 - dz, :] for dz in depths}
            strengths = {dz: {} for dz in depths}
            for dx, steps in bond_steps(depths[0]):
                for dy in steps:
                    limit = patch[base + (dx + REACH) * PATCH_Y + dy + REACH]
                    for dz in depths:
                        strengths[dz][dx, dy] = jnp.minimum(here[dz], limit)

            def sums_of(dz, c):
                terms = {}
                for (dx, dy), strength in strengths[dz].items():
                    k = base + (dx + REACH) * PATCH_Y + dy + REACH
                    terms[dx, dy] = strength * patch[(1 + c) * ENTRIES + k]
                return lattice_sums(terms, c == 0)

            acc = {dz: sums_of(dz, 0) for dz in depths}
            acc_u = {dz: [sums_of(dz, 1 + c) for c in range(3)] for dz in depths}

            for dz in depths:

                def back(value):
                    if value is None or dz == 0:
                        return value
                    return pltpu.roll(value, (-dz) % ROWS, 0)

                moved = {key: back(value) for key, value in acc[dz].items()}
                for key in ("xx", "xy", "yy"):
                    gain(shape, key, moved.get(key))
                gain(shape, "xz", moved.get("x"), dz)
                gain(shape, "yz", moved.get("y"), dz)
                gain(shape, "zz", moved.get("1"), dz * dz)
                gain(first, "x", moved.get("x"))
                gain(first, "y", moved.get("y"))
                gain(first, "z", moved.get("1"), dz)
                for comp in range(3):
                    moved_u = {key: back(value) for key, value in acc_u[dz][comp].items()}
                    gain(moment, (comp, 0), moved_u.get("x"))
                    gain(moment, (comp, 1), moved_u.get("y"))
                    gain(moment, (comp, 2), moved_u.get("1"), dz)
        kxx, kxy, kyy = shape["xx"], shape["xy"], shape["yy"]
        kxz, kyz, kzz = shape["xz"], shape["yz"], shape["zz"]
        plain = [kxx, kxy, kxz, kxy, kyy, kyz, kxz, kyz, kzz]
        arm = [first["x"], first["y"], first["z"]]
        moments = []
        for a in range(3):
            here_u = site[a * SITES + at]
            for b in range(3):
                moments.append(moment[a, b] + plain[3 * a + b] - here_u * arm[b])
        full = [value + 1.0 if k in (0, 4, 8) else value for k, value in enumerate(plain)]
        grad, carried = material(full, moments, site[3 * SITES + at])
        here_vol = patch[ENTRIES + base + REACH * PATCH_Y + REACH]
        for k in range(9):
            result[k * SITES + at] = grad[k]
            stress[k * SITES + at] = carried[k] * here_vol
        for a in range(3):
            result[(9 + a) * SITES + at] = (
                carried[3 * a] * arm[0] + carried[3 * a + 1] * arm[1] + carried[3 * a + 2] * arm[2]
            )

    def quarter_at(x_at, y_at):
        return (x_at + REACH) * PATCH_Y + y_at + REACH

    def site_pairs(source, first, odd, j, count):
        return [
            jnp.concatenate(
                [source[first + k * SITES + 2 * i + j] for i in (odd, odd + 2)], axis=1
            )
            for k in range(count)
        ]

    def quarter_entries(odd):
        parts = [part for j in range(2) for part in site_pairs(stress, 0, odd, j, 9)]
        parts = pieces(jnp.concatenate(parts, axis=0))
        for first in range(0, len(QUARTER_MOVES), CHUNK):
            chosen = QUARTER_MOVES[first : first + CHUNK]
            values = moved(parts, columns(quarter_moves, first, len(chosen)))
            for step, (x_even, half) in enumerate(chosen):
                row = 0
                x_at = x_even - x_even % 2 + odd
                for j in range(2):
                    y_at = 2 * half + j
                    for k in range(9):
                        if (x_at, y_at) in QUARTER_LIST:
                            value = values[row : row + ROWS, step * LANES : (step + 1) * LANES]
                            spread[k * QUARTERS + quarter_at(x_at, y_at)] = value
                        row += ROWS

    own_moves = columns(quarter_moves, QUARTER_MOVES.index((0, 0)), 1)

    def quarter_health():
        values = moved(
            pieces(jnp.concatenate(
                [
                    jnp.concatenate(
                        [patch[entry_index(x_at, y_at)], patch[entry_index(x_at + 2, y_at)]], axis=1
                    )
                    for x_at, y_at in QUARTER_LIST
                ],
                axis=0,
            )),
            own_moves,
        )
        for k, (x_at, y_at) in enumerate(QUARTER_LIST):
            value = values[k * ROWS : (k + 1) * ROWS]
            spread_health[quarter_at(x_at, y_at)] = value
            if 0 <= x_at < 2 and 0 <= y_at < 2:
                row = 24 * (2 * x_at + y_at)
                tall_quarter[row : row + 8, :] = jnp.zeros(tile, jnp.float32)
                tall_quarter[row + 8 : row + 16, :] = value
                tall_quarter[row + 16 : row + 24, :] = jnp.zeros(tile, jnp.float32)

    blocks = nx * ny
    per_group = LANES // blocks

    def gather_grad(group, comps):
        sites = [
            jnp.concatenate([result[comp * SITES + at] for comp in comps], axis=1)
            for at in range(SITES)
        ]
        values = moved(pieces(jnp.concatenate(sites, axis=0)), grad_moves[0 : len(comps) * LANES, :])
        for at in range(SITES):
            for jh in range(2):
                start = group * LANES + (2 * jh + at % 2) * SIDE + at // 2
                gathered[pl.ds(start, ROWS, stride=SIDE * SIDE), :] = values[
                    at * ROWS : (at + 1) * ROWS, jh * LANES : (jh + 1) * LANES
                ]

    def group_out(group, comps, target, first):
        rows_out[group * LANES : (group + 1) * LANES, :] = gathered[
            group * LANES : (group + 1) * LANES, :
        ].T
        for part, comp in enumerate(comps):
            for x in range(nx):
                row = group * LANES + part * blocks + x * ny
                target[x, comp - first, :, :] = rows_out[row : row + ny, :]

    grad_groups = [list(range(9))[k : k + per_group] for k in range(0, 9, per_group)]

    for i in COLUMN_ORDER:
        for j in range(2):
            shape_site(i, j)
    quarter_health()
    quarter_entries(0)
    quarter_entries(1)

    parts = [
        part for i in range(2) for j in range(2) for part in site_pairs(result, 9 * SITES, i, j, 3)
    ]
    values = moved(pieces(jnp.concatenate(parts, axis=0)), own_moves)
    for k in range(12):
        start_force[k] = values[k * ROWS : (k + 1) * ROWS]

    def force_site(i, j):
        at = 2 * i + j
        base = (i + REACH) * PATCH_Y + j + REACH
        here = {
            dz: tall_quarter[24 * at + 8 - dz : 24 * at + 16 - dz, :]
            for dz in range(-REACH, REACH + 1)
        }
        acc = {}
        for dx in range(-REACH, REACH + 1):
            for dy in range(-REACH, REACH + 1):
                if dx * dx + dy * dy > REACH_SQ:
                    continue
                k = base + dx * PATCH_Y + dy
                deep = [
                    dz
                    for dz in range(-REACH, REACH + 1)
                    if dx * dx + dy * dy + dz * dz <= REACH_SQ and (dx, dy, dz) != (0, 0, 0)
                ]
                strength = {dz: jnp.minimum(here[dz], spread_health[k]) for dz in deep}
                for a in range(3):
                    flat = None
                    if dx:
                        flat = add_scaled(flat, spread[3 * a * QUARTERS + k], dx)
                    if dy:
                        flat = add_scaled(flat, spread[(3 * a + 1) * QUARTERS + k], dy)
                    upright = spread[(3 * a + 2) * QUARTERS + k]
                    lifts = {
                        dz: upright if dz == 1 else upright * float(dz) for dz in deep if dz > 0
                    }
                    for dz in deep:
                        if dz > 0:
                            value = lifts[dz] if flat is None else flat + lifts[dz]
                        elif dz < 0:
                            value = -lifts[-dz] if flat is None else flat - lifts[-dz]
                        else:
                            value = flat
                        acc[a, dz] = plus(acc.get((a, dz)), strength[dz] * value)
        for a in range(3):
            total = start_force[3 * at + a]
            for dz in range(-REACH, REACH + 1):
                value = acc[a, dz]
                total = total + (pltpu.roll(value, (-dz) % ROWS, 0) if dz else value)
            start_force[3 * at + a] = total

    force_site(0, 0)
    for group, comps in enumerate(grad_groups):
        gather_grad(group, comps)
        group_out(group, comps, hold_grad, 0)
    grad_copy = pltpu.make_async_copy(hold_grad, out_grad, sems.at[0])
    grad_copy.start()
    force_site(0, 1)
    force_site(1, 0)
    force_site(1, 1)
    group = len(grad_groups)
    sites = [
        jnp.concatenate([start_force[3 * at + a] for a in range(3)], axis=1) for at in range(4)
    ]
    values = moved(pieces(jnp.concatenate(sites, axis=0)), force_moves[...])
    for at in range(4):
        for ih in range(2):
            for jh in range(2):
                start = group * LANES + (2 * jh + at % 2) * SIDE + 2 * ih + at // 2
                column = (2 * ih + jh) * LANES
                gathered[pl.ds(start, ROWS, stride=SIDE * SIDE), :] = values[
                    at * ROWS : (at + 1) * ROWS, column : column + LANES
                ]
    group_out(group, [9, 10, 11], hold_force, 9)
    force_copy = pltpu.make_async_copy(hold_force, out_force, sems.at[1])
    force_copy.start()
    grad_copy.wait()
    force_copy.wait()


def local(displacement, volume, health, damage, block_pairs):
    nx, ny, points = volume.shape
    ext_x = nx + 2 * RING
    f32 = jnp.float32
    pairs = block_pairs.reshape(block_pairs.shape[2:]).T
    raw = (displacement.transpose(0, 2, 1, 3), volume, health, damage)
    params = pltpu.CompilerParams(vmem_limit_bytes=48 * 1024 * 1024)
    x_shape = jax.ShapeDtypeStruct((ROWS + FIELDS * ny + FAR * ny // 2, points), f32)
    own, x_to_even, x_to_odd = pl.pallas_call(
        functools.partial(pack_kernel, nx, ny),
        out_shape=(jax.ShapeDtypeStruct((FIELDS * nx * ny, points), f32), x_shape, x_shape),
        in_specs=[pl.BlockSpec(memory_space=pltpu.HBM)] * 5,
        scratch_shapes=[
            [pltpu.VMEM(a.shape, a.dtype) for a in (*raw, pairs)],
            pltpu.SemaphoreType.DMA((5,)),
        ],
        compiler_params=params,
        name="pack",
    )(*[pltpu.with_memory_space_constraint(a, pltpu.HBM) for a in (*raw, pairs)])
    x_odd = swap(x_to_odd, "gx", True)
    x_even = swap(x_to_even, "gx", False)
    move_shapes = [
        jax.ShapeDtypeStruct((height * LANES, width * LANES), jnp.bfloat16)
        for height, width in (
            (2, len(SIDE_MOVES)),
            (2, len(QUARTER_MOVES)),
            (LANES // (nx * ny), 2),
            (3, 4),
        )
    ]
    moves = pl.pallas_call(
        functools.partial(moves_kernel, nx, ny),
        out_shape=move_shapes,
        in_specs=[pl.BlockSpec(memory_space=pl.ANY)],
        compiler_params=params,
        name="moves",
    )(x_to_even)
    y_shape = jax.ShapeDtypeStruct((ROWS + FIELDS * ext_x + FAR * ext_x // 2, points), f32)
    y_to_even, y_to_odd, beside = pl.pallas_call(
        functools.partial(middle_kernel, nx, ny),
        out_shape=(y_shape, y_shape, jax.ShapeDtypeStruct((FIELDS * 2 * RING * ny, points), f32)),
        scratch_shapes=[pltpu.VMEM((FAR * ext_x, points), f32)],
        compiler_params=params,
        name="middle",
    )(own, x_to_even, x_even, x_odd)
    y_odd = swap(y_to_odd, "gy", True)
    y_even = swap(y_to_even, "gy", False)
    tiles = lambda count: pltpu.VMEM((count, ROWS, LANES), f32)
    rows = lambda count: pltpu.VMEM((count * LANES, LANES), f32)
    grad, force = pl.pallas_call(
        functools.partial(main_kernel, nx, ny),
        out_shape=(
            jax.ShapeDtypeStruct((nx, 9, ny, points), f32),
            jax.ShapeDtypeStruct((nx, 3, ny, points), f32),
        ),
        scratch_shapes=[
            rows(FIELDS),
            rows(FIELDS),
            rows(3),
            tiles(5 * ENTRIES),
            pltpu.VMEM((24 * SITES, LANES), f32),
            tiles(4 * SITES),
            tiles(9 * SITES),
            tiles(9 * QUARTERS),
            tiles(QUARTERS),
            pltpu.VMEM((24 * 4, LANES), f32),
            tiles(12),
            tiles(12 * SITES),
            rows(4),
            rows(4),
            pltpu.VMEM((nx, 9, ny, points), f32),
            pltpu.VMEM((nx, 3, ny, points), f32),
            pltpu.SemaphoreType.DMA((2,)),
        ],
        out_specs=(pl.BlockSpec(memory_space=pltpu.HBM),) * 2,
        compiler_params=params,
        name="main",
    )(own, beside, y_to_even, y_even, y_odd, *moves)
    return grad.transpose(0, 2, 1, 3), force.transpose(0, 2, 1, 3)


def solution(mesh):
    in_specs = (
        P("gx", "gy", None, None),
        P("gx", "gy", None),
        P("gx", "gy", None),
        P("gx", "gy", None),
        P("gx", "gy", None, None),
    )
    out_specs = (P("gx", "gy", None, None), P("gx", "gy", None, None))
    return jax.shard_map(local, mesh=mesh, in_specs=in_specs, out_specs=out_specs, check_vma=False)
```

```python
import functools

import jax
import jax.numpy as jnp
from jax import lax
from jax.experimental import pallas as pl
from jax.experimental.pallas import tpu as pltpu
from jax.sharding import PartitionSpec as P

LANES = 128
ROWS = 8
SIDE = 4
REACH = 3
REACH_SQ = 9
RING = 2
FIELDS = 6
FAR = 5
VOL, HEALTH, DAMAGE = 3, 4, 5
LAME = 24.0
SHEAR = 16.0
KINDS = ((1, 0), (0, 1), (1, 1), (1, -1))
SITES = 2 * SIDE
PATCH_X = SIDE + 2 * REACH
PATCH_Y = 2 + 2 * REACH
ENTRIES = PATCH_X * PATCH_Y
QUARTERS = PATCH_Y * PATCH_Y
COLUMN_ORDER = (0, 2, 1, 3)
CHUNK = 2


def iota(shape, dim):
    return lax.broadcasted_iota(jnp.int32, shape, dim)


def divide(value, step, top):
    total = jnp.zeros_like(value)
    for k in range(1, top):
        total = total + jnp.where(value >= step * k, 1, 0)
    return total


def lanes_of(value, index):
    return jnp.take_along_axis(value, index, axis=1, mode="promise_in_bounds")


def pieces(value):
    high = value.astype(jnp.bfloat16)
    low = (value - high.astype(jnp.float32)).astype(jnp.bfloat16)
    return jnp.concatenate([high, low], axis=0)


def moved(halves, moves):
    both = jnp.dot(halves, moves, preferred_element_type=jnp.float32)
    rows = halves.shape[0] // 2
    return both[0:rows] + both[rows:]


def partner(index, count, odd):
    other = ((index + 1) ^ 1) - 1 if odd else index ^ 1
    return other if 0 <= other < count else None


def swap(array, axis, odd):
    nx, ny = lax.axis_size("gx"), lax.axis_size("gy")
    to, left = {}, []
    for i in range(nx):
        for j in range(ny):
            if axis == "gx":
                other = (partner(i, nx, odd), j)
            else:
                other = (i, partner(j, ny, odd))
            if None in other:
                left.append((i, j))
            else:
                to[i, j] = other
    while left:
        one = left.pop(0)
        if not left:
            to[one] = one
            break
        other = min(left, key=lambda at: (axis == "gy" and at[0] != one[0], abs(at[0] - one[0]) + abs(at[1] - one[1]), -at[0] - at[1]))
        left.remove(other)
        to[one], to[other] = other, one
    pairs = [(i * ny + j, k * ny + l) for (i, j), (k, l) in to.items()]
    return lax.ppermute(array, ("gx", "gy"), pairs)


def entry_list(wide, high):
    return [
        (x_at, y_at)
        for x_at in range(-REACH, wide + REACH)
        for y_at in range(-REACH, high + REACH)
        if any(
            (x_at - i) ** 2 + (y_at - j) ** 2 <= REACH_SQ for i in range(wide) for j in range(high)
        )
    ]


ENTRY_LIST = entry_list(SIDE, 2)
QUARTER_LIST = entry_list(2, 2)


SIDE_MOVES = [(0, -3)] + [(sx, y_at) for sx in (0, -1, 1) for y_at in (-2, 0, 2)] + [(0, 4)]
QUARTER_MOVES = [(x_at, half) for x_at in (-2, 0, 2) for half in (-1, 0, 1)]
QUARTER_MOVES += [(0, -2), (0, 2), (-3, 0), (4, 0)]


def lane_places(nx, ny):
    lane = iota((ROWS, LANES), 1)
    wide = 2 * (ny + 2)
    at_x = divide(lane, wide, nx + 4)
    at_half = lane - wide * at_x
    return lane, wide, at_x, lax.shift_right_logical(at_half, 1), (at_half & 1) == 1


def output_places(nx, ny):
    lane = iota((ROWS, LANES), 1)
    blocks = nx * ny
    slot = divide(lane, blocks, LANES // blocks + 1)
    block = lane - blocks * slot
    block_x = divide(block, ny, nx)
    return slot, block_x, block - ny * block_x


def moves_kernel(nx, ny, after, side_moves, quarter_moves, grad_moves, force_moves):
    lane, wide, at_x, at_y, upper = lane_places(nx, ny)
    ext_x, ext_y = nx + 2 * RING, ny + 2 * RING
    low_x_at, low_y_at = nx * ny, nx * ny + 2 * RING * ny
    rows = iota((2 * ROWS, LANES), 0)

    def block_row(e, f):
        own = (e - RING) * ny + f - RING
        column = jnp.where(e < RING, e, RING + ext_x - 1 - e)
        beside = low_x_at + column * ny + f - RING
        line = jnp.where(f < RING, f, RING + ext_y - 1 - f)
        above = low_y_at + line * ext_x + e
        row = jnp.where((e < RING) | (e >= RING + nx), beside, own)
        return jnp.where((f < RING) | (f >= RING + ny), above, row)

    def fill(target, column, source):
        source = jnp.concatenate([source, source], axis=0)
        for row in range(0, target.shape[0], 2 * ROWS):
            hit = jnp.where(source == rows + row, 1.0, 0.0).astype(jnp.bfloat16)
            target[row : row + 2 * ROWS, column * LANES : (column + 1) * LANES] = hit

    for column, (sx, y_at) in enumerate(SIDE_MOVES):
        sources = []
        for at in (y_at, y_at + 2):
            part = (at % SIDE - y_at % 2) // 2
            sources.append(part * LANES + block_row(at_x + 1 + sx, at_y + 1 + at // SIDE))
        source = jnp.where(upper, sources[1], sources[0])
        fill(side_moves, column, jnp.where(at_x < nx + 2, source, -1))

    quarter_x = divide(lane, 2 * ny, 2 * nx)
    quarter_y = lane - 2 * ny * quarter_x
    right = (quarter_x & 1) == 1
    owner = (lax.shift_right_logical(quarter_x, 1) + 1) * wide + quarter_y + 2
    for column, (x_at, half) in enumerate(QUARTER_MOVES):
        sources = []
        for at in (x_at, x_at + 2):
            part = (at % SIDE - x_at % 2) // 2
            sources.append(part * LANES + owner + (wide * (at // SIDE) + half))
        fill(quarter_moves, column, jnp.where(right, sources[1], sources[0]))

    slot, block_x, block_y = output_places(nx, ny)
    for jh in range(2):
        fill(grad_moves, jh, slot * LANES + (block_x + 1) * wide + 2 * (block_y + 1) + jh)
    for ih in range(2):
        for jh in range(2):
            source = slot * LANES + (2 * block_x + ih) * 2 * ny + 2 * block_y + jh
            fill(force_moves, 2 * ih + jh, jnp.where(slot < 3, source, -1))


def entry_index(x_at, y_at):
    return (x_at + REACH) * PATCH_Y + y_at + REACH


def own_rows(own, nx, ny, field, x, start, count):
    return own[pl.ds((field * nx + x) * ny + start, count), :]


def pack_kernel(nx, ny, disp, vol, health, damage, pairs, own, to_even, to_odd, here, sems):
    copies = []
    for k, (source, target) in enumerate(zip((disp, vol, health, damage, pairs), here)):
        copies.append(pltpu.make_async_copy(source, target, sems.at[k]))
    for k in (4, 0, 1, 2, 3):
        copies[k].start()
    disp, vol, health, damage, pairs = here
    odd_here = lax.rem(lax.axis_index("gx"), 2)
    ext_x = nx + 2 * RING
    slots = pairs.shape[1]
    copies[4].wait()
    ax, ay = pairs[0:1, :], pairs[1:2, :]
    bx, by = pairs[2:3, :], pairs[3:4, :]
    kind = jnp.where(bx == ax, 1, jnp.where(by == ay, 0, jnp.where(by > ay, 2, 3)))
    code = jnp.where(ax >= 0, kind * ext_x + ax + 1, -1)
    hit_x = jnp.where(code == iota((LANES, slots), 0), 1.0, 0.0).astype(jnp.bfloat16)
    hit_y = jnp.where(ay + 1 == iota((2 * ROWS, slots), 0), 1.0, 0.0).astype(jnp.bfloat16)
    table = lax.dot_general(
        hit_y, hit_x, (((1,), (1,)), ((), ())), preferred_element_type=jnp.float32
    )[0:ROWS]
    for copy in copies[:4]:
        copy.wait()
    for x in range(nx):
        for field in range(FIELDS):
            if field < 3:
                value = disp[x, field, :, :]
            elif field == VOL:
                value = vol[x, :, :]
            elif field == HEALTH:
                value = health[x, :, :]
            else:
                value = damage[x, :, :].astype(jnp.float32)
            row = (field * nx + x) * ny
            own[row : row + ny, :] = value
    for target, high in ((to_even, 1 - odd_here), (to_odd, odd_here)):
        target[0:ROWS, :] = table
        for field in range(FIELDS):
            row = ROWS + field * ny
            target[row : row + ny, :] = own_rows(own, nx, ny, field, high * (nx - 1), 0, ny)
        outer = 1 + high * (nx - 3)
        halves = [
            jnp.concatenate(
                [own_rows(own, nx, ny, field, outer, y, ny // 2) for field in range(FAR)], axis=0
            )
            for y in (0, ny // 2)
        ]
        target[ROWS + FIELDS * ny :, :] = folded(*halves, SIDE // 2, high)


def folded(first, second, step, high):
    keep = (iota(first.shape, 1) & step) != 0
    of_high = jnp.where(keep, first, pltpu.roll(second, LANES - step, 1))
    of_low = jnp.where(keep, pltpu.roll(second, step, 1), first)
    return jnp.where(high == 1, of_high, of_low)


def unfolded(rows, step, low):
    return rows, pltpu.roll(rows, step if low else LANES - step, 1)


def sides(from_even, from_odd, axis):
    here = lax.axis_index(axis)
    odd_here = lax.rem(here, 2) == 1
    low = jnp.where(odd_here, from_even, from_odd)
    high = jnp.where(odd_here, from_odd, from_even)
    low = jnp.where(here == 0, 0.0, low)
    return low, jnp.where(here == lax.axis_size(axis) - 1, 0.0, high)


def joined(table, low, high, count, axis, at, size):
    table = table + jnp.where(at >= count, pltpu.roll(high, count, axis), 0.0)
    return table + jnp.where(at < 2 * RING, pltpu.roll(low, size - count, axis), 0.0)


def middle_kernel(nx, ny, own, x_mine, x_even, x_odd, to_even, to_odd, beside, far):
    odd_y = lax.rem(lax.axis_index("gy"), 2)
    ext_x = nx + 2 * RING
    half = ny // 2
    lane = iota((ROWS, LANES), 1)
    at_e = lane - ext_x * divide(lane, ext_x, LANES // ext_x + 1)
    received = sides(x_even[...], x_odd[...], "gx")
    table = joined(x_mine[0:ROWS, :], received[0][0:ROWS], received[1][0:ROWS], nx, 1, at_e, LANES)
    for side, rows in enumerate(received):
        outer = unfolded(rows[ROWS + FIELDS * ny :], SIDE // 2, side == 0)
        for field in range(FIELDS):
            row = (field * 2 + side) * 2 * ny
            for part in range(2):
                if field < FAR:
                    value = outer[part][field * half : (field + 1) * half]
                else:
                    value = jnp.zeros((half, LANES), jnp.float32)
                beside[row + part * half : row + (part + 1) * half, :] = value
            beside[row + ny : row + 2 * ny, :] = rows[ROWS + field * ny : ROWS + (field + 1) * ny]

    def line(target, row, field, low, high):
        y = low + high * (ny - 1 - 2 * low)
        base = field * 4 * ny
        for e, column in ((0, 0), (1, 1), (nx + 2, 3), (nx + 3, 2)):
            target[row + e : row + e + 1, :] = beside[pl.ds(base + column * ny + y, 1), :]
        ends = [own[pl.ds(field * nx * ny + at, nx, stride=ny), :] for at in (low, ny - 1 - low)]
        target[row + RING : row + RING + nx, :] = jnp.where(high == 1, ends[1], ends[0])

    for target, high in ((to_even, 1 - odd_y), (to_odd, odd_y)):
        target[0:ROWS, :] = table
        for field in range(FIELDS):
            line(target, ROWS + field * ext_x, field, 0, high)
        for field in range(FAR):
            line(far, field * ext_x, field, 1, high)
        halves = [
            jnp.concatenate(
                [
                    far[field * ext_x + e : field * ext_x + e + ext_x // 2, :]
                    for field in range(FAR)
                ],
                axis=0,
            )
            for e in (0, ext_x // 2)
        ]
        target[ROWS + FIELDS * ext_x :, :] = folded(*halves, SIDE * SIDE // 2, high)


def bond_steps(dz):
    left = REACH_SQ - dz * dz
    for dx in range(-REACH, REACH + 1):
        steps = [
            dy
            for dy in range(-REACH, REACH + 1)
            if dx * dx + dy * dy <= left and (dx, dy, dz) != (0, 0, 0)
        ]
        if steps:
            yield dx, steps


def plus(total, term):
    return term if total is None else total + term


def weighted_sum(values):
    total = None
    for k, value in sorted(values.items()):
        total = plus(total, value if k == 1 else value * float(k))
    return total


def add_scaled(total, value, factor):
    if factor == 0:
        return total
    if abs(factor) != 1:
        value = value * float(abs(factor))
    if total is None:
        return value if factor > 0 else -value
    return total + value if factor > 0 else total - value


def lattice_sums(terms, second):
    row, slope, odd, even = {}, {}, {}, {}
    for dx in sorted({dx for dx, _ in terms}, key=abs):
        steps = {dy: terms[dx, dy] for x, dy in terms if x == dx}
        differences = {}
        for dy in sorted({abs(dy) for dy in steps}):
            if dy:
                summed = steps[dy] + steps[-dy]
                differences[dy] = steps[dy] - steps[-dy]
                even[dy] = plus(even.get(dy), summed)
                if not second:
                    odd[dy] = plus(odd.get(dy), differences[dy])
            else:
                summed = steps[0]
            row[dx] = plus(row.get(dx), summed)
        if second and differences:
            slope[dx] = weighted_sum(differences)
    rises = {dx: row[dx] - row[-dx] for dx in row if dx > 0}
    pairs = {dx: row[dx] + row[-dx] for dx in row if dx > 0}
    one = row.get(0)
    for value in pairs.values():
        one = plus(one, value)
    sums = {"1": one, "x": weighted_sum(rises)}
    if not second:
        sums["y"] = weighted_sum(odd)
        return sums
    sums["y"] = None
    for value in slope.values():
        sums["y"] = plus(sums["y"], value)
    sums["xx"] = weighted_sum({dx * dx: value for dx, value in pairs.items()})
    sums["yy"] = weighted_sum({dy * dy: value for dy, value in even.items()})
    sums["xy"] = weighted_sum({dx: slope[dx] - slope[-dx] for dx in slope if dx > 0})
    return sums


def product(left, right):
    return [
        sum(left[3 * a + k] * right[3 * k + b] for k in range(1, 3)) + left[3 * a] * right[b]
        for a in range(3)
        for b in range(3)
    ]


def material(shape, moment, alive):
    e = shape
    cof_00 = e[4] * e[8] - e[5] * e[7]
    cof_01 = e[5] * e[6] - e[3] * e[8]
    cof_02 = e[3] * e[7] - e[4] * e[6]
    cof_11 = e[0] * e[8] - e[2] * e[6]
    cof_12 = e[1] * e[6] - e[0] * e[7]
    cof_22 = e[0] * e[4] - e[1] * e[3]
    scale = 1.0 / (e[0] * cof_00 + e[1] * cof_01 + e[2] * cof_02)
    i00, i01, i02 = cof_00 * scale, cof_01 * scale, cof_02 * scale
    i11, i12, i22 = cof_11 * scale, cof_12 * scale, cof_22 * scale
    inverse = [i00, i01, i02, i01, i11, i12, i02, i12, i22]
    grad = product(moment, inverse)
    strain = {}
    for a in range(3):
        for b in range(a, 3):
            value = grad[a] * grad[b] + grad[3 + a] * grad[3 + b] + grad[6 + a] * grad[6 + b]
            strain[a, b] = value - 1.0 if a == b else value
    trace = strain[0, 0] + strain[1, 1] + strain[2, 2]
    second = [None] * 9
    for (a, b), value in strain.items():
        entry = value * SHEAR
        if a == b:
            entry = entry + trace * (0.5 * LAME)
        second[3 * a + b] = second[3 * b + a] = entry
    i00, i01, i02, i11, i12, i22 = [value * alive for value in (i00, i01, i02, i11, i12, i22)]
    inverse = [i00, i01, i02, i01, i11, i12, i02, i12, i22]
    return grad, product(product(grad, second), inverse)


def main_kernel(
    nx, ny, own, beside, y_mine, y_even, y_odd, side_moves, quarter_moves, grad_moves,
    force_moves, out_grad, out_force, ext, turned, weighted, patch, tall, site, stress, spread,
    spread_health, tall_quarter, start_force, result, gathered, rows_out, hold_grad, hold_force, sems
):
    ext_x, ext_y = nx + 2 * RING, ny + 2 * RING
    tile = (ROWS, LANES)
    at_row = iota(tile, 0)
    lane, wide, at_x, at_y, upper = lane_places(nx, ny)

    low_x_at, low_y_at = nx * ny, nx * ny + 2 * RING * ny
    side_x = 2 * RING * ny
    received = sides(y_even[...], y_odd[...], "gy")
    far = [
        unfolded(rows[ROWS + FIELDS * ext_x :], SIDE * SIDE // 2, side == 0)
        for side, rows in enumerate(received)
    ]
    half = ext_x // 2
    for field in range(FIELDS):
        base = field * LANES
        ext[base : base + nx * ny, :] = own_rows(own, nx, ny, field, 0, 0, nx * ny)
        at = base + low_x_at
        ext[at : at + side_x, :] = beside[field * side_x : (field + 1) * side_x, :]
        at = base + low_y_at
        for side in range(2):
            for part in range(2):
                if field < FAR:
                    value = far[side][part][field * half : (field + 1) * half]
                else:
                    value = jnp.zeros((half, LANES), jnp.float32)
                ext[at : at + half, :] = value
                at += half
            near = ROWS + field * ext_x
            ext[at : at + ext_x, :] = received[side][near : near + ext_x]
            at += ext_x
        if at < base + LANES:
            ext[at : base + LANES, :] = jnp.zeros((base + LANES - at, LANES), jnp.float32)

    for field in range(FIELDS):
        turned[field * LANES : (field + 1) * LANES, :] = ext[
            field * LANES : (field + 1) * LANES, :
        ].T
    for comp in range(3):
        weighted[comp * LANES : (comp + 1) * LANES, :] = (
            turned[comp * LANES : (comp + 1) * LANES, :]
            * turned[VOL * LANES : (VOL + 1) * LANES, :]
        )

    table = joined(
        y_mine[0:ROWS, :], received[0][0:ROWS], received[1][0:ROWS], ny, 0, at_row, ROWS
    )
    link = {}
    for kind, step in enumerate(KINDS):
        for sign in (1, -1):
            move = (0, 0) if sign == 1 else (-step[0], -step[1])
            picked = lanes_of(table, kind * ext_x + at_x + 1 + move[0])
            picked = jnp.where(at_row == at_y + 1 + move[1], picked, 0.0)
            link[sign * step[0], sign * step[1]] = jnp.broadcast_to(
                jnp.sum(picked, axis=0, keepdims=True), tile
            )

    masks = {}

    def mask_of(sx, sy0, sy1):
        if (sx, sy0, sy1) not in masks:
            one = jnp.ones(tile, jnp.float32)
            masks[sx, sy0, sy1] = jnp.where(
                upper, link.get((sx, sy1), one), link.get((sx, sy0), one)
            )
        return masks[sx, sy0, sy1]

    def points(source, field, i, odd):
        start = field * LANES + SIDE * odd + i
        near = source[pl.ds(start, ROWS, stride=SIDE * SIDE), :]
        far = source[pl.ds(start + 2 * SIDE, ROWS, stride=SIDE * SIDE), :]
        return jnp.concatenate([near, far], axis=1)

    def columns(moves, first, count):
        return moves[:, first * LANES : (first + count) * LANES]

    moving = ((turned, HEALTH), (turned, VOL), (weighted, 0), (weighted, 1), (weighted, 2))
    parts = pieces(
        jnp.concatenate(
            [
                points(source, field, i, odd)
                for odd in range(2)
                for i in range(SIDE)
                for source, field in moving
            ],
            axis=0,
        )
    )

    def keep(values, step, sx, y_even):
        row = 0
        for odd in range(2):
            y_at = y_even + odd
            for i in range(SIDE):
                x_at = i + SIDE * sx
                for field in range(len(moving)):
                    if (x_at, y_at) in ENTRY_LIST:
                        value = values[row : row + ROWS, step * LANES : (step + 1) * LANES]
                        links = (sx, y_at // SIDE, (y_at + 2) // SIDE)
                        if field == 0 and links != (0, 0, 0):
                            value = value * mask_of(*links)
                        patch[field * ENTRIES + entry_index(x_at, y_at)] = value
                    row += ROWS

    for first in range(0, len(SIDE_MOVES), CHUNK):
        chosen = SIDE_MOVES[first : first + CHUNK]
        values = moved(parts, columns(side_moves, first, len(chosen)))
        for step, (sx, y_at) in enumerate(chosen):
            keep(values, step, sx, y_at - y_at % 2)

    fixed = [0, 1, 2, DAMAGE]
    values = moved(
        pieces(
            jnp.concatenate(
                [points(turned, f, i, odd) for odd in range(2) for i in range(SIDE) for f in fixed],
                axis=0,
            )
        ),
        columns(side_moves, SIDE_MOVES.index((0, 0)), 1),
    )
    for i in range(SIDE):
        for j in range(2):
            at = 2 * i + j
            tall[24 * at : 24 * at + 8, :] = jnp.zeros(tile, jnp.float32)
            tall[24 * at + 8 : 24 * at + 16, :] = patch[entry_index(i, j)]
            tall[24 * at + 16 : 24 * at + 24, :] = jnp.zeros(tile, jnp.float32)
            for k in range(4):
                row = ((j * SIDE + i) * 4 + k) * ROWS
                value = values[row : row + ROWS]
                site[k * SITES + at] = value if k < 3 else 1.0 - value

    def shape_site(i, j):
        at = 2 * i + j
        base = i * PATCH_Y + j
        shape = {}
        moment = {}
        first = {}
        def gain(store, key, value, factor=1):
            if value is not None:
                store[key] = add_scaled(store.get(key), value, factor)

        for depths in ((0,), (1,), (-1,), (2,), (-2,), (3,), (-3,)):
            here = {dz: tall[24 * at + 8 - dz : 24 * at + 16 - dz, :] for dz in depths}
            strengths = {dz: {} for dz in depths}
            for dx, steps in bond_steps(depths[0]):
                for dy in steps:
                    limit = patch[base + (dx + REACH) * PATCH_Y + dy + REACH]
                    for dz in depths:
                        strengths[dz][dx, dy] = jnp.minimum(here[dz], limit)

            def sums_of(dz, c):
                terms = {}
                for (dx, dy), strength in strengths[dz].items():
                    k = base + (dx + REACH) * PATCH_Y + dy + REACH
                    terms[dx, dy] = strength * patch[(1 + c) * ENTRIES + k]
                return lattice_sums(terms, c == 0)

            acc = {dz: sums_of(dz, 0) for dz in depths}
            acc_u = {dz: [sums_of(dz, 1 + c) for c in range(3)] for dz in depths}

            for dz in depths:

                def back(value):
                    if value is None or dz == 0:
                        return value
                    return pltpu.roll(value, (-dz) % ROWS, 0)

                moved = {key: back(value) for key, value in acc[dz].items()}
                for key in ("xx", "xy", "yy"):
                    gain(shape, key, moved.get(key))
                gain(shape, "xz", moved.get("x"), dz)
                gain(shape, "yz", moved.get("y"), dz)
                gain(shape, "zz", moved.get("1"), dz * dz)
                gain(first, "x", moved.get("x"))
                gain(first, "y", moved.get("y"))
                gain(first, "z", moved.get("1"), dz)
                for comp in range(3):
                    moved_u = {key: back(value) for key, value in acc_u[dz][comp].items()}
                    gain(moment, (comp, 0), moved_u.get("x"))
                    gain(moment, (comp, 1), moved_u.get("y"))
                    gain(moment, (comp, 2), moved_u.get("1"), dz)
        kxx, kxy, kyy = shape["xx"], shape["xy"], shape["yy"]
        kxz, kyz, kzz = shape["xz"], shape["yz"], shape["zz"]
        plain = [kxx, kxy, kxz, kxy, kyy, kyz, kxz, kyz, kzz]
        arm = [first["x"], first["y"], first["z"]]
        moments = []
        for a in range(3):
            here_u = site[a * SITES + at]
            for b in range(3):
                moments.append(moment[a, b] + plain[3 * a + b] - here_u * arm[b])
        full = [value + 1.0 if k in (0, 4, 8) else value for k, value in enumerate(plain)]
        grad, carried = material(full, moments, site[3 * SITES + at])
        here_vol = patch[ENTRIES + base + REACH * PATCH_Y + REACH]
        for k in range(9):
            result[k * SITES + at] = grad[k]
            stress[k * SITES + at] = carried[k] * here_vol
        for a in range(3):
            result[(9 + a) * SITES + at] = (
                carried[3 * a] * arm[0] + carried[3 * a + 1] * arm[1] + carried[3 * a + 2] * arm[2]
            )

    def quarter_at(x_at, y_at):
        return (x_at + REACH) * PATCH_Y + y_at + REACH

    def site_pairs(source, first, odd, j, count):
        return [
            jnp.concatenate(
                [source[first + k * SITES + 2 * i + j] for i in (odd, odd + 2)], axis=1
            )
            for k in range(count)
        ]

    def quarter_entries(odd):
        parts = [part for j in range(2) for part in site_pairs(stress, 0, odd, j, 9)]
        parts = pieces(jnp.concatenate(parts, axis=0))
        for first in range(0, len(QUARTER_MOVES), CHUNK):
            chosen = QUARTER_MOVES[first : first + CHUNK]
            values = moved(parts, columns(quarter_moves, first, len(chosen)))
            for step, (x_even, half) in enumerate(chosen):
                row = 0
                x_at = x_even - x_even % 2 + odd
                for j in range(2):
                    y_at = 2 * half + j
                    for k in range(9):
                        if (x_at, y_at) in QUARTER_LIST:
                            value = values[row : row + ROWS, step * LANES : (step + 1) * LANES]
                            spread[k * QUARTERS + quarter_at(x_at, y_at)] = value
                        row += ROWS

    own_moves = columns(quarter_moves, QUARTER_MOVES.index((0, 0)), 1)

    def quarter_health():
        values = moved(
            pieces(jnp.concatenate(
                [
                    jnp.concatenate(
                        [patch[entry_index(x_at, y_at)], patch[entry_index(x_at + 2, y_at)]], axis=1
                    )
                    for x_at, y_at in QUARTER_LIST
                ],
                axis=0,
            )),
            own_moves,
        )
        for k, (x_at, y_at) in enumerate(QUARTER_LIST):
            value = values[k * ROWS : (k + 1) * ROWS]
            spread_health[quarter_at(x_at, y_at)] = value
            if 0 <= x_at < 2 and 0 <= y_at < 2:
                row = 24 * (2 * x_at + y_at)
                tall_quarter[row : row + 8, :] = jnp.zeros(tile, jnp.float32)
                tall_quarter[row + 8 : row + 16, :] = value
                tall_quarter[row + 16 : row + 24, :] = jnp.zeros(tile, jnp.float32)

    blocks = nx * ny
    per_group = LANES // blocks

    def gather_grad(group, comps):
        sites = [
            jnp.concatenate([result[comp * SITES + at] for comp in comps], axis=1)
            for at in range(SITES)
        ]
        values = moved(pieces(jnp.concatenate(sites, axis=0)), grad_moves[0 : len(comps) * LANES, :])
        for at in range(SITES):
            for jh in range(2):
                start = group * LANES + (2 * jh + at % 2) * SIDE + at // 2
                gathered[pl.ds(start, ROWS, stride=SIDE * SIDE), :] = values[
                    at * ROWS : (at + 1) * ROWS, jh * LANES : (jh + 1) * LANES
                ]

    def group_out(group, comps, target, first):
        rows_out[group * LANES : (group + 1) * LANES, :] = gathered[
            group * LANES : (group + 1) * LANES, :
        ].T
        for part, comp in enumerate(comps):
            for x in range(nx):
                row = group * LANES + part * blocks + x * ny
                target[x, comp - first, :, :] = rows_out[row : row + ny, :]

    grad_groups = [list(range(9))[k : k + per_group] for k in range(0, 9, per_group)]

    for i in COLUMN_ORDER:
        for j in range(2):
            shape_site(i, j)
    quarter_health()
    quarter_entries(0)
    quarter_entries(1)

    parts = [
        part for i in range(2) for j in range(2) for part in site_pairs(result, 9 * SITES, i, j, 3)
    ]
    values = moved(pieces(jnp.concatenate(parts, axis=0)), own_moves)
    for k in range(12):
        start_force[k] = values[k * ROWS : (k + 1) * ROWS]

    def force_site(i, j):
        at = 2 * i + j
        base = (i + REACH) * PATCH_Y + j + REACH
        here = {
            dz: tall_quarter[24 * at + 8 - dz : 24 * at + 16 - dz, :]
            for dz in range(-REACH, REACH + 1)
        }
        acc = {}
        for dx in range(-REACH, REACH + 1):
            for dy in range(-REACH, REACH + 1):
                if dx * dx + dy * dy > REACH_SQ:
                    continue
                k = base + dx * PATCH_Y + dy
                deep = [
                    dz
                    for dz in range(-REACH, REACH + 1)
                    if dx * dx + dy * dy + dz * dz <= REACH_SQ and (dx, dy, dz) != (0, 0, 0)
                ]
                strength = {dz: jnp.minimum(here[dz], spread_health[k]) for dz in deep}
                for a in range(3):
                    flat = None
                    if dx:
                        flat = add_scaled(flat, spread[3 * a * QUARTERS + k], dx)
                    if dy:
                        flat = add_scaled(flat, spread[(3 * a + 1) * QUARTERS + k], dy)
                    upright = spread[(3 * a + 2) * QUARTERS + k]
                    lifts = {
                        dz: upright if dz == 1 else upright * float(dz) for dz in deep if dz > 0
                    }
                    for dz in deep:
                        if dz > 0:
                            value = lifts[dz] if flat is None else flat + lifts[dz]
                        elif dz < 0:
                            value = -lifts[-dz] if flat is None else flat - lifts[-dz]
                        else:
                            value = flat
                        acc[a, dz] = plus(acc.get((a, dz)), strength[dz] * value)
        for a in range(3):
            total = start_force[3 * at + a]
            for dz in range(-REACH, REACH + 1):
                value = acc[a, dz]
                total = total + (pltpu.roll(value, (-dz) % ROWS, 0) if dz else value)
            start_force[3 * at + a] = total

    force_site(0, 0)
    for group, comps in enumerate(grad_groups):
        gather_grad(group, comps)
        group_out(group, comps, hold_grad, 0)
    grad_copy = pltpu.make_async_copy(hold_grad, out_grad, sems.at[0])
    grad_copy.start()
    force_site(0, 1)
    force_site(1, 0)
    force_site(1, 1)
    group = len(grad_groups)
    sites = [
        jnp.concatenate([start_force[3 * at + a] for a in range(3)], axis=1) for at in range(4)
    ]
    values = moved(pieces(jnp.concatenate(sites, axis=0)), force_moves[...])
    for at in range(4):
        for ih in range(2):
            for jh in range(2):
                start = group * LANES + (2 * jh + at % 2) * SIDE + 2 * ih + at // 2
                column = (2 * ih + jh) * LANES
                gathered[pl.ds(start, ROWS, stride=SIDE * SIDE), :] = values[
                    at * ROWS : (at + 1) * ROWS, column : column + LANES
                ]
    group_out(group, [9, 10, 11], hold_force, 9)
    force_copy = pltpu.make_async_copy(hold_force, out_force, sems.at[1])
    force_copy.start()
    grad_copy.wait()
    force_copy.wait()


def local(displacement, volume, health, damage, block_pairs):
    nx, ny, points = volume.shape
    ext_x = nx + 2 * RING
    f32 = jnp.float32
    pairs = block_pairs.reshape(block_pairs.shape[2:]).T
    raw = (displacement.transpose(0, 2, 1, 3), volume, health, damage)
    params = pltpu.CompilerParams(vmem_limit_bytes=48 * 1024 * 1024)
    x_shape = jax.ShapeDtypeStruct((ROWS + FIELDS * ny + FAR * ny // 2, points), f32)
    own, x_to_even, x_to_odd = pl.pallas_call(
        functools.partial(pack_kernel, nx, ny),
        out_shape=(jax.ShapeDtypeStruct((FIELDS * nx * ny, points), f32), x_shape, x_shape),
        in_specs=[pl.BlockSpec(memory_space=pltpu.HBM)] * 5,
        scratch_shapes=[
            [pltpu.VMEM(a.shape, a.dtype) for a in (*raw, pairs)],
            pltpu.SemaphoreType.DMA((5,)),
        ],
        compiler_params=params,
        name="pack",
    )(*[pltpu.with_memory_space_constraint(a, pltpu.HBM) for a in (*raw, pairs)])
    x_odd = swap(x_to_odd, "gx", True)
    x_even = swap(x_to_even, "gx", False)
    move_shapes = [
        jax.ShapeDtypeStruct((height * LANES, width * LANES), jnp.bfloat16)
        for height, width in (
            (2, len(SIDE_MOVES)),
            (2, len(QUARTER_MOVES)),
            (LANES // (nx * ny), 2),
            (3, 4),
        )
    ]
    moves = pl.pallas_call(
        functools.partial(moves_kernel, nx, ny),
        out_shape=move_shapes,
        in_specs=[pl.BlockSpec(memory_space=pl.ANY)],
        compiler_params=params,
        name="moves",
    )(x_to_even)
    y_shape = jax.ShapeDtypeStruct((ROWS + FIELDS * ext_x + FAR * ext_x // 2, points), f32)
    y_to_even, y_to_odd, beside = pl.pallas_call(
        functools.partial(middle_kernel, nx, ny),
        out_shape=(y_shape, y_shape, jax.ShapeDtypeStruct((FIELDS * 2 * RING * ny, points), f32)),
        scratch_shapes=[pltpu.VMEM((FAR * ext_x, points), f32)],
        compiler_params=params,
        name="middle",
    )(own, x_to_even, x_even, x_odd)
    y_odd = swap(y_to_odd, "gy", True)
    y_even = swap(y_to_even, "gy", False)
    tiles = lambda count: pltpu.VMEM((count, ROWS, LANES), f32)
    rows = lambda count: pltpu.VMEM((count * LANES, LANES), f32)
    grad, force = pl.pallas_call(
        functools.partial(main_kernel, nx, ny),
        out_shape=(
            jax.ShapeDtypeStruct((nx, 9, ny, points), f32),
            jax.ShapeDtypeStruct((nx, 3, ny, points), f32),
        ),
        scratch_shapes=[
            rows(FIELDS),
            rows(FIELDS),
            rows(3),
            tiles(5 * ENTRIES),
            pltpu.VMEM((24 * SITES, LANES), f32),
            tiles(4 * SITES),
            tiles(9 * SITES),
            tiles(9 * QUARTERS),
            tiles(QUARTERS),
            pltpu.VMEM((24 * 4, LANES), f32),
            tiles(12),
            tiles(12 * SITES),
            rows(4),
            rows(4),
            pltpu.VMEM((nx, 9, ny, points), f32),
            pltpu.VMEM((nx, 3, ny, points), f32),
            pltpu.SemaphoreType.DMA((2,)),
        ],
        out_specs=(pl.BlockSpec(memory_space=pltpu.HBM),) * 2,
        compiler_params=params,
        name="main",
    )(own, beside, y_to_even, y_even, y_odd, *moves)
    return grad.transpose(0, 2, 1, 3), force.transpose(0, 2, 1, 3)


def solution(mesh):
    in_specs = (
        P("gx", "gy", None, None),
        P("gx", "gy", None),
        P("gx", "gy", None),
        P("gx", "gy", None),
        P("gx", "gy", None, None),
    )
    out_specs = (P("gx", "gy", None, None), P("gx", "gy", None, None))
    return jax.shard_map(local, mesh=mesh, in_specs=in_specs, out_specs=out_specs, check_vma=False)
```
